128 devices in a mesh: gx: 4 (over z), gy: 4 (over x), gz: 8 (over y, core).
Axes of the slice: x: 4, y: 4, z: 4, core: 2. Of those that a mesh axis runs over, the one named last changes fastest.
Arguments:
- forces: float32 [3, 64, 64, 1024], P(None, 'gx', 'gy', 'gz'), may hold values from -8 to 8
- mass_shift: float32 [64, 64, 1024], P('gx', 'gy', 'gz'), may hold values from 0.5 to 2
- deflation: float32 [16, 3, 64, 64, 1024], P(None, None, 'gx', 'gy', 'gz'), may hold values from -0.01953125 to 0.01953125
- coarse_factor: float32 [2048, 2048], P('gz'), may hold values from -0.0145165043 to 0.6, as said below
- coarse_slot: int32 [128], replicated, may hold values from 0 to 127, each once
Outputs:
- solution: float32 [3, 64, 64, 1024], P(None, 'gx', 'gy', 'gz')
- residual: float32 [3, 64, 64, 1024], P(None, 'gx', 'gy', 'gz')
- direction: float32 [3, 64, 64, 1024], P(None, 'gx', 'gy', 'gz')
The draws below stay inside these ranges and needn't reach their ends.
Inputs may be any that keep to these rules, and one draw needn't show every extreme that they name: `coarse_factor`: lower triangular: zero above the diagonal; diagonal entries between 0.3 and 0.6. `coarse_slot`: each subdomain has its own coarse position.
All inputs are finite; a program needn't handle non-finite values.
Results may differ from the reference program's by a relative error of at most 0.0003.
Values sent between devices are 32-bit elements; how exact they have to be, the bound alone decides.
No kernel may reach another device: no remote copies, remote signals or barrier semaphores. Data moves between devices by JAX's collectives and lax.ppermute only.
A program may use at most 192 MiB of HBM per device.

```python
import math
import jax
import jax.numpy as jnp
from jax import lax

CX = 16
CY = 16
CZ = 128
K = 16
SWEEPS = 3
ITERS = 4
NX = 64
NY = 64
NZ = 1024
SUBS = 128
NC = 2048
N_GX = 4
N_GY = 4
N_GZ = 8


lower_offset = 0.012


def draw_forces(key, part):
    key_field = jax.random.fold_in(key, 3)
    along_x = (jnp.arange(NX, dtype=jnp.float32) + 0.5) / NX
    along_y = (jnp.arange(NY, dtype=jnp.float32) + 0.5) / NY
    along_z = (jnp.arange(NZ, dtype=jnp.float32) + 0.5) / NZ
    ramp_sum = along_x[:, None, None] + along_y[None, :, None] + along_z[None, None, :]
    rough_part = jax.random.truncated_normal(key_field, -4.0, 4.0, (3, NX, NY, NZ), jnp.float32)
    return rough_part * 3.0 ** (ramp_sum / 6.0)


def draw_coarse_factor(key, part):
    key_lower, key_diag = jax.random.split(jax.random.fold_in(key, 5))
    spread = 0.3 / math.sqrt(NC)
    lower_part = jax.random.truncated_normal(key_lower, -4.0, 4.0, (NC, NC), jnp.float32) * spread
    lower_part = lower_part + lower_offset
    diagonal = jax.random.uniform(key_diag, (NC,), jnp.float32, 0.3, 0.6)
    return jnp.tril(lower_part, -1) + jnp.diag(diagonal)


def level_of(key, extent, pieces, least, high):
    factor_of = 1.0
    for dim, blocks in pieces:
        steps = jax.random.uniform(jax.random.fold_in(jax.random.fold_in(key, 6), dim), (blocks,), jnp.float32, least / len(pieces), high / len(pieces))
        factor_of = factor_of * jnp.repeat(jnp.exp(steps), extent[dim] // blocks).reshape((-1,) + (1,) * (len(extent) - 1 - dim))
    return factor_of


def scatter_about(stream_key, dims, deviation, bound, cuts=(), kind=jnp.bfloat16):
    entries = deviation * jax.random.normal(stream_key, dims, jnp.float32)
    if cuts:
        entries = entries * level_of(stream_key, dims, cuts, -0.22, 0.18)
    return jnp.clip(entries, -bound, bound).astype(kind)


def setup_inputs(seed: int = 0) -> dict:
    keys = jax.random.split(jax.random.key(seed), 6)
    return {
        "forces": draw_forces(jax.random.fold_in(keys[5], 71), 0),
        "mass_shift": jnp.clip(jnp.exp(math.log(2.0) - 1.3862944 * jax.random.uniform(keys[1], (NX, NY, NZ), jnp.float32) ** level_of(keys[1], (NX, NY, NZ), ((0, 4), (1, 4), (2, 8)), -0.2, 0.2)), 0.5, 2.0),
        "deflation": scatter_about(keys[2], (K, 3, NX, NY, NZ), ((3 * CX * CY * CZ) ** -0.5), 0.01953125, ((2, 4), (3, 4), (4, 8)), jnp.float32),
        "coarse_factor": draw_coarse_factor(jax.random.fold_in(keys[5], 71), 0),
        "coarse_slot": jax.random.permutation(keys[4], SUBS).astype(jnp.int32),
    }


shear_modulus = 0.25
lame_first = 0.375
relaxation = 0.6
offsets_unit = ((1, 0, 0), (0, 1, 0), (0, 0, 1))

def stencil(padded, mass_shift):
    size_x = padded.shape[1] - 2
    size_y = padded.shape[2] - 2
    size_z = padded.shape[3] - 2
    stiffer = lame_first + shear_modulus

    def neighbor(component, shift_x, shift_y, shift_z):
        return padded[component, 1 + shift_x:1 + shift_x + size_x, 1 + shift_y:1 + shift_y + size_y, 1 + shift_z:1 + shift_z + size_z]

    def moved(component, first_unit, second_unit, sign_first, sign_second):
        return neighbor(component, sign_first * first_unit[0] + sign_second * second_unit[0], sign_first * first_unit[1] + sign_second * second_unit[1], sign_first * first_unit[2] + sign_second * second_unit[2])
    outputs = []
    for component in range(3):
        middle = neighbor(component, 0, 0, 0)
        summed = mass_shift * middle
        for axis_number in range(3):
            unit_step = offsets_unit[axis_number]
            second_diff = moved(component, unit_step, unit_step, 1, 0) + moved(component, unit_step, unit_step, -1, 0) - 2.0 * middle
            weight = shear_modulus + stiffer if axis_number == component else shear_modulus
            summed = summed - weight * second_diff
        own_unit = offsets_unit[component]
        for partner in range(3):
            if partner != component:
                partner_unit = offsets_unit[partner]
                mixed_term = moved(partner, own_unit, partner_unit, 1, 1) - moved(partner, own_unit, partner_unit, 1, -1) - moved(partner, own_unit, partner_unit, -1, 1) + moved(partner, own_unit, partner_unit, -1, -1)
                summed = summed - 0.25 * stiffer * mixed_term
        outputs.append(summed)
    return jnp.stack(outputs)

def reference(forces, mass_shift, deflation, coarse_factor, coarse_slot):
    diagonal = mass_shift + (6.0 * shear_modulus + 2.0 * (lame_first + shear_modulus))
    blocked_shape = (3, N_GX, CX, N_GY, CY, N_GZ, CZ)

    def operate(field):
        return stencil(jnp.pad(field, ((0, 0), (1, 1), (1, 1), (1, 1))), mass_shift)

    def restrict(field):
        blocked = field.reshape(blocked_shape)

        def one_vector(vector):
            return jnp.sum(vector.reshape(blocked_shape) * blocked, axis=(0, 2, 4, 6))
        sums = lax.map(one_vector, deflation)
        return jnp.transpose(sums, (1, 2, 3, 0)).reshape(N_GX * N_GY * N_GZ, K)

    def prolong(weights):
        grid = jnp.transpose(weights.reshape(N_GX, N_GY, N_GZ, K), (3, 0, 1, 2))

        def add_vector(summed, pair):
            vector, scales = pair
            return (summed + vector.reshape(blocked_shape) * scales[None, :, None, :, None, :, None], None)
        start = jnp.zeros(blocked_shape, jnp.float32)
        summed, ignored = lax.scan(add_vector, start, (deflation, grid))
        return summed.reshape(3, NX, NY, NZ)

    def precondition(field):
        restricted = restrict(field)
        ordered = jnp.zeros_like(restricted).at[coarse_slot].set(restricted).reshape(-1)
        forward = jax.scipy.linalg.solve_triangular(coarse_factor, ordered, lower=True)
        coarse = jax.scipy.linalg.solve_triangular(coarse_factor, forward, lower=True, trans=1)
        correction = prolong(coarse.reshape(-1, K)[coarse_slot])
        smooth = jnp.zeros_like(field)
        for sweep_index in range(SWEEPS):
            smooth = smooth + relaxation * (field - operate(smooth)) / diagonal
        return correction + smooth
    solution = jnp.zeros_like(forces)
    residual = forces
    direction = forces
    precond_prior = jnp.float32(1.0)
    for iteration in range(ITERS):
        preconditioned = precondition(residual)
        precond_norm = jnp.sum(residual * preconditioned)
        if iteration == 0:
            direction = preconditioned
        else:
            direction = preconditioned + precond_norm / precond_prior * direction
        image_field = operate(direction)
        step_size = precond_norm / jnp.sum(direction * image_field)
        solution = solution + step_size * direction
        residual = residual - step_size * image_field
        precond_prior = precond_norm
    return (solution, residual, direction)
```

```python
import functools

import jax
import jax.numpy as jnp
from jax import lax
from jax.experimental import pallas as pl
from jax.experimental.pallas import tpu as pltpu
from jax.sharding import Mesh
from jax.sharding import PartitionSpec as P

ITERS = 4
GZ = ("gz_0", "gz_1")
EVERY = ("gx", "gy", "gz_0", "gz_1")

relaxation = 0.6
off_diagonal = 0.25
stiffer = 0.625
highest = lax.Precision.HIGHEST
f32 = jnp.float32
H = 3
MIB = 1 << 20


def call(kernel, outs, ins, scratch=(), aliases=None, limit=56):
    vmem = pl.BlockSpec(memory_space=pltpu.VMEM)
    specs = []
    for a in ins:
        specs.append(pl.BlockSpec(memory_space=pltpu.SMEM) if a.dtype == jnp.int32 else vmem)
    return pl.pallas_call(
        kernel,
        out_shape=[jax.ShapeDtypeStruct(s, f32) for s in outs],
        in_specs=specs,
        out_specs=[vmem] * len(outs),
        scratch_shapes=list(scratch),
        input_output_aliases=aliases or {},
        compiler_params=pltpu.CompilerParams(vmem_limit_bytes=limit * MIB),
    )(*ins)


def iota(shape, dim):
    return lax.broadcasted_iota(jnp.int32, shape, dim)


def mm(a, b):
    return jnp.dot(a, b, precision=highest, preferred_element_type=f32)


def factor_kernel(place, rows, out):
    j = place[0]
    n = rows.shape[0]
    tiles = n // 128
    start = pl.multiple_of(j * n, n)
    own = rows[:, pl.ds(start, n)]
    i0, i1 = iota((n, n), 0), iota((n, n), 1)
    eye = i0 == i1
    inverse = jnp.where(eye, 1.0 / jnp.sum(jnp.where(eye, own, 0.0), axis=1, keepdims=True), 0.0)
    size = 1
    while size < n:
        same = (i0 // (2 * size)) == (i1 // (2 * size))
        block = jnp.where(same & ((i0 // size) > (i1 // size)), own, 0.0)
        inverse = inverse - mm(inverse, mm(block, inverse))
        size *= 2
    for t in range(rows.shape[1] // n):

        @pl.when(t < j)
        def _():
            scaled = mm(inverse, rows[:, t * n : (t + 1) * n])
            for u in range(tiles):
                out[t * tiles + u] = scaled[:, u * 128 : (u + 1) * 128]

        @pl.when(t >= j)
        def _():
            for u in range(tiles):
                out[t * tiles + u] = inverse[:, u * 128 : (u + 1) * 128]


def lanes_of(sums):
    count = sums.shape[0]
    column = jnp.sum(sums, axis=1, keepdims=True)
    placed = jnp.where(iota((count, 128), 0) == iota((count, 128), 1), column, 0.0)
    return jnp.sum(placed, axis=0, keepdims=True)


def restrict_rows(vectors, field):
    count = vectors.shape[0]

    def plane(x, acc):
        acc = list(acc)
        for c in range(3):
            values = field[c, x]
            for k in range(count):
                part = vectors[k, c, x] * values
                acc[k] = acc[k] + (part[:8] + part[8:])
        return tuple(acc)

    acc = lax.fori_loop(0, 16, plane, tuple(jnp.zeros((8, 128), f32) for _ in range(count)))
    rows = [jnp.sum(a, axis=0, keepdims=True) for a in acc]
    return jnp.concatenate(rows, axis=0)


def restrict_kernel(vectors, field, out):
    out[...] = lanes_of(restrict_rows(vectors, field))


def pack_y(tile0, tile1):
    return jnp.where(iota(tile0.shape, tile0.ndim - 2) < 4, tile0, tile1)


def pack_y_kernel(own, low, high, out):
    for c in range(own.shape[0]):
        for x in range(H):
            out[c, x] = pack_y(low[c, x, :8], low[c, x, 8:])
            out[c, H + 16 + x] = pack_y(high[c, x, :8], high[c, x, 8:])
        for x in range(16):
            out[c, H + x] = pack_y(own[c, x, :8], own[c, x, 8:])


def plane_parts(own, low, high, c, i):
    if i < H:
        return low[c, i]
    if i < H + 16:
        return own[c, i - H]
    return high[c, i - H - 16]


def pack_z_kernel(own, low, high, yplus, yminus, out):
    lane = iota((24, 128), 1)
    edge = (lane < H) | (lane >= 128 - H)
    for c in range(own.shape[0]):
        packed = [jnp.zeros((24, 128), f32), jnp.zeros((24, 128), f32)]
        for i in range(22):
            ytile = pack_y(yplus[c, i], yminus[c, i])
            plane = jnp.concatenate([plane_parts(own, low, high, c, i), ytile], axis=0)
            plane = jnp.where(edge, plane, 0.0)
            shift = (8 * i) % 128
            if shift:
                plane = pltpu.roll(plane, shift, 1)
            packed[i // 16] = packed[i // 16] + plane
        out[c, :, :128] = packed[0]
        out[c, :, 128:] = packed[1]


def assemble(own, low, high, yplus, yminus, zplus, zminus, c, i):
    lane = iota((24, 128), 1)
    ytile = pack_y(yplus[c, i], yminus[c, i])
    centre = jnp.concatenate([plane_parts(own, low, high, c, i), ytile], axis=0)
    half = slice(0, 128) if i < 16 else slice(128, 256)
    side = jnp.where(lane % 8 < 4, zplus[c, :, half], zminus[c, :, half])
    shift = (8 * i) % 128
    if shift:
        side = pltpu.roll(side, 128 - shift, 1)
    side = jnp.where((lane < H) | (lane >= 128 - H), side, 0.0)
    return jnp.concatenate([centre, side], axis=1)


def start_kernel(inside, own, low, high, yplus, yminus, zplus, zminus, residual, scale):
    row, lane = iota((24, 256), 0), iota((24, 256), 1)
    keep = jnp.where(row < 16, 1, jnp.where(row < 20, inside[3], inside[2]))
    keep = keep * jnp.where(lane < 128, 1, jnp.where(lane < 192, inside[5], inside[4]))
    keep = jnp.where((row >= 16 + H) & (row < 24 - H), 0, keep)
    for i in range(22):
        for c in range(4):
            plane = assemble(own, low, high, yplus, yminus, zplus, zminus, c, i)
            if c < 3:
                residual[c, i] = plane
            else:
                here = keep
                if i < H:
                    here = keep * inside[0]
                elif i >= H + 16:
                    here = keep * inside[1]
                lanes_in = (lane < 128 + H) | (lane >= 256 - H)
                scale[i] = jnp.where((here > 0) & lanes_in, plane, 0.0)


def rows_to_column(row, eye):
    return jnp.sum(jnp.where(eye, row, 0.0), axis=1, keepdims=True)


def column_to_row(column, eye):
    return jnp.sum(jnp.where(eye, column, 0.0), axis=0, keepdims=True)


def coarse_kernel(stage, pieces, slots, near, factor, *refs):
    if stage == 0:
        g_out, wx, wy, wz = refs
    elif stage == 1:
        g_in, g_out, wx, wy, wz, hdir_out, scalars_out = refs
    else:
        g_in, hdir_in, scalars_in, g_out, wx, wy, wz, hdir_out, scalars_out = refs
    blocks = factor.shape[0]
    n = factor.shape[2]
    q0, l256 = iota((128, 256), 0), iota((128, 256), 1)
    spot = (l256 // 16) == (q0 % 16)
    got = pieces[...]
    spread = jnp.where(iota((128, 256), 0) == iota((128, 256), 1) % 16, 1.0, 0.0)
    spread = jnp.where(iota((128, 256), 0) < 16, spread, 0.0)
    tiled = mm(got, spread)
    ordered = jnp.where(spot, mm(slots[...], tiled), 0.0)
    ordered = jnp.sum(ordered.reshape(8, 16, 256), axis=1)
    if stage == 0:
        g = ordered
    else:
        totals = jnp.sum(got, axis=0, keepdims=True)
        lane = iota((1, 128), 1)
        rho = jnp.sum(jnp.where(lane == 16, totals, 0.0), axis=1, keepdims=True)
        energy = jnp.sum(jnp.where(lane == 17, totals, 0.0), axis=1, keepdims=True)
        if stage == 1:
            momentum = jnp.zeros_like(rho)
            step = rho / energy
            hdir = ordered
        else:
            rho_prior = scalars_in[0:1, 0:1]
            step_prior = scalars_in[1:2, 0:1]
            momentum = rho / rho_prior
            step = rho / (energy - momentum * rho / step_prior)
            hdir = ordered + momentum * hdir_in[...]
        g = g_in[...] - step * hdir
        hdir_out[...] = hdir
        r8 = iota((8, 128), 0)
        scalars_out[...] = jnp.where(r8 == 0, rho, jnp.where(r8 == 1, step, momentum))
    g_out[...] = g
    eye = iota((128, 128), 0) == iota((128, 128), 1)
    yrow, ycol = [], []
    for j in range(blocks):
        acc = factor[j, 2 * j] * g[j : j + 1, :128] + factor[j, 2 * j + 1] * g[j : j + 1, 128:]
        for t in range(2 * j):
            acc = acc - factor[j, t] * yrow[t]
        column = jnp.sum(acc, axis=1, keepdims=True)
        for u in range(2):
            yrow.append(column_to_row(column[u * 128 : (u + 1) * 128], eye))
    vcol = [None] * blocks
    crow = [None] * blocks
    for i in range(blocks - 1, -1, -1):
        columns = []
        for u in range(2):
            t = 2 * i + u
            value = yrow[t]
            if i < blocks - 1:
                acc = factor[i + 1, t] * vcol[i + 1]
                for k in range(i + 2, blocks):
                    acc = acc + factor[k, t] * vcol[k]
                value = value - jnp.sum(acc, axis=0, keepdims=True)
            columns.append(rows_to_column(value, eye))
        vcol[i] = jnp.concatenate(columns, axis=0)
        crow[i] = jnp.concatenate(
            [jnp.sum(factor[i, 2 * i + u] * vcol[i], axis=0, keepdims=True) for u in range(2)],
            axis=1,
        )
    spread_c = jnp.concatenate(
        [jnp.broadcast_to(crow[b], (16, 256)) for b in range(blocks)], axis=0
    )
    spread_c = jnp.where(spot, spread_c, 0.0)
    fold = jnp.where(iota((256, 128), 0) % 16 == iota((256, 128), 1) % 16, 1.0, 0.0)
    by_slot = mm(spread_c, fold)
    weights = mm(near[...], by_slot)

    def w(x, y, z):
        n = x * 9 + y * 3 + z
        return weights[n : n + 1, :]

    r16, l16 = iota((16, 128), 0), iota((16, 128), 1)
    pick16 = r16 == l16
    row24, lane24 = iota((24, 128), 0), iota((24, 128), 1)
    for x in range(3):
        wx[16 * x : 16 * x + 16] = jnp.broadcast_to(
            jnp.sum(jnp.where(pick16, w(x, 1, 1), 0.0), axis=1, keepdims=True), (16, 128)
        )
        for side, y in ((0, 2), (1, 0)):
            wy[x, 16 * side : 16 * side + 16] = jnp.broadcast_to(
                jnp.sum(jnp.where(pick16, w(x, y, 1), 0.0), axis=1, keepdims=True), (16, 128)
            )

        def side_plane(z):
            return jnp.where(
                row24 < 16,
                w(x, 1, z),
                jnp.where(row24 == 16, w(x, 2, z), jnp.where(row24 == 23, w(x, 0, z), 0.0)),
            )

        wz[x] = jnp.where(
            lane24 < 16, side_plane(2), jnp.where(lane24 < 32, side_plane(0), 0.0)
        )


def stencil_terms(u, i):
    um = [u[c, i - 1] for c in range(3)]
    u0 = [u[c, i] for c in range(3)]
    up = [u[c, i + 1] for c in range(3)]

    def y(f):
        return pltpu.roll(f, 23, 0), pltpu.roll(f, 1, 0)

    def z(f):
        return pltpu.roll(f, 255, 1), pltpu.roll(f, 1, 1)

    dx = [up[c] - um[c] for c in range(3)]
    sx = [up[c] + um[c] for c in range(3)]
    yp, ym, zp, zm = [], [], [], []
    for c in range(3):
        a, b = y(u0[c])
        yp.append(a)
        ym.append(b)
        a, b = z(u0[c])
        zp.append(a)
        zm.append(b)
    sy = [yp[c] + ym[c] for c in range(3)]
    sz = [zp[c] + zm[c] for c in range(3)]
    a, b = y(dx[1])
    mixed0 = a - b
    a, b = z(dx[2])
    mixed0 = mixed0 + (a - b)
    a, b = y(dx[0] + (zp[2] - zm[2]))
    mixed1 = a - b
    a, b = z(dx[0] + (yp[1] - ym[1]))
    mixed2 = a - b
    mixed = [mixed0, mixed1, mixed2]
    own = [sx[0], sy[1], sz[2]]
    return u0, [
        off_diagonal * (sx[c] + sy[c] + sz[c]) + stiffer * own[c] + (0.25 * stiffer) * mixed[c]
        for c in range(3)
    ]


def main_kernel(first, *refs):
    if first:
        (residual_in, scale, wx, wy, wz, vectors, vx, vy, vz, z_out, image_out, low_out, high_out, payload,
         s1, s2, zed) = refs
        residual = residual_in
    else:
        (scalars, residual_in, held_in, own, low, high, yplus, yminus, zplus, zminus, zprev, solution_in,
         direction_in, scale, wx, wy, wz, vectors, vx, vy, vz,
         residual, held, solution_out, direction_out,
         z_out, image_out, low_out, high_out, payload, s1, s2, zed) = refs
        step = scalars[1:2, 0:1]
        momentum = scalars[2:3, 0:1]
        for i in range(22):
            for c in range(3):
                image = assemble(own, low, high, yplus, yminus, zplus, zminus, c, i)
                image = image + momentum * held_in[c, i]
                held[c, i] = image
                residual[c, i] = residual_in[c, i] - step * image

        def advance(x, carry):
            for c in range(3):
                d = zprev[c, x] + momentum * direction_in[c, x]
                direction_out[c, x] = d
                solution_out[c, x] = solution_in[c, x] + step * d
            return carry

        lax.fori_loop(0, 16, advance, 0)

    def sweep1(i, carry):
        w = scale[i]
        for c in range(3):
            s1[c, i] = w * residual[c, i]
        return carry

    lax.fori_loop(0, 22, sweep1, 0)

    def sweep2(i, carry):
        w = scale[i]
        u0, terms = stencil_terms(s1, i)
        for c in range(3):
            s2[c, i] = (1.0 - relaxation) * u0[c] + w * (residual[c, i] + terms[c])
        return carry

    lax.fori_loop(1, 21, sweep2, 0)

    def correct(source, x, i, region):
        accs = []
        for c in range(3):
            acc = wx[pl.ds(16 * region, 1), :] * source[0, c, x]
            for k in range(1, 16):
                acc = acc + wx[pl.ds(16 * region + k, 1), :] * source[k, c, x]
            accs.append(acc)
        lane = iota((24, 128), 1)
        row = iota((8, 128), 0)
        for c in range(3):
            prod = vy[c, i - 2] * wy[region]
            plus = jnp.sum(prod[:16], axis=0, keepdims=True)
            minus = jnp.sum(prod[16:], axis=0, keepdims=True)
            ytile = jnp.where(row == 0, plus, jnp.where(row == 7, minus, 0.0))
            prod = vz[c, i - 2] * wz[region]
            plus = jnp.sum(jnp.where(lane < 16, prod, 0.0), axis=1, keepdims=True)
            minus = jnp.sum(jnp.where(lane >= 16, prod, 0.0), axis=1, keepdims=True)
            side = jnp.where(lane == 0, plus, jnp.where(lane == 127, minus, 0.0))
            zed[c, i, 0:16, 0:128] = accs[c]
            zed[c, i, 16:24, 0:128] = ytile
            zed[c, i, :, 128:256] = side

    correct(vx, 0, 2, 0)

    def correct_own(x, carry):
        correct(vectors, x, x + 3, 1)
        return carry

    lax.fori_loop(0, 16, correct_own, 0)
    correct(vx, 1, 19, 2)

    def sweep3(i, carry):
        w = scale[i]
        u0, terms = stencil_terms(s2, i)
        for c in range(3):
            s3 = (1.0 - relaxation) * u0[c] + w * (residual[c, i] + terms[c])
            zed[c, i] = zed[c, i] + s3
        return carry

    lax.fori_loop(2, 20, sweep3, 0)

    def apply(x, carry):
        rz, zz = carry
        i = x + 3
        diagonal = relaxation / scale[i, 0:16, 0:128]
        u0, terms = stencil_terms(zed, i)
        for c in range(3):
            zc = u0[c][0:16, 0:128]
            image = diagonal * zc - terms[c][0:16, 0:128]
            z_out[c, x] = zc
            image_out[c, x] = image
            rz = rz + residual[c, i, 0:16, 0:128] * zc
            zz = zz + zc * image
        return rz, zz

    zero = jnp.zeros((16, 128), f32)
    rz, zz = lax.fori_loop(0, 16, apply, (zero, zero))
    for c in range(3):
        for x in range(H):
            low_out[c, x] = image_out[c, x]
            high_out[c, x] = image_out[c, 16 - H + x]
    rows = restrict_rows(vectors, image_out)
    rows = jnp.concatenate(
        [rows, jnp.sum(rz, axis=0, keepdims=True), jnp.sum(zz, axis=0, keepdims=True),
         jnp.zeros((6, 128), f32)], axis=0)
    payload[...] = lanes_of(rows)


def final_kernel(pieces, scalars, residual_in, held, image, zprev, solution_in, direction_in,
                 solution_out, residual_out, direction_out):
    totals = jnp.sum(pieces[...], axis=0, keepdims=True)
    lane = iota((1, 128), 1)
    rho = jnp.sum(jnp.where(lane == 16, totals, 0.0), axis=1, keepdims=True)
    energy = jnp.sum(jnp.where(lane == 17, totals, 0.0), axis=1, keepdims=True)
    momentum = rho / scalars[0:1, 0:1]
    step = rho / (energy - momentum * rho / scalars[1:2, 0:1])

    def plane(x, carry):
        for c in range(3):
            d = zprev[c, x] + momentum * direction_in[c, x]
            direction_out[c, x] = d
            solution_out[c, x] = solution_in[c, x] + step * d
            full = image[c, x] + momentum * held[c, x + H, 0:16, 0:128]
            residual_out[c, x] = residual_in[c, x + H, 0:16, 0:128] - step * full
        return carry

    lax.fori_loop(0, 16, plane, 0)


def both_ways(to_next, to_prev, axis):
    count = lax.axis_size(axis)
    ahead = [(i, (i + 1) % count) for i in range(count)]
    back = [((i + 1) % count, i) for i in range(count)]
    return lax.ppermute(to_next, axis, ahead), lax.ppermute(to_prev, axis, back)


def halo(own, low_edge, high_edge):
    comps = own.shape[0]
    low, high = both_ways(high_edge, low_edge, "gx")
    (ypack,) = call(pack_y_kernel, [(comps, 22, 8, 128)], [own, low, high])
    yminus, yplus = both_ways(ypack, ypack, "gy")
    (zpack,) = call(pack_z_kernel, [(comps, 24, 256)], [own, low, high, yplus, yminus])
    zminus, zplus = both_ways(zpack, zpack, GZ)
    return low, high, yplus, yminus, zplus, zminus


def share(row):
    count = lax.axis_size(EVERY)
    sent = jnp.broadcast_to(row[None], (count, 1, 128))
    return lax.all_to_all(sent, EVERY, 0, 0, tiled=True).reshape(count, 128)


def vector_halo(vectors):
    low, high = both_ways(vectors[:, :, 15], vectors[:, :, 0], "gx")
    vx = jnp.stack([low, high], axis=2)

    def edge(y):
        parts = [low[:, :, None, y], vectors[:, :, :, y], high[:, :, None, y]]
        return jnp.concatenate(parts, axis=2).transpose(1, 2, 0, 3)

    yminus, yplus = both_ways(edge(15), edge(0), "gy")
    vy = jnp.concatenate([yplus, yminus], axis=2)

    def face(z):
        middle = jnp.concatenate([low[:, :, None, :, z], vectors[:, :, :, :, z], high[:, :, None, :, z]], axis=2)
        middle = middle.transpose(1, 2, 3, 0)
        above = yplus[:, :, None, :, z]
        below = yminus[:, :, None, :, z]
        gap = jnp.zeros((3, 18, 6, 16), f32)
        return jnp.concatenate([middle, above, gap, below], axis=2)

    zminus, zplus = both_ways(face(127), face(0), GZ)
    vz = jnp.concatenate([zplus, zminus, jnp.zeros((3, 18, 24, 96), f32)], axis=3)
    return vx, vy, vz


def body(forces, mass_shift, deflation, coarse_factor, coarse_slot):
    gx, gy, gz = lax.axis_index("gx"), lax.axis_index("gy"), lax.axis_index(GZ)
    nx, ny, nz = lax.axis_size("gx"), lax.axis_size("gy"), lax.axis_size(GZ)
    n = coarse_factor.shape[0]
    tiles = coarse_factor.shape[1] // 128
    (scaled,) = call(factor_kernel, [(tiles, n, 128)], [gz[None].astype(jnp.int32), coarse_factor])
    factor = lax.all_gather(scaled, GZ)

    order = jnp.arange(coarse_slot.shape[0], dtype=jnp.int32)
    slots = (order[:, None] == coarse_slot[None, :]).astype(f32)
    moves = jnp.arange(-1, 2, dtype=jnp.int32)
    px = (gx + moves)[:, None, None]
    py = (gy + moves)[None, :, None]
    pz = (gz + moves)[None, None, :]
    valid = (px >= 0) & (px < nx) & (py >= 0) & (py < ny) & (pz >= 0) & (pz < nz)
    where = ((px * ny + py) * nz + pz).reshape(-1)
    valid = valid.reshape(-1)
    chosen = (where[:, None] == order[None, :]) & valid[:, None]
    near = jnp.sum(jnp.where(chosen[:, None, :], slots[None], 0.0), axis=2)
    near = jnp.concatenate([near, jnp.zeros((5, near.shape[1]), f32)], axis=0)
    inside = jnp.stack([gx > 0, gx < nx - 1, gy > 0, gy < ny - 1, gz > 0, gz < nz - 1, gz > 0, gz > 0])
    inside = inside.astype(jnp.int32)

    scale_own = relaxation / (mass_shift + (6.0 * off_diagonal + 2.0 * stiffer))
    fields = jnp.concatenate([forces, scale_own[None]], axis=0)
    (row,) = call(restrict_kernel, [(1, 128)], [deflation, forces])
    pieces = share(row)
    received = halo(fields, fields[:, :H], fields[:, 16 - H :])
    ext = (22, 24, 256)
    residual, scale = call(start_kernel, [(3, *ext), ext], [inside, fields, *received])
    vx, vy, vz = vector_halo(deflation)
    weight_shapes = [(48, 128), (3, 32, 128), (3, 24, 128)]
    block = (3, 16, 16, 128)
    edge = (3, H, 16, 128)
    work = [pltpu.VMEM((3, *ext), f32)] * 3
    main_outs = [block, block, edge, edge, (1, 128)]

    g, wx, wy, wz = call(
        functools.partial(coarse_kernel, 0), [(8, 256)] + weight_shapes, [pieces, slots, near, factor]
    )
    z, image, low_edge, high_edge, row = call(
        functools.partial(main_kernel, True),
        main_outs,
        [residual, scale, wx, wy, wz, deflation, vx, vy, vz],
        work,
    )
    held = jnp.zeros_like(residual)
    solution = jnp.zeros_like(forces)
    direction = jnp.zeros_like(forces)
    state = ()
    for iteration in range(1, ITERS):
        pieces = share(row)
        received = halo(image, low_edge, high_edge)
        stage = min(iteration, 2)
        g, wx, wy, wz, hdir, scalars = call(
            functools.partial(coarse_kernel, stage),
            [(8, 256)] + weight_shapes + [(8, 256), (8, 128)],
            [pieces, slots, near, factor, g, *state],
        )
        state = (hdir, scalars)
        residual, held, solution, direction, z, image, low_edge, high_edge, row = call(
            functools.partial(main_kernel, False),
            [(3, *ext), (3, *ext), block, block] + main_outs,
            [scalars, residual, held, image, *received, z, solution, direction,
             scale, wx, wy, wz, deflation, vx, vy, vz],
            work,
        )
    pieces = share(row)
    return tuple(
        call(
            final_kernel,
            [block] * 3,
            [pieces, scalars, residual, held, image, z, solution, direction],
        )
    )


def solution(mesh):
    finer = Mesh(
        mesh.devices.reshape(mesh.shape["gx"], mesh.shape["gy"], 4, 2), ("gx", "gy", "gz_0", "gz_1")
    )
    return jax.shard_map(
        body,
        mesh=finer,
        in_specs=(
            P(None, "gx", "gy", GZ),
            P("gx", "gy", GZ),
            P(None, None, "gx", "gy", GZ),
            P(GZ, None),
            P(),
        ),
        out_specs=(P(None, "gx", "gy", GZ), P(None, "gx", "gy", GZ), P(None, "gx", "gy", GZ)),
        check_vma=False,
    )
```

```python
import functools

import jax
import jax.numpy as jnp
from jax import lax
from jax.experimental import pallas as pl
from jax.experimental.pallas import tpu as pltpu
from jax.sharding import Mesh
from jax.sharding import PartitionSpec as P

ITERS = 4
GZ = ("gz_0", "gz_1")
EVERY = ("gx", "gy", "gz_0", "gz_1")

relaxation = 0.6
off_diagonal = 0.25
stiffer = 0.625
highest = lax.Precision.HIGHEST
f32 = jnp.float32
H = 3
MIB = 1 << 20


def call(kernel, outs, ins, scratch=(), after=None, limit=12, micros=2):
    vmem = pl.BlockSpec(memory_space=pltpu.VMEM)
    specs = []
    for a in ins:
        specs.append(pl.BlockSpec(memory_space=pltpu.SMEM) if a.dtype == jnp.int32 else vmem)
    if after is not None:
        specs = [pl.BlockSpec(memory_space=pl.ANY)] + specs
        ins = [after, *ins]
        inner = kernel

        def kernel(unused, *refs):
            inner(*refs)

    return pl.pallas_call(
        kernel,
        out_shape=[jax.ShapeDtypeStruct(s, f32) for s in outs],
        in_specs=specs,
        out_specs=[vmem] * len(outs),
        scratch_shapes=list(scratch),
        cost_estimate=pl.CostEstimate(flops=0, bytes_accessed=micros * 3_000_000, transcendentals=0),
        compiler_params=pltpu.CompilerParams(vmem_limit_bytes=limit * MIB),
    )(*ins)


def iota(shape, dim):
    return lax.broadcasted_iota(jnp.int32, shape, dim)


def mm(a, b):
    return jnp.dot(a, b, precision=highest, preferred_element_type=f32)


def factor_kernel(place, rows, keep, send, hold):
    j, part = place[0], place[1]
    n = rows.shape[0]
    share = keep.shape[1]
    tiles = n // 128
    start = pl.multiple_of(j * n, n)
    own = rows[:, pl.ds(start, n)]
    i0, i1 = iota((n, n), 0), iota((n, n), 1)
    eye = i0 == i1
    inverse = jnp.where(eye, 1.0 / jnp.sum(jnp.where(eye, own, 0.0), axis=1, keepdims=True), 0.0)
    size = 1
    while size < n:
        same = (i0 // (2 * size)) == (i1 // (2 * size))
        block = jnp.where(same & ((i0 // size) > (i1 // size)), own, 0.0)
        inverse = inverse - mm(inverse, mm(block, inverse))
        size *= 2
    hold[...] = inverse
    mine = hold[pl.ds(pl.multiple_of(part * share, share), share), :]

    def put(t, value):
        for u in range(tiles):
            i = t * tiles + u
            piece = value[:, u * 128 : (u + 1) * 128]
            if i < keep.shape[0]:
                keep[i] = piece
            else:
                send[i - keep.shape[0]] = piece

    for t in range(rows.shape[1] // n):

        @pl.when(t < j)
        def _():
            put(t, mm(mine, rows[:, t * n : (t + 1) * n]))

        @pl.when(t == j)
        def _():
            put(t, mine)

        @pl.when(t > j)
        def _():
            put(t, jnp.zeros_like(mine))


def fold_kernel(place, keep, received, out):
    j = place[0]
    out[...] = keep[...]
    for i in range(7):

        @pl.when(i < 7 - 2 * j)
        def _():
            out[2 * j + 2 + i] = received[i]


def lanes_of(sums):
    count = sums.shape[0]
    column = jnp.sum(sums, axis=1, keepdims=True)
    placed = jnp.where(iota((count, 128), 0) == iota((count, 128), 1), column, 0.0)
    return jnp.sum(placed, axis=0, keepdims=True)


def restrict_rows(vectors, field):
    count = vectors.shape[0]

    def plane(x, acc):
        acc = list(acc)
        for c in range(3):
            values = field[c, x]
            for k in range(count):
                part = vectors[k, c, x] * values
                acc[k] = acc[k] + (part[:8] + part[8:])
        return tuple(acc)

    acc = lax.fori_loop(0, 16, plane, tuple(jnp.zeros((8, 128), f32) for _ in range(count)))
    rows = [jnp.sum(a, axis=0, keepdims=True) for a in acc]
    return jnp.concatenate(rows, axis=0)


def face_lanes(vector_of):
    lane = iota((16, 128), 1)
    face = jnp.zeros((16, 128), f32)
    for k in range(16):
        v = vector_of(k)
        first = pltpu.roll(v, k, 1) if k else v
        face = face + jnp.where(lane == k, first, jnp.where(lane == 16 + k, pltpu.roll(v, 17 + k, 1), 0.0))
    return face


def vectors_kernel(vectors, field, out, ylow, yhigh, face):
    out[...] = lanes_of(restrict_rows(vectors, field))

    def plane(x, carry):
        for c in range(3):
            for k in range(16):
                ylow[c, x, k : k + 1] = vectors[k, c, x, 0:1]
                yhigh[c, x, k : k + 1] = vectors[k, c, x, 15:16]
            face[c, x] = face_lanes(lambda k: vectors[k, c, x])
        return carry

    lax.fori_loop(0, 16, plane, 0)


def vectors_y_kernel(ylow, yhigh, low, high, to_low, to_high):
    for c in range(3):
        for x in range(16):
            to_low[c, x + 1] = ylow[c, x]
            to_high[c, x + 1] = yhigh[c, x]
        for source, i in ((low, 0), (high, 17)):
            for k in range(16):
                to_low[c, i, k : k + 1] = source[k, c, 0:1]
                to_high[c, i, k : k + 1] = source[k, c, 15:16]


def vectors_z_kernel(face, low, high, yplus, yminus, out):
    row, lane = iota((16, 128), 0), iota((16, 128), 1)

    def lines(source, c, i):
        v = source[c, i]
        first = jnp.sum(jnp.where(lane == 0, v, 0.0), axis=1, keepdims=True)
        last = jnp.sum(jnp.where(lane == 127, v, 0.0), axis=1, keepdims=True)
        placed = jnp.where(lane == row, first, jnp.where(lane == row + 16, last, 0.0))
        return jnp.sum(placed, axis=0, keepdims=True)

    r8 = iota((8, 128), 0)

    def fill(c, i):
        out[c, i, 16:24] = jnp.where(
            r8 == 0, lines(yplus, c, i), jnp.where(r8 == 7, lines(yminus, c, i), 0.0)
        )

    def plane(x, carry):
        for c in range(3):
            out[c, x + 1, 0:16] = face[c, x]
            fill(c, x + 1)
        return carry

    lax.fori_loop(0, 16, plane, 0)
    for c in range(3):
        for source, i in ((low, 0), (high, 17)):
            out[c, i, 0:16] = face_lanes(lambda k: source[k, c])
            fill(c, i)


def pack_y(tile0, tile1):
    return jnp.where(iota(tile0.shape, tile0.ndim - 2) < 4, tile0, tile1)


def pack_y_kernel(own, low, high, out):
    for c in range(own.shape[0]):
        for x in range(H):
            out[c, x] = pack_y(low[c, x, :8], low[c, x, 8:])
            out[c, H + 16 + x] = pack_y(high[c, x, :8], high[c, x, 8:])
        for x in range(16):
            out[c, H + x] = pack_y(own[c, x, :8], own[c, x, 8:])


def plane_parts(own, low, high, c, i):
    if i < H:
        return low[c, i]
    if i < H + 16:
        return own[c, i - H]
    return high[c, i - H - 16]


def pack_z_kernel(own, low, high, yplus, yminus, out):
    lane = iota((24, 128), 1)
    edge = (lane < H) | (lane >= 128 - H)
    for c in range(own.shape[0]):
        packed = [jnp.zeros((24, 128), f32), jnp.zeros((24, 128), f32)]
        for i in range(22):
            ytile = pack_y(yplus[c, i], yminus[c, i])
            plane = jnp.concatenate([plane_parts(own, low, high, c, i), ytile], axis=0)
            plane = jnp.where(edge, plane, 0.0)
            shift = (8 * i) % 128
            if shift:
                plane = pltpu.roll(plane, shift, 1)
            packed[i // 16] = packed[i // 16] + plane
        out[c, :, :128] = packed[0]
        out[c, :, 128:] = packed[1]


def assemble(own, low, high, yplus, yminus, zplus, zminus, c, i):
    lane = iota((24, 128), 1)
    ytile = pack_y(yplus[c, i], yminus[c, i])
    centre = jnp.concatenate([plane_parts(own, low, high, c, i), ytile], axis=0)
    half = slice(0, 128) if i < 16 else slice(128, 256)
    side = jnp.where(lane % 8 < 4, zplus[c, :, half], zminus[c, :, half])
    shift = (8 * i) % 128
    if shift:
        side = pltpu.roll(side, 128 - shift, 1)
    side = jnp.where((lane < H) | (lane >= 128 - H), side, 0.0)
    return jnp.concatenate([centre, side], axis=1)


def start_kernel(inside, own, low, high, yplus, yminus, zplus, zminus, residual, scale):
    row, lane = iota((24, 256), 0), iota((24, 256), 1)
    keep = jnp.where(row < 16, 1, jnp.where(row < 20, inside[3], inside[2]))
    keep = keep * jnp.where(lane < 128, 1, jnp.where(lane < 192, inside[5], inside[4]))
    keep = jnp.where((row >= 16 + H) & (row < 24 - H), 0, keep)
    for i in range(22):
        for c in range(4):
            plane = assemble(own, low, high, yplus, yminus, zplus, zminus, c, i)
            if c < 3:
                residual[c, i] = plane
            else:
                here = keep
                if i < H:
                    here = keep * inside[0]
                elif i >= H + 16:
                    here = keep * inside[1]
                lanes_in = (lane < 128 + H) | (lane >= 256 - H)
                scale[i] = jnp.where((here > 0) & lanes_in, plane, 0.0)


def rows_to_column(row, eye):
    return jnp.sum(jnp.where(eye, row, 0.0), axis=1, keepdims=True)


def column_to_row(column, eye):
    return jnp.sum(jnp.where(eye, column, 0.0), axis=0, keepdims=True)


def coarse_kernel(stage, pieces, slots, near, factor, *refs):
    if stage == 0:
        g_out, wx, wy, wz = refs
    elif stage == 1:
        g_in, g_out, wx, wy, wz, hdir_out, scalars_out = refs
    else:
        g_in, hdir_in, scalars_in, g_out, wx, wy, wz, hdir_out, scalars_out = refs
    blocks = factor.shape[1]

    def tile(j, t):
        if t > 8:
            j, t = 7 - j, 2 * (7 - j) + t - 7
        return jnp.concatenate([factor[p, j, t] for p in range(factor.shape[0])], axis=0)

    q0, l256 = iota((128, 256), 0), iota((128, 256), 1)
    spot = (l256 // 16) == (q0 % 16)
    got = pieces[...]
    spread = jnp.where(iota((128, 256), 0) == iota((128, 256), 1) % 16, 1.0, 0.0)
    spread = jnp.where(iota((128, 256), 0) < 16, spread, 0.0)
    tiled = mm(got, spread)
    ordered = jnp.where(spot, mm(slots[...], tiled), 0.0)
    ordered = jnp.sum(ordered.reshape(8, 16, 256), axis=1)
    if stage == 0:
        g = ordered
    else:
        totals = jnp.sum(got, axis=0, keepdims=True)
        lane = iota((1, 128), 1)
        rho = jnp.sum(jnp.where(lane == 16, totals, 0.0), axis=1, keepdims=True)
        energy = jnp.sum(jnp.where(lane == 17, totals, 0.0), axis=1, keepdims=True)
        if stage == 1:
            momentum = jnp.zeros_like(rho)
            step = rho / energy
            hdir = ordered
        else:
            rho_prior = scalars_in[0:1, 0:1]
            step_prior = scalars_in[1:2, 0:1]
            momentum = rho / rho_prior
            step = rho / (energy - momentum * rho / step_prior)
            hdir = ordered + momentum * hdir_in[...]
        g = g_in[...] - step * hdir
        hdir_out[...] = hdir
        r8 = iota((8, 128), 0)
        scalars_out[...] = jnp.where(r8 == 0, rho, jnp.where(r8 == 1, step, momentum))
    g_out[...] = g
    eye = iota((128, 128), 0) == iota((128, 128), 1)
    yrow, ycol = [], []
    for j in range(blocks):
        acc = tile(j, 2 * j) * g[j : j + 1, :128] + tile(j, 2 * j + 1) * g[j : j + 1, 128:]
        for t in range(2 * j):
            acc = acc - tile(j, t) * yrow[t]
        column = jnp.sum(acc, axis=1, keepdims=True)
        for u in range(2):
            yrow.append(column_to_row(column[u * 128 : (u + 1) * 128], eye))
    vcol = [None] * blocks
    crow = [None] * blocks
    for i in range(blocks - 1, -1, -1):
        columns = []
        for u in range(2):
            t = 2 * i + u
            value = yrow[t]
            if i < blocks - 1:
                acc = tile(i + 1, t) * vcol[i + 1]
                for k in range(i + 2, blocks):
                    acc = acc + tile(k, t) * vcol[k]
                value = value - jnp.sum(acc, axis=0, keepdims=True)
            columns.append(rows_to_column(value, eye))
        vcol[i] = jnp.concatenate(columns, axis=0)
        crow[i] = jnp.concatenate(
            [jnp.sum(tile(i, 2 * i + u) * vcol[i], axis=0, keepdims=True) for u in range(2)],
            axis=1,
        )
    spread_c = jnp.concatenate(
        [jnp.broadcast_to(crow[b], (16, 256)) for b in range(blocks)], axis=0
    )
    spread_c = jnp.where(spot, spread_c, 0.0)
    fold = jnp.where(iota((256, 128), 0) % 16 == iota((256, 128), 1) % 16, 1.0, 0.0)
    by_slot = mm(spread_c, fold)
    weights = mm(near[...], by_slot)

    def w(x, y, z):
        n = x * 9 + y * 3 + z
        return weights[n : n + 1, :]

    r16, l16 = iota((16, 128), 0), iota((16, 128), 1)
    pick16 = r16 == l16
    row24, lane24 = iota((24, 128), 0), iota((24, 128), 1)
    for x in range(3):
        wx[16 * x : 16 * x + 16] = jnp.broadcast_to(
            jnp.sum(jnp.where(pick16, w(x, 1, 1), 0.0), axis=1, keepdims=True), (16, 128)
        )
        for side, y in ((0, 2), (1, 0)):
            wy[x, 16 * side : 16 * side + 16] = jnp.broadcast_to(
                jnp.sum(jnp.where(pick16, w(x, y, 1), 0.0), axis=1, keepdims=True), (16, 128)
            )

        def side_plane(z):
            return jnp.where(
                row24 < 16,
                w(x, 1, z),
                jnp.where(row24 == 16, w(x, 2, z), jnp.where(row24 == 23, w(x, 0, z), 0.0)),
            )

        wz[x] = jnp.where(
            lane24 < 16, side_plane(2), jnp.where(lane24 < 32, side_plane(0), 0.0)
        )


def stencil_terms(u, i):
    um = [u[c, i - 1] for c in range(3)]
    u0 = [u[c, i] for c in range(3)]
    up = [u[c, i + 1] for c in range(3)]

    def y(f):
        return pltpu.roll(f, 23, 0), pltpu.roll(f, 1, 0)

    def z(f):
        return pltpu.roll(f, 255, 1), pltpu.roll(f, 1, 1)

    dx = [up[c] - um[c] for c in range(3)]
    sx = [up[c] + um[c] for c in range(3)]
    yp, ym, zp, zm = [], [], [], []
    for c in range(3):
        a, b = y(u0[c])
        yp.append(a)
        ym.append(b)
        a, b = z(u0[c])
        zp.append(a)
        zm.append(b)
    sy = [yp[c] + ym[c] for c in range(3)]
    sz = [zp[c] + zm[c] for c in range(3)]
    a, b = y(dx[1])
    mixed0 = a - b
    a, b = z(dx[2])
    mixed0 = mixed0 + (a - b)
    a, b = y(dx[0] + (zp[2] - zm[2]))
    mixed1 = a - b
    a, b = z(dx[0] + (yp[1] - ym[1]))
    mixed2 = a - b
    mixed = [mixed0, mixed1, mixed2]
    own = [sx[0], sy[1], sz[2]]
    return u0, [
        off_diagonal * (sx[c] + sy[c] + sz[c]) + stiffer * own[c] + (0.25 * stiffer) * mixed[c]
        for c in range(3)
    ]


def correct_kernel(first, *refs):
    if first:
        wx, wy, wz, vectors, vx, vy, vz, zed = refs
    else:
        (scalars, zprev, solution_in, direction_in, wx, wy, wz, vectors, vx, vy, vz,
         zed, solution_out, direction_out) = refs
        step = scalars[1:2, 0:1]
        momentum = scalars[2:3, 0:1]

        def advance(x, carry):
            for c in range(3):
                d = zprev[c, x] + momentum * direction_in[c, x]
                direction_out[c, x] = d
                solution_out[c, x] = solution_in[c, x] + step * d
            return carry

        lax.fori_loop(0, 16, advance, 0)

    def correct(source, x, i, region):
        accs = []
        for c in range(3):
            acc = wx[pl.ds(16 * region, 1), :] * source[0, c, x]
            for k in range(1, 16):
                acc = acc + wx[pl.ds(16 * region + k, 1), :] * source[k, c, x]
            accs.append(acc)
        lane = iota((24, 128), 1)
        row = iota((8, 128), 0)
        for c in range(3):
            prod = vy[c, i] * wy[region]
            plus = jnp.sum(prod[:16], axis=0, keepdims=True)
            minus = jnp.sum(prod[16:], axis=0, keepdims=True)
            ytile = jnp.where(row == 0, plus, jnp.where(row == 7, minus, 0.0))
            prod = vz[c, i] * wz[region]
            plus = jnp.sum(jnp.where(lane < 16, prod, 0.0), axis=1, keepdims=True)
            minus = jnp.sum(jnp.where(lane >= 16, prod, 0.0), axis=1, keepdims=True)
            side = jnp.where(lane == 0, plus, jnp.where(lane == 127, minus, 0.0))
            zed[c, i, 0:16, 0:128] = accs[c]
            zed[c, i, 16:24, 0:128] = ytile
            zed[c, i, :, 128:256] = side

    correct(vx, 0, 0, 0)

    def correct_own(x, carry):
        correct(vectors, x, x + 1, 1)
        return carry

    lax.fori_loop(0, 16, correct_own, 0)
    correct(vx, 1, 17, 2)


def main_kernel(first, *refs):
    if first:
        (residual_in, scale, vectors, correction, z_out, image_out, low_out, high_out, payload,
         s1, s2, zed) = refs
        residual = residual_in
    else:
        (scalars, residual_in, held_in, own, low, high, yplus, yminus, zplus, zminus, scale,
         vectors, correction, residual, held,
         z_out, image_out, low_out, high_out, payload, s1, s2, zed) = refs
        step = scalars[1:2, 0:1]
        momentum = scalars[2:3, 0:1]
        for i in range(22):
            for c in range(3):
                image = assemble(own, low, high, yplus, yminus, zplus, zminus, c, i)
                image = image + momentum * held_in[c, i]
                held[c, i] = image
                residual[c, i] = residual_in[c, i] - step * image

    def sweep1(i, carry):
        w = scale[i]
        for c in range(3):
            s1[c, i] = w * residual[c, i]
        return carry

    lax.fori_loop(0, 22, sweep1, 0)

    def sweep2(i, carry):
        w = scale[i]
        u0, terms = stencil_terms(s1, i)
        for c in range(3):
            s2[c, i] = (1.0 - relaxation) * u0[c] + w * (residual[c, i] + terms[c])
        return carry

    lax.fori_loop(1, 21, sweep2, 0)

    def sweep3(i, carry):
        w = scale[i]
        u0, terms = stencil_terms(s2, i)
        for c in range(3):
            s3 = (1.0 - relaxation) * u0[c] + w * (residual[c, i] + terms[c])
            zed[c, i] = correction[c, i - 2] + s3
        return carry

    lax.fori_loop(2, 20, sweep3, 0)

    def apply(x, carry):
        rz, zz = carry
        i = x + 3
        diagonal = relaxation / scale[i, 0:16, 0:128]
        u0, terms = stencil_terms(zed, i)
        for c in range(3):
            zc = u0[c][0:16, 0:128]
            image = diagonal * zc - terms[c][0:16, 0:128]
            z_out[c, x] = zc
            image_out[c, x] = image
            rz = rz + residual[c, i, 0:16, 0:128] * zc
            zz = zz + zc * image
        return rz, zz

    zero = jnp.zeros((16, 128), f32)
    rz, zz = lax.fori_loop(0, 16, apply, (zero, zero))
    for c in range(3):
        for x in range(H):
            low_out[c, x] = image_out[c, x]
            high_out[c, x] = image_out[c, 16 - H + x]
    rows = restrict_rows(vectors, image_out)
    rows = jnp.concatenate(
        [rows, jnp.sum(rz, axis=0, keepdims=True), jnp.sum(zz, axis=0, keepdims=True),
         jnp.zeros((6, 128), f32)], axis=0)
    payload[...] = lanes_of(rows)


def final_kernel(pieces, scalars, residual_in, held, image, zprev, solution_in, direction_in,
                 solution_out, residual_out, direction_out):
    totals = jnp.sum(pieces[...], axis=0, keepdims=True)
    lane = iota((1, 128), 1)
    rho = jnp.sum(jnp.where(lane == 16, totals, 0.0), axis=1, keepdims=True)
    energy = jnp.sum(jnp.where(lane == 17, totals, 0.0), axis=1, keepdims=True)
    momentum = rho / scalars[0:1, 0:1]
    step = rho / (energy - momentum * rho / scalars[1:2, 0:1])

    def plane(x, carry):
        for c in range(3):
            d = zprev[c, x] + momentum * direction_in[c, x]
            direction_out[c, x] = d
            solution_out[c, x] = solution_in[c, x] + step * d
            full = image[c, x] + momentum * held[c, x + H, 0:16, 0:128]
            residual_out[c, x] = residual_in[c, x + H, 0:16, 0:128] - step * full
        return carry

    lax.fori_loop(0, 16, plane, 0)


def both_ways(to_next, to_prev, axis):
    count = lax.axis_size(axis)
    ahead = [(i, (i + 1) % count) for i in range(count)]
    back = [((i + 1) % count, i) for i in range(count)]
    return lax.ppermute(to_next, axis, ahead), lax.ppermute(to_prev, axis, back)


def halo(own, low_edge, high_edge, pieces=None, middle=None):
    comps = own.shape[0]
    low, high = both_ways(high_edge, low_edge, "gx")
    (ypack,) = call(pack_y_kernel, [(comps, 22, 8, 128)], [own, low, high], after=pieces)
    yminus, yplus = both_ways(ypack, ypack, "gy")
    done = middle(ypack) if middle else None
    (zpack,) = call(
        pack_z_kernel, [(comps, 24, 256)], [own, low, high, yplus, yminus],
        after=done[0] if middle else None,
    )
    zminus, zplus = both_ways(zpack, zpack, GZ)
    return (low, high, yplus, yminus, zplus, zminus), zpack, done


def share(row):
    count = lax.axis_size(EVERY)
    sent = jnp.broadcast_to(row[None], (count, 1, 128))
    return lax.all_to_all(sent, EVERY, 0, 0, tiled=True).reshape(count, 128)


def vector_halo(vectors, ylow, yhigh, face):
    low, high = both_ways(vectors[:, :, 15], vectors[:, :, 0], "gx")
    shape = (3, 18, 16, 128)
    to_low, to_high = call(vectors_y_kernel, [shape, shape], [ylow, yhigh, low, high])
    yminus, yplus = both_ways(to_high, to_low, "gy")
    (packed,) = call(vectors_z_kernel, [(3, 18, 24, 128)], [face, low, high, yplus, yminus])
    zminus, zplus = both_ways(packed, packed, GZ)
    vz = jnp.where(iota(zplus.shape, 3) < 16, zplus, zminus)
    return jnp.stack([low, high], axis=2), jnp.concatenate([yplus, yminus], axis=2), vz


def body(forces, mass_shift, deflation, coarse_factor, coarse_slot):
    gx, gy, gz = lax.axis_index("gx"), lax.axis_index("gy"), lax.axis_index(GZ)
    nx, ny, nz = lax.axis_size("gx"), lax.axis_size("gy"), lax.axis_size(GZ)
    place = jnp.stack([gz, gy]).astype(jnp.int32)
    keep, send = call(
        factor_kernel, [(9, 64, 128), (7, 64, 128)], [place, coarse_factor],
        [pltpu.VMEM((256, 256), f32)],
    )
    received = lax.ppermute(send, GZ, [(i, 7 - i) for i in range(8)])
    (folded,) = call(fold_kernel, [(9, 64, 128)], [place, keep, received])
    factor = lax.all_gather(folded, ("gy", *GZ)).reshape(4, 8, 9, 64, 128)

    order = jnp.arange(coarse_slot.shape[0], dtype=jnp.int32)
    slots = (order[:, None] == coarse_slot[None, :]).astype(f32)
    moves = jnp.arange(-1, 2, dtype=jnp.int32)
    px = (gx + moves)[:, None, None]
    py = (gy + moves)[None, :, None]
    pz = (gz + moves)[None, None, :]
    valid = (px >= 0) & (px < nx) & (py >= 0) & (py < ny) & (pz >= 0) & (pz < nz)
    where = ((px * ny + py) * nz + pz).reshape(-1)
    valid = valid.reshape(-1)
    chosen = (where[:, None] == order[None, :]) & valid[:, None]
    near = jnp.sum(jnp.where(chosen[:, None, :], slots[None], 0.0), axis=2)
    near = jnp.concatenate([near, jnp.zeros((5, near.shape[1]), f32)], axis=0)
    inside = jnp.stack([gx > 0, gx < nx - 1, gy > 0, gy < ny - 1, gz > 0, gz < nz - 1, gz > 0, gz > 0])
    inside = inside.astype(jnp.int32)

    scale_own = relaxation / (mass_shift + (6.0 * off_diagonal + 2.0 * stiffer))
    fields = jnp.concatenate([forces, scale_own[None]], axis=0)
    block = (3, 16, 16, 128)
    lines = (3, 16, 16, 128)
    row, ylow, yhigh, face = call(
        vectors_kernel, [(1, 128), lines, lines, lines], [deflation, forces], micros=6
    )
    pieces = share(row)
    received, _, _ = halo(fields, fields[:, :H], fields[:, 16 - H :])
    ext = (22, 24, 256)
    residual, scale = call(start_kernel, [(3, *ext), ext], [inside, fields, *received])
    around = vector_halo(deflation, ylow, yhigh, face)
    weight_shapes = [(48, 128), (3, 32, 128), (3, 24, 128)]
    edge = (3, H, 16, 128)
    work = [pltpu.VMEM((3, *ext), f32)] * 3
    main_outs = [block, block, edge, edge, (1, 128)]
    patch = (3, 18, 24, 256)

    g, wx, wy, wz = call(
        functools.partial(coarse_kernel, 0), [(8, 256)] + weight_shapes,
        [pieces, slots, near, factor], limit=20, micros=8,
    )
    (correction,) = call(
        functools.partial(correct_kernel, True), [patch], [wx, wy, wz, deflation, *around],
        limit=20, micros=6,
    )
    z, image, low_edge, high_edge, row = call(
        functools.partial(main_kernel, True), main_outs,
        [residual, scale, deflation, correction], work, limit=28, micros=10,
    )
    held = jnp.zeros_like(residual)
    solution = jnp.zeros_like(forces)
    direction = jnp.zeros_like(forces)
    state = ()
    for iteration in range(1, ITERS):
        pieces = share(row)

        def coarse(token):
            return call(
                functools.partial(coarse_kernel, min(iteration, 2)),
                [(8, 256)] + weight_shapes + [(8, 256), (8, 128)],
                [pieces, slots, near, factor, g, *state],
                after=token, limit=20, micros=8,
            )

        received, zpack, done = halo(image, low_edge, high_edge, pieces, coarse)
        g, wx, wy, wz, hdir, scalars = done
        state = (hdir, scalars)
        correction, solution, direction = call(
            functools.partial(correct_kernel, False), [patch, block, block],
            [scalars, z, solution, direction, wx, wy, wz, deflation, *around],
            after=zpack, limit=20, micros=6,
        )
        residual, held, z, image, low_edge, high_edge, row = call(
            functools.partial(main_kernel, False), [(3, *ext), (3, *ext)] + main_outs,
            [scalars, residual, held, image, *received, scale, deflation, correction],
            work, limit=28, micros=10,
        )
    pieces = share(row)
    return tuple(
        call(
            final_kernel,
            [block] * 3,
            [pieces, scalars, residual, held, image, z, solution, direction],
        )
    )


def solution(mesh):
    finer = Mesh(
        mesh.devices.reshape(mesh.shape["gx"], mesh.shape["gy"], 4, 2), ("gx", "gy", "gz_0", "gz_1")
    )
    return jax.shard_map(
        body,
        mesh=finer,
        in_specs=(
            P(None, "gx", "gy", GZ),
            P("gx", "gy", GZ),
            P(None, None, "gx", "gy", GZ),
            P(GZ, None),
            P(),
        ),
        out_specs=(P(None, "gx", "gy", GZ), P(None, "gx", "gy", GZ), P(None, "gx", "gy", GZ)),
        check_vma=False,
    )
```

```python
import functools

import jax
import jax.numpy as jnp
from jax import lax
from jax.experimental import pallas as pl
from jax.experimental.pallas import tpu as pltpu
from jax.sharding import Mesh
from jax.sharding import PartitionSpec as P

ITERS = 4
GZ = ("gz_0", "gz_1")
EVERY = ("gx", "gy", "gz_0", "gz_1")

relaxation = 0.6
off_diagonal = 0.25
stiffer = 0.625
highest = lax.Precision.HIGHEST
f32 = jnp.float32
H = 3
MIB = 1 << 20


def call(kernel, outs, ins, scratch=(), after=None, limit=12, micros=2):
    vmem = pl.BlockSpec(memory_space=pltpu.VMEM)
    specs = []
    for a in ins:
        specs.append(pl.BlockSpec(memory_space=pltpu.SMEM) if a.dtype == jnp.int32 else vmem)
    if after is not None:
        specs = [pl.BlockSpec(memory_space=pl.ANY)] + specs
        ins = [after, *ins]
        inner = kernel

        def kernel(unused, *refs):
            inner(*refs)

    return pl.pallas_call(
        kernel,
        out_shape=[jax.ShapeDtypeStruct(s, f32) for s in outs],
        in_specs=specs,
        out_specs=[vmem] * len(outs),
        scratch_shapes=list(scratch),
        cost_estimate=pl.CostEstimate(flops=0, bytes_accessed=micros * 3_000_000, transcendentals=0),
        compiler_params=pltpu.CompilerParams(vmem_limit_bytes=limit * MIB),
    )(*ins)


def iota(shape, dim):
    return lax.broadcasted_iota(jnp.int32, shape, dim)


def mm(a, b):
    return jnp.dot(a, b, precision=highest, preferred_element_type=f32)


def factor_kernel(place, rows, keep, send, hold):
    j, part = place[0], place[1]
    n = rows.shape[0]
    share = keep.shape[1]
    tiles = n // 128
    start = pl.multiple_of(j * n, n)
    own = rows[:, pl.ds(start, n)]
    i0, i1 = iota((n, n), 0), iota((n, n), 1)
    eye = i0 == i1
    across = 1.0 / jnp.sum(jnp.where(eye, own, 0.0), axis=1, keepdims=True)
    down = 1.0 / jnp.sum(jnp.where(eye, own, 0.0), axis=0, keepdims=True)
    lower = jnp.where(((i0 // 4) == (i1 // 4)) & (i0 > i1), own, 0.0) * across
    square = mm(lower, lower)
    inverse = jnp.where(eye, 1.0, 0.0) - lower + square - mm(lower, square)
    inverse = inverse * down
    size = 4
    while size < n:
        same = (i0 // (2 * size)) == (i1 // (2 * size))
        block = jnp.where(same & ((i0 // size) > (i1 // size)), own, 0.0)
        inverse = inverse - mm(inverse, mm(block, inverse))
        size *= 2
    hold[...] = inverse
    mine = hold[pl.ds(pl.multiple_of(part * share, share), share), :]

    def put(t, value):
        for u in range(tiles):
            i = t * tiles + u
            piece = value[:, u * 128 : (u + 1) * 128]
            if i < keep.shape[0]:
                keep[i] = piece
            else:
                send[i - keep.shape[0]] = piece

    for t in range(rows.shape[1] // n):

        @pl.when(t < j)
        def _():
            put(t, mm(mine, rows[:, t * n : (t + 1) * n]))

        @pl.when(t == j)
        def _():
            put(t, mine)

        @pl.when(t > j)
        def _():
            put(t, jnp.zeros_like(mine))


def fold_kernel(place, keep, received, out):
    j = place[0]
    out[...] = keep[...]
    for i in range(7):

        @pl.when(i < 7 - 2 * j)
        def _():
            out[2 * j + 2 + i] = received[i]


def lanes_of(sums):
    count = sums.shape[0]
    column = jnp.sum(sums, axis=1, keepdims=True)
    placed = jnp.where(iota((count, 128), 0) == iota((count, 128), 1), column, 0.0)
    return jnp.sum(placed, axis=0, keepdims=True)


def restrict_rows(vectors, field):
    count = vectors.shape[0]

    def plane(x, acc):
        acc = list(acc)
        for c in range(3):
            values = field[c, x]
            for k in range(count):
                part = vectors[k, c, x] * values
                acc[k] = acc[k] + (part[:8] + part[8:])
        return tuple(acc)

    acc = lax.fori_loop(0, 16, plane, tuple(jnp.zeros((8, 128), f32) for _ in range(count)))
    rows = [jnp.sum(a, axis=0, keepdims=True) for a in acc]
    return jnp.concatenate(rows, axis=0)


def face_lanes(vector_of):
    lane = iota((16, 128), 1)
    face = jnp.zeros((16, 128), f32)
    for k in range(16):
        v = vector_of(k)
        first = pltpu.roll(v, k, 1) if k else v
        face = face + jnp.where(lane == k, first, jnp.where(lane == 16 + k, pltpu.roll(v, 17 + k, 1), 0.0))
    return face


def vectors_kernel(vectors, field, out, ylow, yhigh, face):
    out[...] = jnp.broadcast_to(lanes_of(restrict_rows(vectors, field)), (128, 128))

    def plane(x, carry):
        for c in range(3):
            for k in range(16):
                ylow[c, x, k : k + 1] = vectors[k, c, x, 0:1]
                yhigh[c, x, k : k + 1] = vectors[k, c, x, 15:16]
            face[c, x] = face_lanes(lambda k: vectors[k, c, x])
        return carry

    lax.fori_loop(0, 16, plane, 0)


def vectors_y_kernel(ylow, yhigh, low, high, to_low, to_high):
    for c in range(3):
        for x in range(16):
            to_low[c, x + 1] = ylow[c, x]
            to_high[c, x + 1] = yhigh[c, x]
        for source, i in ((low, 0), (high, 17)):
            for k in range(16):
                to_low[c, i, k : k + 1] = source[k, c, 0:1]
                to_high[c, i, k : k + 1] = source[k, c, 15:16]


def vectors_z_kernel(face, low, high, yplus, yminus, out):
    row, lane = iota((16, 128), 0), iota((16, 128), 1)

    def lines(source, c, i):
        v = source[c, i]
        first = jnp.sum(jnp.where(lane == 0, v, 0.0), axis=1, keepdims=True)
        last = jnp.sum(jnp.where(lane == 127, v, 0.0), axis=1, keepdims=True)
        placed = jnp.where(lane == row, first, jnp.where(lane == row + 16, last, 0.0))
        return jnp.sum(placed, axis=0, keepdims=True)

    r8 = iota((8, 128), 0)

    for c in range(3):
        for group in range(5):
            packed = jnp.zeros((24, 128), f32)
            for i in range(4 * group, min(4 * group + 4, 18)):
                if i == 0:
                    own = face_lanes(lambda k: low[k, c])
                elif i == 17:
                    own = face_lanes(lambda k: high[k, c])
                else:
                    own = face[c, i - 1]
                line = jnp.where(
                    r8 == 0, lines(yplus, c, i), jnp.where(r8 == 7, lines(yminus, c, i), 0.0)
                )
                plane = jnp.concatenate([own, line], axis=0)
                if i % 4:
                    plane = pltpu.roll(plane, 32 * (i % 4), 1)
                packed = packed + plane
            out[c, group] = packed


def vectors_end_kernel(low, high, yplus, yminus, zplus, zminus, vx, vy, vz):
    lane = iota((24, 128), 1)
    vx[:, :, 0] = low[...]
    vx[:, :, 1] = high[...]
    vy[:, :, 0:16] = yplus[...]
    vy[:, :, 16:32] = yminus[...]
    for c in range(3):
        for i in range(18):
            plane = jnp.where(lane % 32 < 16, zplus[c, i // 4], zminus[c, i // 4])
            if i % 4:
                plane = pltpu.roll(plane, 128 - 32 * (i % 4), 1)
            vz[c, i] = plane


def pack_y(tile0, tile1):
    return jnp.where(iota(tile0.shape, tile0.ndim - 2) < 4, tile0, tile1)


def pack_y_kernel(own, low, high, out):
    for c in range(own.shape[0]):
        for x in range(H):
            out[c, x] = pack_y(low[c, x, :8], low[c, x, 8:])
            out[c, H + 16 + x] = pack_y(high[c, x, :8], high[c, x, 8:])
        for x in range(16):
            out[c, H + x] = pack_y(own[c, x, :8], own[c, x, 8:])


def plane_parts(own, low, high, c, i):
    if i < H:
        return low[c, i]
    if i < H + 16:
        return own[c, i - H]
    return high[c, i - H - 16]


def pack_z_kernel(own, low, high, yplus, yminus, out):
    lane = iota((24, 128), 1)
    edge = (lane < H) | (lane >= 128 - H)
    for c in range(own.shape[0]):
        packed = [jnp.zeros((24, 128), f32), jnp.zeros((24, 128), f32)]
        for i in range(22):
            ytile = pack_y(yplus[c, i], yminus[c, i])
            plane = jnp.concatenate([plane_parts(own, low, high, c, i), ytile], axis=0)
            plane = jnp.where(edge, plane, 0.0)
            shift = (8 * i) % 128
            if shift:
                plane = pltpu.roll(plane, shift, 1)
            packed[i // 16] = packed[i // 16] + plane
        out[c, :, :128] = packed[0]
        out[c, :, 128:] = packed[1]


def assemble(own, low, high, yplus, yminus, zplus, zminus, c, i):
    lane = iota((24, 128), 1)
    ytile = pack_y(yplus[c, i], yminus[c, i])
    centre = jnp.concatenate([plane_parts(own, low, high, c, i), ytile], axis=0)
    half = slice(0, 128) if i < 16 else slice(128, 256)
    side = jnp.where(lane % 8 < 4, zplus[c, :, half], zminus[c, :, half])
    shift = (8 * i) % 128
    if shift:
        side = pltpu.roll(side, 128 - shift, 1)
    side = jnp.where((lane < H) | (lane >= 128 - H), side, 0.0)
    return jnp.concatenate([centre, side], axis=1)


def start_kernel(inside, own, low, high, yplus, yminus, zplus, zminus, residual, scale):
    row, lane = iota((24, 256), 0), iota((24, 256), 1)
    keep = jnp.where(row < 16, 1, jnp.where(row < 20, inside[3], inside[2]))
    keep = keep * jnp.where(lane < 128, 1, jnp.where(lane < 192, inside[5], inside[4]))
    keep = jnp.where((row >= 16 + H) & (row < 24 - H), 0, keep)
    for i in range(22):
        for c in range(4):
            plane = assemble(own, low, high, yplus, yminus, zplus, zminus, c, i)
            if c < 3:
                residual[c, i] = plane
            else:
                here = keep
                if i < H:
                    here = keep * inside[0]
                elif i >= H + 16:
                    here = keep * inside[1]
                lanes_in = (lane < 128 + H) | (lane >= 256 - H)
                scale[i] = jnp.where((here > 0) & lanes_in, plane, 0.0)


def rows_to_column(row, eye):
    return jnp.sum(jnp.where(eye, row, 0.0), axis=1, keepdims=True)


def column_to_row(column, eye):
    return jnp.sum(jnp.where(eye, column, 0.0), axis=0, keepdims=True)


def coarse_kernel(stage, pieces, slots, near, factor, *refs):
    if stage == 0:
        g_out, wx, wy, wz = refs
    elif stage == 1:
        g_in, g_out, wx, wy, wz, hdir_out, scalars_out = refs
    else:
        g_in, hdir_in, scalars_in, g_out, wx, wy, wz, hdir_out, scalars_out = refs
    blocks = factor.shape[1]

    def tile(j, t):
        if t > 8:
            j, t = 7 - j, 2 * (7 - j) + t - 7
        return jnp.concatenate([factor[p, j, t] for p in range(factor.shape[0])], axis=0)

    q0, l256 = iota((128, 256), 0), iota((128, 256), 1)
    spot = (l256 // 16) == (q0 % 16)
    got = pieces[...]
    spread = jnp.where(iota((128, 256), 0) == iota((128, 256), 1) % 16, 1.0, 0.0)
    spread = jnp.where(iota((128, 256), 0) < 16, spread, 0.0)
    tiled = mm(got, spread)
    ordered = jnp.where(spot, mm(slots[...], tiled), 0.0)
    ordered = jnp.sum(ordered.reshape(8, 16, 256), axis=1)
    if stage == 0:
        g = ordered
    else:
        totals = jnp.sum(got, axis=0, keepdims=True)
        lane = iota((1, 128), 1)
        rho = jnp.sum(jnp.where(lane == 16, totals, 0.0), axis=1, keepdims=True)
        energy = jnp.sum(jnp.where(lane == 17, totals, 0.0), axis=1, keepdims=True)
        if stage == 1:
            momentum = jnp.zeros_like(rho)
            step = rho / energy
            hdir = ordered
        else:
            rho_prior = scalars_in[0:1, 0:1]
            step_prior = scalars_in[1:2, 0:1]
            momentum = rho / rho_prior
            step = rho / (energy - momentum * rho / step_prior)
            hdir = ordered + momentum * hdir_in[...]
        g = g_in[...] - step * hdir
        hdir_out[...] = hdir
        r8 = iota((8, 128), 0)
        scalars_out[...] = jnp.where(r8 == 0, rho, jnp.where(r8 == 1, step, momentum))
    g_out[...] = g
    eye = iota((128, 128), 0) == iota((128, 128), 1)
    yrow, ycol = [], []
    for j in range(blocks):
        acc = tile(j, 2 * j) * g[j : j + 1, :128] + tile(j, 2 * j + 1) * g[j : j + 1, 128:]
        for t in range(2 * j):
            acc = acc - tile(j, t) * yrow[t]
        column = jnp.sum(acc, axis=1, keepdims=True)
        for u in range(2):
            yrow.append(column_to_row(column[u * 128 : (u + 1) * 128], eye))
    vcol = [None] * blocks
    crow = [None] * blocks
    for i in range(blocks - 1, -1, -1):
        columns = []
        for u in range(2):
            t = 2 * i + u
            value = yrow[t]
            if i < blocks - 1:
                acc = tile(i + 1, t) * vcol[i + 1]
                for k in range(i + 2, blocks):
                    acc = acc + tile(k, t) * vcol[k]
                value = value - jnp.sum(acc, axis=0, keepdims=True)
            columns.append(rows_to_column(value, eye))
        vcol[i] = jnp.concatenate(columns, axis=0)
        crow[i] = jnp.concatenate(
            [jnp.sum(tile(i, 2 * i + u) * vcol[i], axis=0, keepdims=True) for u in range(2)],
            axis=1,
        )
    spread_c = jnp.concatenate(
        [jnp.broadcast_to(crow[b], (16, 256)) for b in range(blocks)], axis=0
    )
    spread_c = jnp.where(spot, spread_c, 0.0)
    fold = jnp.where(iota((256, 128), 0) % 16 == iota((256, 128), 1) % 16, 1.0, 0.0)
    by_slot = mm(spread_c, fold)
    weights = mm(near[...], by_slot)

    def w(x, y, z):
        n = x * 9 + y * 3 + z
        return weights[n : n + 1, :]

    r16, l16 = iota((16, 128), 0), iota((16, 128), 1)
    pick16 = r16 == l16
    row24, lane24 = iota((24, 128), 0), iota((24, 128), 1)
    for x in range(3):
        wx[16 * x : 16 * x + 16] = jnp.broadcast_to(
            jnp.sum(jnp.where(pick16, w(x, 1, 1), 0.0), axis=1, keepdims=True), (16, 128)
        )
        for side, y in ((0, 2), (1, 0)):
            wy[x, 16 * side : 16 * side + 16] = jnp.broadcast_to(
                jnp.sum(jnp.where(pick16, w(x, y, 1), 0.0), axis=1, keepdims=True), (16, 128)
            )

        def side_plane(z):
            return jnp.where(
                row24 < 16,
                w(x, 1, z),
                jnp.where(row24 == 16, w(x, 2, z), jnp.where(row24 == 23, w(x, 0, z), 0.0)),
            )

        wz[x] = jnp.where(
            lane24 < 16, side_plane(2), jnp.where(lane24 < 32, side_plane(0), 0.0)
        )


def stencil_terms(u, i):
    um = [u[c, i - 1] for c in range(3)]
    u0 = [u[c, i] for c in range(3)]
    up = [u[c, i + 1] for c in range(3)]

    def y(f):
        return pltpu.roll(f, 23, 0), pltpu.roll(f, 1, 0)

    def z(f):
        return pltpu.roll(f, 255, 1), pltpu.roll(f, 1, 1)

    dx = [up[c] - um[c] for c in range(3)]
    sx = [up[c] + um[c] for c in range(3)]
    yp, ym, zp, zm = [], [], [], []
    for c in range(3):
        a, b = y(u0[c])
        yp.append(a)
        ym.append(b)
        a, b = z(u0[c])
        zp.append(a)
        zm.append(b)
    sy = [yp[c] + ym[c] for c in range(3)]
    sz = [zp[c] + zm[c] for c in range(3)]
    a, b = y(dx[1])
    mixed0 = a - b
    a, b = z(dx[2])
    mixed0 = mixed0 + (a - b)
    a, b = y(dx[0] + (zp[2] - zm[2]))
    mixed1 = a - b
    a, b = z(dx[0] + (yp[1] - ym[1]))
    mixed2 = a - b
    mixed = [mixed0, mixed1, mixed2]
    own = [sx[0], sy[1], sz[2]]
    return u0, [
        off_diagonal * (sx[c] + sy[c] + sz[c]) + stiffer * own[c] + (0.25 * stiffer) * mixed[c]
        for c in range(3)
    ]


def correct_kernel(first, *refs):
    if first:
        wx, wy, wz, vectors, vx, vy, vz, zed = refs
    else:
        (scalars, zprev, solution_in, direction_in, wx, wy, wz, vectors, vx, vy, vz,
         zed, solution_out, direction_out) = refs
        step = scalars[1:2, 0:1]
        momentum = scalars[2:3, 0:1]

        def advance(x, carry):
            for c in range(3):
                d = zprev[c, x] + momentum * direction_in[c, x]
                direction_out[c, x] = d
                solution_out[c, x] = solution_in[c, x] + step * d
            return carry

        lax.fori_loop(0, 16, advance, 0)

    def correct(source, x, i, region):
        accs = []
        for c in range(3):
            acc = wx[pl.ds(16 * region, 1), :] * source[0, c, x]
            for k in range(1, 16):
                acc = acc + wx[pl.ds(16 * region + k, 1), :] * source[k, c, x]
            accs.append(acc)
        lane = iota((24, 128), 1)
        row = iota((8, 128), 0)
        for c in range(3):
            prod = vy[c, i] * wy[region]
            plus = jnp.sum(prod[:16], axis=0, keepdims=True)
            minus = jnp.sum(prod[16:], axis=0, keepdims=True)
            ytile = jnp.where(row == 0, plus, jnp.where(row == 7, minus, 0.0))
            prod = vz[c, i] * wz[region]
            plus = jnp.sum(jnp.where(lane < 16, prod, 0.0), axis=1, keepdims=True)
            minus = jnp.sum(jnp.where(lane >= 16, prod, 0.0), axis=1, keepdims=True)
            side = jnp.where(lane == 0, plus, jnp.where(lane == 127, minus, 0.0))
            zed[c, i, 0:16, 0:128] = accs[c]
            zed[c, i, 16:24, 0:128] = ytile
            zed[c, i, :, 128:256] = side

    correct(vx, 0, 0, 0)

    def correct_own(x, carry):
        correct(vectors, x, x + 1, 1)
        return carry

    lax.fori_loop(0, 16, correct_own, 0)
    correct(vx, 1, 17, 2)


def sweeps(residual, scale, s1, s2, emit):
    def sweep1(i, carry):
        w = scale[i]
        for c in range(3):
            s1[c, i] = w * residual[c, i]
        return carry

    lax.fori_loop(0, 22, sweep1, 0, unroll=2)

    def sweep2(i, carry):
        w = scale[i]
        u0, terms = stencil_terms(s1, i)
        for c in range(3):
            s2[c, i] = (1.0 - relaxation) * u0[c] + w * (residual[c, i] + terms[c])
        return carry

    lax.fori_loop(1, 21, sweep2, 0, unroll=2)

    def sweep3(i, carry):
        w = scale[i]
        u0, terms = stencil_terms(s2, i)
        for c in range(3):
            emit(c, i, (1.0 - relaxation) * u0[c] + w * (residual[c, i] + terms[c]))
        return carry

    lax.fori_loop(2, 20, sweep3, 0, unroll=2)


def sweeps_kernel(residual, scale, smooth, s1, s2):
    def emit(c, i, value):
        smooth[c, i - 2] = value

    sweeps(residual, scale, s1, s2, emit)


def main_kernel(first, *refs):
    if first:
        (residual_in, scale, vectors, correction, smooth, z_out, image_out, low_out, high_out, payload,
         zed) = refs
        residual = residual_in
    else:
        (scalars, residual_in, held_in, own, low, high, yplus, yminus, zplus, zminus, scale,
         vectors, correction, residual, held,
         z_out, image_out, low_out, high_out, payload, s1, s2, zed) = refs
        step = scalars[1:2, 0:1]
        momentum = scalars[2:3, 0:1]
        for i in range(22):
            for c in range(3):
                image = assemble(own, low, high, yplus, yminus, zplus, zminus, c, i)
                image = image + momentum * held_in[c, i]
                held[c, i] = image
                residual[c, i] = residual_in[c, i] - step * image

    if first:
        for i in range(2, 20):
            for c in range(3):
                zed[c, i] = smooth[c, i - 2] + correction[c, i - 2]
    else:

        def emit(c, i, value):
            zed[c, i] = correction[c, i - 2] + value

        sweeps(residual, scale, s1, s2, emit)

    def apply(x, carry):
        rz, zz = carry
        i = x + 3
        diagonal = relaxation / scale[i, 0:16, 0:128]
        u0, terms = stencil_terms(zed, i)
        for c in range(3):
            zc = u0[c][0:16, 0:128]
            image = diagonal * zc - terms[c][0:16, 0:128]
            z_out[c, x] = zc
            image_out[c, x] = image
            rz = rz + residual[c, i, 0:16, 0:128] * zc
            zz = zz + zc * image
        return rz, zz

    zero = jnp.zeros((16, 128), f32)
    rz, zz = lax.fori_loop(0, 16, apply, (zero, zero), unroll=2)
    for c in range(3):
        for x in range(H):
            low_out[c, x] = image_out[c, x]
            high_out[c, x] = image_out[c, 16 - H + x]
    rows = restrict_rows(vectors, image_out)
    rows = jnp.concatenate(
        [rows, jnp.sum(rz, axis=0, keepdims=True), jnp.sum(zz, axis=0, keepdims=True),
         jnp.zeros((6, 128), f32)], axis=0)
    payload[...] = jnp.broadcast_to(lanes_of(rows), (128, 128))


def final_kernel(pieces, scalars, residual_in, held, image, zprev, solution_in, direction_in,
                 solution_out, residual_out, direction_out):
    totals = jnp.sum(pieces[...], axis=0, keepdims=True)
    lane = iota((1, 128), 1)
    rho = jnp.sum(jnp.where(lane == 16, totals, 0.0), axis=1, keepdims=True)
    energy = jnp.sum(jnp.where(lane == 17, totals, 0.0), axis=1, keepdims=True)
    momentum = rho / scalars[0:1, 0:1]
    step = rho / (energy - momentum * rho / scalars[1:2, 0:1])

    def plane(x, carry):
        for c in range(3):
            d = zprev[c, x] + momentum * direction_in[c, x]
            direction_out[c, x] = d
            solution_out[c, x] = solution_in[c, x] + step * d
            full = image[c, x] + momentum * held[c, x + H, 0:16, 0:128]
            residual_out[c, x] = residual_in[c, x + H, 0:16, 0:128] - step * full
        return carry

    lax.fori_loop(0, 16, plane, 0)


def both_ways(to_next, to_prev, axis):
    count = lax.axis_size(axis)
    ahead = [(i, (i + 1) % count) for i in range(count)]
    back = [((i + 1) % count, i) for i in range(count)]
    return lax.ppermute(to_next, axis, ahead), lax.ppermute(to_prev, axis, back)


def halo(own, low_edge, high_edge, pieces=None, middle=None):
    comps = own.shape[0]
    low, high = both_ways(high_edge, low_edge, "gx")
    (ypack,) = call(pack_y_kernel, [(comps, 22, 8, 128)], [own, low, high], after=pieces)
    yminus, yplus = both_ways(ypack, ypack, "gy")
    done = middle(ypack) if middle else None
    (zpack,) = call(
        pack_z_kernel, [(comps, 24, 256)], [own, low, high, yplus, yminus],
        after=done[0] if middle else None,
    )
    zminus, zplus = both_ways(zpack, zpack, GZ)
    return (low, high, yplus, yminus, zplus, zminus), zpack, done


def share(rows):
    count = lax.axis_size(EVERY)
    return lax.all_to_all(rows.reshape(count, 1, 128), EVERY, 0, 0, tiled=True).reshape(count, 128)


def vector_halo(faces, ylow, yhigh, face):
    low, high = both_ways(*faces, "gx")
    shape = (3, 18, 16, 128)
    to_low, to_high = call(vectors_y_kernel, [shape, shape], [ylow, yhigh, low, high])
    yminus, yplus = both_ways(to_high, to_low, "gy")
    (packed,) = call(vectors_z_kernel, [(3, 5, 24, 128)], [face, low, high, yplus, yminus])
    zminus, zplus = both_ways(packed, packed, GZ)
    shapes = [(16, 3, 2, 16, 128), (3, 18, 32, 128), (3, 18, 24, 128)]
    return call(vectors_end_kernel, shapes, [low, high, yplus, yminus, zplus, zminus])


def body(forces, mass_shift, deflation, coarse_factor, coarse_slot):
    gx, gy, gz = lax.axis_index("gx"), lax.axis_index("gy"), lax.axis_index(GZ)
    nx, ny, nz = lax.axis_size("gx"), lax.axis_size("gy"), lax.axis_size(GZ)
    place = jnp.stack([gz, gy]).astype(jnp.int32)
    keep, send = call(
        factor_kernel, [(9, 64, 128), (7, 64, 128)], [place, coarse_factor],
        [pltpu.VMEM((256, 256), f32)],
    )
    received = lax.ppermute(send, GZ, [(i, 7 - i) for i in range(8)])
    faces = deflation[:, :, 15], deflation[:, :, 0]
    (folded,) = call(fold_kernel, [(9, 64, 128)], [place, keep, received], after=faces[0])
    factor = lax.all_gather(folded, ("gy", *GZ)).reshape(4, 8, 9, 64, 128)

    order = jnp.arange(coarse_slot.shape[0], dtype=jnp.int32)
    slots = (order[:, None] == coarse_slot[None, :]).astype(f32)
    moves = jnp.arange(-1, 2, dtype=jnp.int32)
    px = (gx + moves)[:, None, None]
    py = (gy + moves)[None, :, None]
    pz = (gz + moves)[None, None, :]
    valid = (px >= 0) & (px < nx) & (py >= 0) & (py < ny) & (pz >= 0) & (pz < nz)
    where = ((px * ny + py) * nz + pz).reshape(-1)
    valid = valid.reshape(-1)
    chosen = (where[:, None] == order[None, :]) & valid[:, None]
    near = jnp.sum(jnp.where(chosen[:, None, :], slots[None], 0.0), axis=2)
    near = jnp.concatenate([near, jnp.zeros((5, near.shape[1]), f32)], axis=0)
    inside = jnp.stack([gx > 0, gx < nx - 1, gy > 0, gy < ny - 1, gz > 0, gz < nz - 1, gz > 0, gz > 0])
    inside = inside.astype(jnp.int32)

    scale_own = relaxation / (mass_shift + (6.0 * off_diagonal + 2.0 * stiffer))
    fields = jnp.concatenate([forces, scale_own[None]], axis=0)
    block = (3, 16, 16, 128)
    lines = (3, 16, 16, 128)
    row, ylow, yhigh, face = call(
        vectors_kernel, [(128, 128), lines, lines, lines], [deflation, forces], micros=6
    )
    pieces = share(row)
    received, _, _ = halo(fields, fields[:, :H], fields[:, 16 - H :])
    ext = (22, 24, 256)
    patch = (3, 18, 24, 256)
    work = [pltpu.VMEM((3, *ext), f32)] * 3
    residual, scale = call(start_kernel, [(3, *ext), ext], [inside, fields, *received])
    (smooth,) = call(sweeps_kernel, [patch], [residual, scale], work[:2], limit=16, micros=5)
    around = vector_halo(faces, ylow, yhigh, face)
    weight_shapes = [(48, 128), (3, 32, 128), (3, 24, 128)]
    edge = (3, H, 16, 128)
    main_outs = [block, block, edge, edge, (128, 128)]

    g, wx, wy, wz = call(
        functools.partial(coarse_kernel, 0), [(8, 256)] + weight_shapes,
        [pieces, slots, near, factor], limit=20, micros=8,
    )
    (correction,) = call(
        functools.partial(correct_kernel, True), [patch], [wx, wy, wz, deflation, *around],
        limit=20, micros=6,
    )
    z, image, low_edge, high_edge, row = call(
        functools.partial(main_kernel, True), main_outs,
        [residual, scale, deflation, correction, smooth], work[:1], limit=24, micros=5,
    )
    held = jnp.zeros_like(residual)
    solution = jnp.zeros_like(forces)
    direction = jnp.zeros_like(forces)
    state = ()
    for iteration in range(1, ITERS):
        pieces = share(row)

        def coarse(token):
            return call(
                functools.partial(coarse_kernel, min(iteration, 2)),
                [(8, 256)] + weight_shapes + [(8, 256), (8, 128)],
                [pieces, slots, near, factor, g, *state],
                after=token, limit=20, micros=8,
            )

        received, zpack, done = halo(image, low_edge, high_edge, pieces, coarse)
        g, wx, wy, wz, hdir, scalars = done
        state = (hdir, scalars)
        correction, solution, direction = call(
            functools.partial(correct_kernel, False), [patch, block, block],
            [scalars, z, solution, direction, wx, wy, wz, deflation, *around],
            after=zpack, limit=20, micros=6,
        )
        residual, held, z, image, low_edge, high_edge, row = call(
            functools.partial(main_kernel, False), [(3, *ext), (3, *ext)] + main_outs,
            [scalars, residual, held, image, *received, scale, deflation, correction],
            work, limit=28, micros=10,
        )
    pieces = share(row)
    return tuple(
        call(
            final_kernel,
            [block] * 3,
            [pieces, scalars, residual, held, image, z, solution, direction],
        )
    )


def solution(mesh):
    finer = Mesh(
        mesh.devices.reshape(mesh.shape["gx"], mesh.shape["gy"], 4, 2), ("gx", "gy", "gz_0", "gz_1")
    )
    return jax.shard_map(
        body,
        mesh=finer,
        in_specs=(
            P(None, "gx", "gy", GZ),
            P("gx", "gy", GZ),
            P(None, None, "gx", "gy", GZ),
            P(GZ, None),
            P(),
        ),
        out_specs=(P(None, "gx", "gy", GZ), P(None, "gx", "gy", GZ), P(None, "gx", "gy", GZ)),
        check_vma=False,
    )
```

```python
import functools

import jax
import jax.numpy as jnp
from jax import lax
from jax.experimental import pallas as pl
from jax.experimental.pallas import tpu as pltpu
from jax.sharding import Mesh
from jax.sharding import PartitionSpec as P

ITERS = 4
GZ = ("gz_0", "gz_1")
EVERY = ("gx", "gy", "gz_0", "gz_1")

relaxation = 0.6
off_diagonal = 0.25
stiffer = 0.625
highest = lax.Precision.HIGHEST
f32 = jnp.float32
H = 3
MIB = 1 << 20


def call(kernel, outs, ins, scratch=(), after=None, limit=8, micros=1):
    vmem = pl.BlockSpec(memory_space=pltpu.VMEM)
    specs = []
    for a in ins:
        specs.append(pl.BlockSpec(memory_space=pltpu.SMEM) if a.dtype == jnp.int32 else vmem)
    if after is not None:
        specs = [pl.BlockSpec(memory_space=pl.ANY)] + specs
        ins = [after, *ins]
        inner = kernel

        def kernel(unused, *refs):
            inner(*refs)

    return pl.pallas_call(
        kernel,
        out_shape=[jax.ShapeDtypeStruct(s, f32) for s in outs],
        in_specs=specs,
        out_specs=[vmem] * len(outs),
        scratch_shapes=list(scratch),
        cost_estimate=pl.CostEstimate(flops=0, bytes_accessed=micros * 3_000_000, transcendentals=0),
        compiler_params=pltpu.CompilerParams(vmem_limit_bytes=limit * MIB),
    )(*ins)


def iota(shape, dim):
    return lax.broadcasted_iota(jnp.int32, shape, dim)


def mm(a, b):
    return jnp.dot(a, b, precision=highest, preferred_element_type=f32)


def factor_kernel(place, rows, keep, send, hold):
    j, part = place[0], place[1]
    n = rows.shape[0]
    share = keep.shape[1]
    tiles = n // 128
    start = pl.multiple_of(j * n, n)
    own = rows[:, pl.ds(start, n)]
    i0, i1 = iota((n, n), 0), iota((n, n), 1)
    eye = i0 == i1
    across = 1.0 / jnp.sum(jnp.where(eye, own, 0.0), axis=1, keepdims=True)
    down = 1.0 / jnp.sum(jnp.where(eye, own, 0.0), axis=0, keepdims=True)
    lower = jnp.where(((i0 // 4) == (i1 // 4)) & (i0 > i1), own, 0.0) * across
    square = mm(lower, lower)
    inverse = jnp.where(eye, 1.0, 0.0) - lower + square - mm(lower, square)
    inverse = inverse * down
    size = 4
    while size < n:
        same = (i0 // (2 * size)) == (i1 // (2 * size))
        block = jnp.where(same & ((i0 // size) > (i1 // size)), own, 0.0)
        inverse = inverse - mm(inverse, mm(block, inverse))
        size *= 2
    hold[...] = inverse
    mine = hold[pl.ds(pl.multiple_of(part * share, share), share), :]

    def put(t, value):
        for u in range(tiles):
            i = t * tiles + u
            piece = value[:, u * 128 : (u + 1) * 128]
            if i < keep.shape[0]:
                keep[i] = piece
            else:
                send[i - keep.shape[0]] = piece

    for t in range(rows.shape[1] // n):

        @pl.when(t < j)
        def _():
            put(t, mm(mine, rows[:, t * n : (t + 1) * n]))

        @pl.when(t == j)
        def _():
            put(t, mine)

        @pl.when(t > j)
        def _():
            put(t, jnp.zeros_like(mine))


def fold_kernel(place, keep, received, out):
    j = place[0]
    out[...] = keep[...]
    for i in range(7):

        @pl.when(i < 7 - 2 * j)
        def _():
            out[2 * j + 2 + i] = received[i]


def lanes_of(sums):
    count = sums.shape[0]
    column = jnp.sum(sums, axis=1, keepdims=True)
    placed = jnp.where(iota((count, 128), 0) == iota((count, 128), 1), column, 0.0)
    return jnp.sum(placed, axis=0, keepdims=True)


def restrict_rows(vectors, field):
    count = vectors.shape[0]

    def plane(x, acc):
        acc = list(acc)
        for c in range(3):
            values = field[c, x]
            for k in range(count):
                part = vectors[k, c, x] * values
                acc[k] = acc[k] + (part[:8] + part[8:])
        return tuple(acc)

    acc = lax.fori_loop(0, 16, plane, tuple(jnp.zeros((8, 128), f32) for _ in range(count)))
    rows = [jnp.sum(a, axis=0, keepdims=True) for a in acc]
    return jnp.concatenate(rows, axis=0)


def face_lanes(vector_of):
    lane = iota((16, 128), 1)
    face = jnp.zeros((16, 128), f32)
    for k in range(16):
        v = vector_of(k)
        first = pltpu.roll(v, k, 1) if k else v
        face = face + jnp.where(lane == k, first, jnp.where(lane == 16 + k, pltpu.roll(v, 17 + k, 1), 0.0))
    return face


def vectors_kernel(vectors, field, out, ylow, yhigh, face):
    out[...] = jnp.broadcast_to(lanes_of(restrict_rows(vectors, field)), (128, 128))

    def plane(x, carry):
        for c in range(3):
            for k in range(16):
                ylow[c, x, k : k + 1] = vectors[k, c, x, 0:1]
                yhigh[c, x, k : k + 1] = vectors[k, c, x, 15:16]
            face[c, x] = face_lanes(lambda k: vectors[k, c, x])
        return carry

    lax.fori_loop(0, 16, plane, 0)


def vectors_y_kernel(ylow, yhigh, low, high, to_low, to_high):
    for c in range(3):
        for x in range(16):
            to_low[c, x + 1] = ylow[c, x]
            to_high[c, x + 1] = yhigh[c, x]
        for source, i in ((low, 0), (high, 17)):
            for k in range(16):
                to_low[c, i, k : k + 1] = source[k, c, 0:1]
                to_high[c, i, k : k + 1] = source[k, c, 15:16]


def vectors_z_kernel(face, low, high, yplus, yminus, sums, out, sums_out):
    sums_out[...] = sums[...]
    row, lane = iota((16, 128), 0), iota((16, 128), 1)

    def lines(source, c, i):
        v = source[c, i]
        first = jnp.sum(jnp.where(lane == 0, v, 0.0), axis=1, keepdims=True)
        last = jnp.sum(jnp.where(lane == 127, v, 0.0), axis=1, keepdims=True)
        placed = jnp.where(lane == row, first, jnp.where(lane == row + 16, last, 0.0))
        return jnp.sum(placed, axis=0, keepdims=True)

    r8 = iota((8, 128), 0)

    for c in range(3):
        for group in range(5):
            packed = jnp.zeros((24, 128), f32)
            for i in range(4 * group, min(4 * group + 4, 18)):
                if i == 0:
                    own = face_lanes(lambda k: low[k, c])
                elif i == 17:
                    own = face_lanes(lambda k: high[k, c])
                else:
                    own = face[c, i - 1]
                line = jnp.where(
                    r8 == 0, lines(yplus, c, i), jnp.where(r8 == 7, lines(yminus, c, i), 0.0)
                )
                plane = jnp.concatenate([own, line], axis=0)
                if i % 4:
                    plane = pltpu.roll(plane, 32 * (i % 4), 1)
                packed = packed + plane
            out[c, group] = packed


def vectors_end_kernel(low, high, yplus, yminus, zplus, zminus, vx, vy, vz):
    lane = iota((24, 128), 1)
    vx[:, :, 0] = low[...]
    vx[:, :, 1] = high[...]
    vy[:, :, 0:16] = yplus[...]
    vy[:, :, 16:32] = yminus[...]
    for c in range(3):
        for i in range(18):
            plane = jnp.where(lane % 32 < 16, zplus[c, i // 4], zminus[c, i // 4])
            if i % 4:
                plane = pltpu.roll(plane, 128 - 32 * (i % 4), 1)
            vz[c, i] = plane


def pack_y(tile0, tile1):
    return jnp.where(iota(tile0.shape, tile0.ndim - 2) < 4, tile0, tile1)


def pack_y_kernel(own, low, high, out):
    for c in range(own.shape[0]):
        for x in range(H):
            out[c, x] = pack_y(low[c, x, :8], low[c, x, 8:])
            out[c, H + 16 + x] = pack_y(high[c, x, :8], high[c, x, 8:])
        for x in range(16):
            out[c, H + x] = pack_y(own[c, x, :8], own[c, x, 8:])


def plane_parts(own, low, high, c, i):
    if i < H:
        return low[c, i]
    if i < H + 16:
        return own[c, i - H]
    return high[c, i - H - 16]


def pack_z_kernel(own, low, high, yplus, yminus, out):
    lane = iota((24, 128), 1)
    edge = (lane < H) | (lane >= 128 - H)
    for c in range(own.shape[0]):
        packed = [jnp.zeros((24, 128), f32), jnp.zeros((24, 128), f32)]
        for i in range(22):
            ytile = pack_y(yplus[c, i], yminus[c, i])
            plane = jnp.concatenate([plane_parts(own, low, high, c, i), ytile], axis=0)
            plane = jnp.where(edge, plane, 0.0)
            shift = (8 * i) % 128
            if shift:
                plane = pltpu.roll(plane, shift, 1)
            packed[i // 16] = packed[i // 16] + plane
        out[c, :, :128] = packed[0]
        out[c, :, 128:] = packed[1]


def assemble(own, low, high, yplus, yminus, zplus, zminus, c, i):
    lane = iota((24, 128), 1)
    ytile = pack_y(yplus[c, i], yminus[c, i])
    centre = jnp.concatenate([plane_parts(own, low, high, c, i), ytile], axis=0)
    half = slice(0, 128) if i < 16 else slice(128, 256)
    side = jnp.where(lane % 8 < 4, zplus[c, :, half], zminus[c, :, half])
    shift = (8 * i) % 128
    if shift:
        side = pltpu.roll(side, 128 - shift, 1)
    side = jnp.where((lane < H) | (lane >= 128 - H), side, 0.0)
    return jnp.concatenate([centre, side], axis=1)


def start_kernel(inside, own, low, high, yplus, yminus, zplus, zminus, residual, scale):
    row, lane = iota((24, 256), 0), iota((24, 256), 1)
    keep = jnp.where(row < 16, 1, jnp.where(row < 20, inside[3], inside[2]))
    keep = keep * jnp.where(lane < 128, 1, jnp.where(lane < 192, inside[5], inside[4]))
    keep = jnp.where((row >= 16 + H) & (row < 24 - H), 0, keep)
    for i in range(22):
        for c in range(4):
            plane = assemble(own, low, high, yplus, yminus, zplus, zminus, c, i)
            if c < 3:
                residual[c, i] = plane
            else:
                here = keep
                if i < H:
                    here = keep * inside[0]
                elif i >= H + 16:
                    here = keep * inside[1]
                lanes_in = (lane < 128 + H) | (lane >= 256 - H)
                scale[i] = jnp.where((here > 0) & lanes_in, plane, 0.0)


def rows_to_column(row, eye):
    return jnp.sum(jnp.where(eye, row, 0.0), axis=1, keepdims=True)


def column_to_row(column, eye):
    return jnp.sum(jnp.where(eye, column, 0.0), axis=0, keepdims=True)


def coarse_kernel(stage, pieces, slots, near, factor, *refs):
    if stage == 0:
        g_out, wx, wy, wz = refs
    elif stage == 1:
        g_in, g_out, wx, wy, wz, hdir_out, scalars_out = refs
    else:
        g_in, hdir_in, scalars_in, g_out, wx, wy, wz, hdir_out, scalars_out = refs
    blocks = factor.shape[1]

    def tile(j, t):
        if t > 8:
            j, t = 7 - j, 2 * (7 - j) + t - 7
        return jnp.concatenate([factor[p, j, t] for p in range(factor.shape[0])], axis=0)

    q0, l256 = iota((128, 256), 0), iota((128, 256), 1)
    spot = (l256 // 16) == (q0 % 16)
    got = pieces[...]
    spread = jnp.where(iota((128, 256), 0) == iota((128, 256), 1) % 16, 1.0, 0.0)
    spread = jnp.where(iota((128, 256), 0) < 16, spread, 0.0)
    tiled = mm(got, spread)
    ordered = jnp.where(spot, mm(slots[...], tiled), 0.0)
    ordered = jnp.sum(ordered.reshape(8, 16, 256), axis=1)
    if stage == 0:
        g = ordered
    else:
        totals = jnp.sum(got, axis=0, keepdims=True)
        lane = iota((1, 128), 1)
        rho = jnp.sum(jnp.where(lane == 16, totals, 0.0), axis=1, keepdims=True)
        energy = jnp.sum(jnp.where(lane == 17, totals, 0.0), axis=1, keepdims=True)
        if stage == 1:
            momentum = jnp.zeros_like(rho)
            step = rho / energy
            hdir = ordered
        else:
            rho_prior = scalars_in[0:1, 0:1]
            step_prior = scalars_in[1:2, 0:1]
            momentum = rho / rho_prior
            step = rho / (energy - momentum * rho / step_prior)
            hdir = ordered + momentum * hdir_in[...]
        g = g_in[...] - step * hdir
        hdir_out[...] = hdir
        r8 = iota((8, 128), 0)
        scalars_out[...] = jnp.where(r8 == 0, rho, jnp.where(r8 == 1, step, momentum))
    g_out[...] = g
    eye = iota((128, 128), 0) == iota((128, 128), 1)
    yrow, ycol = [], []
    for j in range(blocks):
        acc = tile(j, 2 * j) * g[j : j + 1, :128] + tile(j, 2 * j + 1) * g[j : j + 1, 128:]
        for t in range(2 * j):
            acc = acc - tile(j, t) * yrow[t]
        column = jnp.sum(acc, axis=1, keepdims=True)
        for u in range(2):
            yrow.append(column_to_row(column[u * 128 : (u + 1) * 128], eye))
    vcol = [None] * blocks
    crow = [None] * blocks
    for i in range(blocks - 1, -1, -1):
        columns = []
        for u in range(2):
            t = 2 * i + u
            value = yrow[t]
            if i < blocks - 1:
                acc = tile(i + 1, t) * vcol[i + 1]
                for k in range(i + 2, blocks):
                    acc = acc + tile(k, t) * vcol[k]
                value = value - jnp.sum(acc, axis=0, keepdims=True)
            columns.append(rows_to_column(value, eye))
        vcol[i] = jnp.concatenate(columns, axis=0)
        crow[i] = jnp.concatenate(
            [jnp.sum(tile(i, 2 * i + u) * vcol[i], axis=0, keepdims=True) for u in range(2)],
            axis=1,
        )
    spread_c = jnp.concatenate(
        [jnp.broadcast_to(crow[b], (16, 256)) for b in range(blocks)], axis=0
    )
    spread_c = jnp.where(spot, spread_c, 0.0)
    fold = jnp.where(iota((256, 128), 0) % 16 == iota((256, 128), 1) % 16, 1.0, 0.0)
    by_slot = mm(spread_c, fold)
    weights = mm(near[...], by_slot)

    def w(x, y, z):
        n = x * 9 + y * 3 + z
        return weights[n : n + 1, :]

    r16, l16 = iota((16, 128), 0), iota((16, 128), 1)
    pick16 = r16 == l16
    row24, lane24 = iota((24, 128), 0), iota((24, 128), 1)
    for x in range(3):
        wx[16 * x : 16 * x + 16] = jnp.broadcast_to(
            jnp.sum(jnp.where(pick16, w(x, 1, 1), 0.0), axis=1, keepdims=True), (16, 128)
        )
        for side, y in ((0, 2), (1, 0)):
            wy[x, 16 * side : 16 * side + 16] = jnp.broadcast_to(
                jnp.sum(jnp.where(pick16, w(x, y, 1), 0.0), axis=1, keepdims=True), (16, 128)
            )

        def side_plane(z):
            return jnp.where(
                row24 < 16,
                w(x, 1, z),
                jnp.where(row24 == 16, w(x, 2, z), jnp.where(row24 == 23, w(x, 0, z), 0.0)),
            )

        wz[x] = jnp.where(
            lane24 < 16, side_plane(2), jnp.where(lane24 < 32, side_plane(0), 0.0)
        )


def stencil_terms(u, i):
    um = [u[c, i - 1] for c in range(3)]
    u0 = [u[c, i] for c in range(3)]
    up = [u[c, i + 1] for c in range(3)]

    def y(f):
        return pltpu.roll(f, 23, 0), pltpu.roll(f, 1, 0)

    def z(f):
        return pltpu.roll(f, 255, 1), pltpu.roll(f, 1, 1)

    dx = [up[c] - um[c] for c in range(3)]
    sx = [up[c] + um[c] for c in range(3)]
    yp, ym, zp, zm = [], [], [], []
    for c in range(3):
        a, b = y(u0[c])
        yp.append(a)
        ym.append(b)
        a, b = z(u0[c])
        zp.append(a)
        zm.append(b)
    sy = [yp[c] + ym[c] for c in range(3)]
    sz = [zp[c] + zm[c] for c in range(3)]
    a, b = y(dx[1])
    mixed0 = a - b
    a, b = z(dx[2])
    mixed0 = mixed0 + (a - b)
    a, b = y(dx[0] + (zp[2] - zm[2]))
    mixed1 = a - b
    a, b = z(dx[0] + (yp[1] - ym[1]))
    mixed2 = a - b
    mixed = [mixed0, mixed1, mixed2]
    own = [sx[0], sy[1], sz[2]]
    return u0, [
        off_diagonal * (sx[c] + sy[c] + sz[c]) + stiffer * own[c] + (0.25 * stiffer) * mixed[c]
        for c in range(3)
    ]


def correct_kernel(first, *refs):
    if first:
        wx, wy, wz, vectors, vx, vy, vz, zed = refs
    else:
        (scalars, zprev, solution_in, direction_in, wx, wy, wz, vectors, vx, vy, vz,
         zed, solution_out, direction_out) = refs
        step = scalars[1:2, 0:1]
        momentum = scalars[2:3, 0:1]

        def advance(x, carry):
            for c in range(3):
                d = zprev[c, x] + momentum * direction_in[c, x]
                direction_out[c, x] = d
                solution_out[c, x] = solution_in[c, x] + step * d
            return carry

        lax.fori_loop(0, 16, advance, 0)

    def correct(source, x, i, region):
        accs = []
        for c in range(3):
            acc = wx[pl.ds(16 * region, 1), :] * source[0, c, x]
            for k in range(1, 16):
                acc = acc + wx[pl.ds(16 * region + k, 1), :] * source[k, c, x]
            accs.append(acc)
        lane = iota((24, 128), 1)
        row = iota((8, 128), 0)
        for c in range(3):
            prod = vy[c, i] * wy[region]
            plus = jnp.sum(prod[:16], axis=0, keepdims=True)
            minus = jnp.sum(prod[16:], axis=0, keepdims=True)
            ytile = jnp.where(row == 0, plus, jnp.where(row == 7, minus, 0.0))
            prod = vz[c, i] * wz[region]
            plus = jnp.sum(jnp.where(lane < 16, prod, 0.0), axis=1, keepdims=True)
            minus = jnp.sum(jnp.where(lane >= 16, prod, 0.0), axis=1, keepdims=True)
            side = jnp.where(lane == 0, plus, jnp.where(lane == 127, minus, 0.0))
            zed[c, i, 0:16, 0:128] = accs[c]
            zed[c, i, 16:24, 0:128] = ytile
            zed[c, i, :, 128:256] = side

    correct(vx, 0, 0, 0)

    def correct_own(x, carry):
        correct(vectors, x, x + 1, 1)
        return carry

    lax.fori_loop(0, 16, correct_own, 0)
    correct(vx, 1, 17, 2)


def sweeps(residual, scale, s1, s2, emit):
    def sweep1(i, carry):
        w = scale[i]
        for c in range(3):
            s1[c, i] = w * residual[c, i]
        return carry

    lax.fori_loop(0, 22, sweep1, 0, unroll=2)

    def sweep2(i, carry):
        w = scale[i]
        u0, terms = stencil_terms(s1, i)
        for c in range(3):
            s2[c, i] = (1.0 - relaxation) * u0[c] + w * (residual[c, i] + terms[c])
        return carry

    lax.fori_loop(1, 21, sweep2, 0, unroll=2)

    def sweep3(i, carry):
        w = scale[i]
        u0, terms = stencil_terms(s2, i)
        for c in range(3):
            emit(c, i, (1.0 - relaxation) * u0[c] + w * (residual[c, i] + terms[c]))
        return carry

    lax.fori_loop(2, 20, sweep3, 0, unroll=2)


def sweeps_kernel(residual, scale, smooth, s1, s2):
    def emit(c, i, value):
        smooth[c, i - 2] = value

    sweeps(residual, scale, s1, s2, emit)


def main_kernel(first, *refs):
    if first:
        (residual_in, scale, vectors, correction, smooth, z_out, image_out, low_out, high_out, payload,
         zed) = refs
        residual = residual_in
    else:
        (scalars, residual_in, held_in, own, low, high, yplus, yminus, zplus, zminus, scale,
         vectors, correction, residual, held,
         z_out, image_out, low_out, high_out, payload, s1, s2, zed) = refs
        step = scalars[1:2, 0:1]
        momentum = scalars[2:3, 0:1]
        for i in range(22):
            for c in range(3):
                image = assemble(own, low, high, yplus, yminus, zplus, zminus, c, i)
                image = image + momentum * held_in[c, i]
                held[c, i] = image
                residual[c, i] = residual_in[c, i] - step * image

    if first:
        for i in range(2, 20):
            for c in range(3):
                zed[c, i] = smooth[c, i - 2] + correction[c, i - 2]
    else:

        def emit(c, i, value):
            zed[c, i] = correction[c, i - 2] + value

        sweeps(residual, scale, s1, s2, emit)

    def apply(x, carry):
        rz, zz = carry
        i = x + 3
        diagonal = relaxation / scale[i, 0:16, 0:128]
        u0, terms = stencil_terms(zed, i)
        for c in range(3):
            zc = u0[c][0:16, 0:128]
            image = diagonal * zc - terms[c][0:16, 0:128]
            z_out[c, x] = zc
            image_out[c, x] = image
            rz = rz + residual[c, i, 0:16, 0:128] * zc
            zz = zz + zc * image
        return rz, zz

    zero = jnp.zeros((16, 128), f32)
    rz, zz = lax.fori_loop(0, 16, apply, (zero, zero), unroll=2)
    for c in range(3):
        for x in range(H):
            low_out[c, x] = image_out[c, x]
            high_out[c, x] = image_out[c, 16 - H + x]
    rows = restrict_rows(vectors, image_out)
    rows = jnp.concatenate(
        [rows, jnp.sum(rz, axis=0, keepdims=True), jnp.sum(zz, axis=0, keepdims=True),
         jnp.zeros((6, 128), f32)], axis=0)
    payload[...] = jnp.broadcast_to(lanes_of(rows), (128, 128))


def final_kernel(pieces, scalars, residual_in, held, image, zprev, solution_in, direction_in,
                 solution_out, residual_out, direction_out):
    totals = jnp.sum(pieces[...], axis=0, keepdims=True)
    lane = iota((1, 128), 1)
    rho = jnp.sum(jnp.where(lane == 16, totals, 0.0), axis=1, keepdims=True)
    energy = jnp.sum(jnp.where(lane == 17, totals, 0.0), axis=1, keepdims=True)
    momentum = rho / scalars[0:1, 0:1]
    step = rho / (energy - momentum * rho / scalars[1:2, 0:1])

    def plane(x, carry):
        for c in range(3):
            d = zprev[c, x] + momentum * direction_in[c, x]
            direction_out[c, x] = d
            solution_out[c, x] = solution_in[c, x] + step * d
            full = image[c, x] + momentum * held[c, x + H, 0:16, 0:128]
            residual_out[c, x] = residual_in[c, x + H, 0:16, 0:128] - step * full
        return carry

    lax.fori_loop(0, 16, plane, 0)


def both_ways(to_next, to_prev, axis):
    count = lax.axis_size(axis)
    ahead = [(i, (i + 1) % count) for i in range(count)]
    back = [((i + 1) % count, i) for i in range(count)]
    return lax.ppermute(to_next, axis, ahead), lax.ppermute(to_prev, axis, back)


def halo(own, low_edge, high_edge, pieces=None, middle=None):
    comps = own.shape[0]
    low, high = both_ways(high_edge, low_edge, "gx")
    (ypack,) = call(pack_y_kernel, [(comps, 22, 8, 128)], [own, low, high], after=pieces)
    yminus, yplus = both_ways(ypack, ypack, "gy")
    done = middle(ypack) if middle else None
    (zpack,) = call(
        pack_z_kernel, [(comps, 24, 256)], [own, low, high, yplus, yminus],
        after=done[0] if middle else None,
    )
    zminus, zplus = both_ways(zpack, zpack, GZ)
    return (low, high, yplus, yminus, zplus, zminus), zpack, done


def share(rows):
    count = lax.axis_size(EVERY)
    return lax.all_to_all(rows.reshape(count, 1, 128), EVERY, 0, 0, tiled=True).reshape(count, 128)


def vector_halo(faces, ylow, yhigh, face, row):
    low, high = both_ways(*faces, "gx")
    shape = (3, 18, 16, 128)
    to_low, to_high = call(vectors_y_kernel, [shape, shape], [ylow, yhigh, low, high])
    yminus, yplus = both_ways(to_high, to_low, "gy")
    packed, row = call(
        vectors_z_kernel, [(3, 5, 24, 128), (128, 128)], [face, low, high, yplus, yminus, row]
    )
    zminus, zplus = both_ways(packed, packed, GZ)
    shapes = [(16, 3, 2, 16, 128), (3, 18, 32, 128), (3, 18, 24, 128)]
    return call(vectors_end_kernel, shapes, [low, high, yplus, yminus, zplus, zminus]), row


def body(forces, mass_shift, deflation, coarse_factor, coarse_slot):
    gx, gy, gz = lax.axis_index("gx"), lax.axis_index("gy"), lax.axis_index(GZ)
    nx, ny, nz = lax.axis_size("gx"), lax.axis_size("gy"), lax.axis_size(GZ)
    faces = deflation[:, :, 15], deflation[:, :, 0]
    place = jnp.stack([gz, gx]).astype(jnp.int32)
    keep, send = call(
        factor_kernel, [(9, 64, 128), (7, 64, 128)], [place, coarse_factor],
        [pltpu.VMEM((256, 256), f32)], after=faces[0],
    )
    received = lax.ppermute(send, GZ, [(i, 7 - i) for i in range(8)])
    (folded,) = call(fold_kernel, [(9, 64, 128)], [place, keep, received])
    factor = lax.all_gather(folded, ("gx", *GZ)).reshape(4, 8, 9, 64, 128)

    order = jnp.arange(coarse_slot.shape[0], dtype=jnp.int32)
    slots = (order[:, None] == coarse_slot[None, :]).astype(f32)
    moves = jnp.arange(-1, 2, dtype=jnp.int32)
    px = (gx + moves)[:, None, None]
    py = (gy + moves)[None, :, None]
    pz = (gz + moves)[None, None, :]
    valid = (px >= 0) & (px < nx) & (py >= 0) & (py < ny) & (pz >= 0) & (pz < nz)
    where = ((px * ny + py) * nz + pz).reshape(-1)
    valid = valid.reshape(-1)
    chosen = (where[:, None] == order[None, :]) & valid[:, None]
    near = jnp.sum(jnp.where(chosen[:, None, :], slots[None], 0.0), axis=2)
    near = jnp.concatenate([near, jnp.zeros((5, near.shape[1]), f32)], axis=0)
    inside = jnp.stack([gx > 0, gx < nx - 1, gy > 0, gy < ny - 1, gz > 0, gz < nz - 1, gz > 0, gz > 0])
    inside = inside.astype(jnp.int32)

    scale_own = relaxation / (mass_shift + (6.0 * off_diagonal + 2.0 * stiffer))
    fields = jnp.concatenate([forces, scale_own[None]], axis=0)
    block = (3, 16, 16, 128)
    lines = (3, 16, 16, 128)
    row, ylow, yhigh, face = call(
        vectors_kernel, [(128, 128), lines, lines, lines], [deflation, forces], limit=10, micros=6
    )
    received, _, _ = halo(fields, fields[:, :H], fields[:, 16 - H :])
    ext = (22, 24, 256)
    patch = (3, 18, 24, 256)
    work = [pltpu.VMEM((3, *ext), f32)] * 3
    residual, scale = call(start_kernel, [(3, *ext), ext], [inside, fields, *received])
    (smooth,) = call(sweeps_kernel, [patch], [residual, scale], work[:2], limit=8, micros=4)
    around, row = vector_halo(faces, ylow, yhigh, face, row)
    pieces = share(row)
    weight_shapes = [(48, 128), (3, 32, 128), (3, 24, 128)]
    edge = (3, H, 16, 128)
    main_outs = [block, block, edge, edge, (128, 128)]

    g, wx, wy, wz = call(
        functools.partial(coarse_kernel, 0), [(8, 256)] + weight_shapes,
        [pieces, slots, near, factor], limit=12, micros=5,
    )
    (correction,) = call(
        functools.partial(correct_kernel, True), [patch], [wx, wy, wz, deflation, *around],
        limit=13, micros=3,
    )
    z, image, low_edge, high_edge, row = call(
        functools.partial(main_kernel, True), main_outs,
        [residual, scale, deflation, correction, smooth], work[:1], limit=16, micros=3,
    )
    held = jnp.zeros_like(residual)
    solution = jnp.zeros_like(forces)
    direction = jnp.zeros_like(forces)
    state = ()
    for iteration in range(1, ITERS):
        pieces = share(row)

        def coarse(token):
            return call(
                functools.partial(coarse_kernel, min(iteration, 2)),
                [(8, 256)] + weight_shapes + [(8, 256), (8, 128)],
                [pieces, slots, near, factor, g, *state],
                after=token, limit=12, micros=5,
            )

        received, zpack, done = halo(image, low_edge, high_edge, pieces, coarse)
        g, wx, wy, wz, hdir, scalars = done
        state = (hdir, scalars)
        correction, solution, direction = call(
            functools.partial(correct_kernel, False), [patch, block, block],
            [scalars, z, solution, direction, wx, wy, wz, deflation, *around],
            after=zpack, limit=14, micros=3,
        )
        residual, held, z, image, low_edge, high_edge, row = call(
            functools.partial(main_kernel, False), [(3, *ext), (3, *ext)] + main_outs,
            [scalars, residual, held, image, *received, scale, deflation, correction],
            work, limit=23, micros=7,
        )
    pieces = share(row)
    return tuple(
        call(
            final_kernel,
            [block] * 3,
            [pieces, scalars, residual, held, image, z, solution, direction],
        )
    )


def solution(mesh):
    finer = Mesh(
        mesh.devices.reshape(mesh.shape["gx"], mesh.shape["gy"], 4, 2), ("gx", "gy", "gz_0", "gz_1")
    )
    return jax.shard_map(
        body,
        mesh=finer,
        in_specs=(
            P(None, "gx", "gy", GZ),
            P("gx", "gy", GZ),
            P(None, None, "gx", "gy", GZ),
            P(GZ, None),
            P(),
        ),
        out_specs=(P(None, "gx", "gy", GZ), P(None, "gx", "gy", GZ), P(None, "gx", "gy", GZ)),
        check_vma=False,
    )
```

```python
import functools

import jax
import jax.numpy as jnp
from jax import lax
from jax.experimental import pallas as pl
from jax.experimental.pallas import tpu as pltpu
from jax.sharding import Mesh
from jax.sharding import PartitionSpec as P

ITERS = 4
GZ = ("gz_0", "gz_1")
EVERY = ("gx", "gy", "gz_0", "gz_1")

relaxation = 0.6
off_diagonal = 0.25
stiffer = 0.625
highest = lax.Precision.HIGHEST
f32 = jnp.float32
H = 3
MIB = 1 << 20


def call(kernel, outs, ins, scratch=(), after=None, limit=8, micros=1):
    vmem = pl.BlockSpec(memory_space=pltpu.VMEM)
    specs = []
    for a in ins:
        specs.append(pl.BlockSpec(memory_space=pltpu.SMEM) if a.dtype == jnp.int32 else vmem)
    if after is not None:
        specs = [pl.BlockSpec(memory_space=pl.ANY)] + specs
        ins = [after, *ins]
        inner = kernel

        def kernel(unused, *refs):
            inner(*refs)

    return pl.pallas_call(
        kernel,
        out_shape=[jax.ShapeDtypeStruct(s, f32) for s in outs],
        in_specs=specs,
        out_specs=[vmem] * len(outs),
        scratch_shapes=list(scratch),
        cost_estimate=pl.CostEstimate(flops=0, bytes_accessed=micros * 3_000_000, transcendentals=0),
        compiler_params=pltpu.CompilerParams(vmem_limit_bytes=limit * MIB),
    )(*ins)


def iota(shape, dim):
    return lax.broadcasted_iota(jnp.int32, shape, dim)


def mm(a, b):
    return jnp.dot(a, b, precision=highest, preferred_element_type=f32)


def inverse_of(own):
    n = own.shape[0]
    i0, i1 = iota((n, n), 0), iota((n, n), 1)
    eye = i0 == i1
    across = 1.0 / jnp.sum(jnp.where(eye, own, 0.0), axis=1, keepdims=True)
    down = 1.0 / jnp.sum(jnp.where(eye, own, 0.0), axis=0, keepdims=True)
    lower = jnp.where(((i0 // 4) == (i1 // 4)) & (i0 > i1), own, 0.0) * across
    square = mm(lower, lower)
    inverse = jnp.where(eye, 1.0, 0.0) - lower + square - mm(lower, square)
    inverse = inverse * down
    size = 4
    while size < n:
        same = (i0 // (2 * size)) == (i1 // (2 * size))
        block = jnp.where(same & ((i0 // size) > (i1 // size)), own, 0.0)
        inverse = inverse - mm(inverse, mm(block, inverse))
        size *= 2
    return inverse


def factor_kernel(place, rows, keep, send, hold):
    j, part = place[0], place[1]
    n = rows.shape[0]
    share = keep.shape[1]
    tiles = n // 128
    start = pl.multiple_of(j * n, n)
    own = rows[:, pl.ds(start, n)]
    half = n // 2
    upper = inverse_of(own[:half, :half])
    lower = inverse_of(own[half:, half:])
    inverse = jnp.concatenate(
        [
            jnp.concatenate([upper, jnp.zeros_like(upper)], axis=1),
            jnp.concatenate([-mm(lower, mm(own[half:, :half], upper)), lower], axis=1),
        ],
        axis=0,
    )
    hold[...] = inverse
    mine = hold[pl.ds(pl.multiple_of(part * share, share), share), :]

    def put(t, value):
        for u in range(tiles):
            i = t * tiles + u
            piece = value[:, u * 128 : (u + 1) * 128]
            if i < keep.shape[0]:
                keep[i] = piece
            else:
                send[i - keep.shape[0]] = piece

    for t in range(rows.shape[1] // n):

        @pl.when(t < j)
        def _():
            put(t, mm(mine, rows[:, t * n : (t + 1) * n]))

        @pl.when(t == j)
        def _():
            put(t, mine)

        @pl.when(t > j)
        def _():
            put(t, jnp.zeros_like(mine))


def fold_kernel(place, keep, received, out):
    j = place[0]
    out[...] = keep[...]
    for i in range(7):

        @pl.when(i < 7 - 2 * j)
        def _():
            out[2 * j + 2 + i] = received[i]


def lanes_of(sums):
    count = sums.shape[0]
    column = jnp.sum(sums, axis=1, keepdims=True)
    placed = jnp.where(iota((count, 128), 0) == iota((count, 128), 1), column, 0.0)
    return jnp.sum(placed, axis=0, keepdims=True)


def restrict_rows(vectors, field):
    count = vectors.shape[0]

    def plane(x, acc):
        acc = list(acc)
        for c in range(3):
            values = field[c, x]
            for k in range(count):
                part = vectors[k, c, x] * values
                acc[k] = acc[k] + (part[:8] + part[8:])
        return tuple(acc)

    acc = lax.fori_loop(0, 16, plane, tuple(jnp.zeros((8, 128), f32) for _ in range(count)))
    rows = [jnp.sum(a, axis=0, keepdims=True) for a in acc]
    return jnp.concatenate(rows, axis=0)


def face_lanes(vector_of):
    lane = iota((16, 128), 1)
    face = jnp.zeros((16, 128), f32)
    for k in range(16):
        v = vector_of(k)
        first = pltpu.roll(v, k, 1) if k else v
        face = face + jnp.where(lane == k, first, jnp.where(lane == 16 + k, pltpu.roll(v, 17 + k, 1), 0.0))
    return face


def vectors_kernel(vectors, field, out, face):
    out[...] = jnp.broadcast_to(lanes_of(restrict_rows(vectors, field)), (128, 128))

    def plane(x, carry):
        for c in range(3):
            face[c, x] = face_lanes(lambda k: vectors[k, c, x])
        return carry

    lax.fori_loop(0, 16, plane, 0)


def vectors_y_kernel(vectors, low, high, to_low, to_high):
    def plane(x, carry):
        for c in range(3):
            for k in range(16):
                to_low[c, x + 1, k : k + 1] = vectors[k, c, x, 0:1]
                to_high[c, x + 1, k : k + 1] = vectors[k, c, x, 15:16]
        return carry

    lax.fori_loop(0, 16, plane, 0)
    for c in range(3):
        for source, i in ((low, 0), (high, 17)):
            for k in range(16):
                to_low[c, i, k : k + 1] = source[k, c, 0:1]
                to_high[c, i, k : k + 1] = source[k, c, 15:16]


def vectors_z_kernel(face, low, high, yplus, yminus, sums, out, sums_out):
    sums_out[...] = sums[...]
    row, lane = iota((16, 128), 0), iota((16, 128), 1)

    def lines(source, c, i):
        v = source[c, i]
        first = jnp.sum(jnp.where(lane == 0, v, 0.0), axis=1, keepdims=True)
        last = jnp.sum(jnp.where(lane == 127, v, 0.0), axis=1, keepdims=True)
        placed = jnp.where(lane == row, first, jnp.where(lane == row + 16, last, 0.0))
        return jnp.sum(placed, axis=0, keepdims=True)

    r8 = iota((8, 128), 0)

    for c in range(3):
        for group in range(5):
            packed = jnp.zeros((24, 128), f32)
            for i in range(4 * group, min(4 * group + 4, 18)):
                if i == 0:
                    own = face_lanes(lambda k: low[k, c])
                elif i == 17:
                    own = face_lanes(lambda k: high[k, c])
                else:
                    own = face[c, i - 1]
                line = jnp.where(
                    r8 == 0, lines(yplus, c, i), jnp.where(r8 == 7, lines(yminus, c, i), 0.0)
                )
                plane = jnp.concatenate([own, line], axis=0)
                if i % 4:
                    plane = pltpu.roll(plane, 32 * (i % 4), 1)
                packed = packed + plane
            out[c, group] = packed


def vectors_end_kernel(zplus, zminus, vz):
    lane = iota((24, 128), 1)
    for c in range(3):
        for i in range(18):
            plane = jnp.where(lane % 32 < 16, zplus[c, i // 4], zminus[c, i // 4])
            if i % 4:
                plane = pltpu.roll(plane, 128 - 32 * (i % 4), 1)
            vz[c, i] = plane


def pack_y(tile0, tile1):
    return jnp.where(iota(tile0.shape, tile0.ndim - 2) < 4, tile0, tile1)


def pack_y_kernel(own, low, high, out):
    for c in range(own.shape[0]):
        for x in range(H):
            out[c, x] = pack_y(low[c, x, :8], low[c, x, 8:])
            out[c, H + 16 + x] = pack_y(high[c, x, :8], high[c, x, 8:])
        for x in range(16):
            out[c, H + x] = pack_y(own[c, x, :8], own[c, x, 8:])


def plane_parts(own, low, high, c, i):
    if i < H:
        return low[c, i]
    if i < H + 16:
        return own[c, i - H]
    return high[c, i - H - 16]


def pack_z_kernel(own, low, high, yplus, yminus, out):
    lane = iota((24, 128), 1)
    edge = (lane < H) | (lane >= 128 - H)
    for c in range(own.shape[0]):
        packed = [jnp.zeros((24, 128), f32), jnp.zeros((24, 128), f32)]
        for i in range(22):
            ytile = pack_y(yplus[c, i], yminus[c, i])
            plane = jnp.concatenate([plane_parts(own, low, high, c, i), ytile], axis=0)
            plane = jnp.where(edge, plane, 0.0)
            shift = (8 * i) % 128
            if shift:
                plane = pltpu.roll(plane, shift, 1)
            packed[i // 16] = packed[i // 16] + plane
        out[c, :, :128] = packed[0]
        out[c, :, 128:] = packed[1]


def assemble(own, low, high, yplus, yminus, zplus, zminus, c, i):
    lane = iota((24, 128), 1)
    ytile = pack_y(yplus[c, i], yminus[c, i])
    centre = jnp.concatenate([plane_parts(own, low, high, c, i), ytile], axis=0)
    half = slice(0, 128) if i < 16 else slice(128, 256)
    side = jnp.where(lane % 8 < 4, zplus[c, :, half], zminus[c, :, half])
    shift = (8 * i) % 128
    if shift:
        side = pltpu.roll(side, 128 - shift, 1)
    side = jnp.where((lane < H) | (lane >= 128 - H), side, 0.0)
    return jnp.concatenate([centre, side], axis=1)


def start_kernel(inside, own, low, high, yplus, yminus, zplus, zminus, residual, scale):
    row, lane = iota((24, 256), 0), iota((24, 256), 1)
    keep = jnp.where(row < 16, 1, jnp.where(row < 20, inside[3], inside[2]))
    keep = keep * jnp.where(lane < 128, 1, jnp.where(lane < 192, inside[5], inside[4]))
    keep = jnp.where((row >= 16 + H) & (row < 24 - H), 0, keep)
    for i in range(22):
        for c in range(4):
            plane = assemble(own, low, high, yplus, yminus, zplus, zminus, c, i)
            if c < 3:
                residual[c, i] = plane
            else:
                here = keep
                if i < H:
                    here = keep * inside[0]
                elif i >= H + 16:
                    here = keep * inside[1]
                lanes_in = (lane < 128 + H) | (lane >= 256 - H)
                scale[i] = jnp.where((here > 0) & lanes_in, plane, 0.0)


def rows_to_column(row, eye):
    return jnp.sum(jnp.where(eye, row, 0.0), axis=1, keepdims=True)


def column_to_row(column, eye):
    return jnp.sum(jnp.where(eye, column, 0.0), axis=0, keepdims=True)


def repeat_lanes(x):
    for shift in (16, 32, 64):
        x = x + pltpu.roll(x, shift, 1)
    return x


def coarse_kernel(stage, pieces, slots, near, factor, *refs):
    if stage == 0:
        g_out, wx, wy, wz = refs
    elif stage == 1:
        g_in, g_out, wx, wy, wz, hdir_out, scalars_out = refs
    else:
        g_in, hdir_in, scalars_in, g_out, wx, wy, wz, hdir_out, scalars_out = refs
    blocks = factor.shape[1]

    def tile(j, t):
        if t > 8:
            j, t = 7 - j, 2 * (7 - j) + t - 7
        return jnp.concatenate([factor[p, j, t] for p in range(factor.shape[0])], axis=0)

    q0, l256 = iota((128, 256), 0), iota((128, 256), 1)
    spot = (l256 // 16) == (q0 % 16)
    got = pieces[...]
    ordering = jnp.where(iota((128, 128), 0).astype(f32) == slots[...], 1.0, 0.0)
    tiled = mm(ordering, repeat_lanes(jnp.where(iota((128, 128), 1) < 16, got, 0.0)))
    ordered = jnp.where(spot, jnp.concatenate([tiled, tiled], axis=1), 0.0)
    ordered = jnp.sum(ordered.reshape(8, 16, 256), axis=1)
    if stage == 0:
        g = ordered
    else:
        totals = jnp.sum(got, axis=0, keepdims=True)
        lane = iota((1, 128), 1)
        rho = jnp.sum(jnp.where(lane == 16, totals, 0.0), axis=1, keepdims=True)
        energy = jnp.sum(jnp.where(lane == 17, totals, 0.0), axis=1, keepdims=True)
        if stage == 1:
            momentum = jnp.zeros_like(rho)
            step = rho / energy
            hdir = ordered
        else:
            rho_prior = scalars_in[0:1, 0:1]
            step_prior = scalars_in[1:2, 0:1]
            momentum = rho / rho_prior
            step = rho / (energy - momentum * rho / step_prior)
            hdir = ordered + momentum * hdir_in[...]
        g = g_in[...] - step * hdir
        hdir_out[...] = hdir
        r8 = iota((8, 128), 0)
        scalars_out[...] = jnp.where(r8 == 0, rho, jnp.where(r8 == 1, step, momentum))
    g_out[...] = g
    eye = iota((128, 128), 0) == iota((128, 128), 1)
    yrow, ycol = [], []
    for j in range(blocks):
        acc = tile(j, 2 * j) * g[j : j + 1, :128] + tile(j, 2 * j + 1) * g[j : j + 1, 128:]
        for t in range(2 * j):
            acc = acc - tile(j, t) * yrow[t]
        column = jnp.sum(acc, axis=1, keepdims=True)
        for u in range(2):
            yrow.append(column_to_row(column[u * 128 : (u + 1) * 128], eye))
    vcol = [None] * blocks
    crow = [None] * blocks
    for i in range(blocks - 1, -1, -1):
        columns = []
        for u in range(2):
            t = 2 * i + u
            value = yrow[t]
            if i < blocks - 1:
                acc = tile(i + 1, t) * vcol[i + 1]
                for k in range(i + 2, blocks):
                    acc = acc + tile(k, t) * vcol[k]
                value = value - jnp.sum(acc, axis=0, keepdims=True)
            columns.append(rows_to_column(value, eye))
        vcol[i] = jnp.concatenate(columns, axis=0)
        crow[i] = jnp.concatenate(
            [jnp.sum(tile(i, 2 * i + u) * vcol[i], axis=0, keepdims=True) for u in range(2)],
            axis=1,
        )
    spread_c = jnp.concatenate(
        [jnp.broadcast_to(crow[b], (16, 256)) for b in range(blocks)], axis=0
    )
    spread_c = jnp.where(spot, spread_c, 0.0)
    by_slot = repeat_lanes(spread_c[:, :128] + spread_c[:, 128:])
    weights = mm(near[...], by_slot)

    def w(x, y, z):
        n = x * 9 + y * 3 + z
        return weights[n : n + 1, :]

    r16, l16 = iota((16, 128), 0), iota((16, 128), 1)
    pick16 = r16 == l16
    row24, lane24 = iota((24, 128), 0), iota((24, 128), 1)
    for x in range(3):
        wx[16 * x : 16 * x + 16] = jnp.broadcast_to(
            jnp.sum(jnp.where(pick16, w(x, 1, 1), 0.0), axis=1, keepdims=True), (16, 128)
        )
        for side, y in ((0, 2), (1, 0)):
            wy[x, 16 * side : 16 * side + 16] = jnp.broadcast_to(
                jnp.sum(jnp.where(pick16, w(x, y, 1), 0.0), axis=1, keepdims=True), (16, 128)
            )

        def side_plane(z):
            return jnp.where(
                row24 < 16,
                w(x, 1, z),
                jnp.where(row24 == 16, w(x, 2, z), jnp.where(row24 == 23, w(x, 0, z), 0.0)),
            )

        wz[x] = jnp.where(
            lane24 < 16, side_plane(2), jnp.where(lane24 < 32, side_plane(0), 0.0)
        )


def stencil_terms(u, i):
    um = [u[c, i - 1] for c in range(3)]
    u0 = [u[c, i] for c in range(3)]
    up = [u[c, i + 1] for c in range(3)]

    def y(f):
        return pltpu.roll(f, 23, 0), pltpu.roll(f, 1, 0)

    def z(f):
        return pltpu.roll(f, 255, 1), pltpu.roll(f, 1, 1)

    dx = [up[c] - um[c] for c in range(3)]
    sx = [up[c] + um[c] for c in range(3)]
    yp, ym, zp, zm = [], [], [], []
    for c in range(3):
        a, b = y(u0[c])
        yp.append(a)
        ym.append(b)
        a, b = z(u0[c])
        zp.append(a)
        zm.append(b)
    sy = [yp[c] + ym[c] for c in range(3)]
    sz = [zp[c] + zm[c] for c in range(3)]
    a, b = y(dx[1])
    mixed0 = a - b
    a, b = z(dx[2])
    mixed0 = mixed0 + (a - b)
    a, b = y(dx[0] + (zp[2] - zm[2]))
    mixed1 = a - b
    a, b = z(dx[0] + (yp[1] - ym[1]))
    mixed2 = a - b
    mixed = [mixed0, mixed1, mixed2]
    own = [sx[0], sy[1], sz[2]]
    return u0, [
        off_diagonal * (sx[c] + sy[c] + sz[c]) + stiffer * own[c] + (0.25 * stiffer) * mixed[c]
        for c in range(3)
    ]


def correct_kernel(first, *refs):
    if first:
        wx, wy, wz, vectors, low, high, yplus, yminus, vz, zed = refs
    else:
        (scalars, zprev, solution_in, direction_in, wx, wy, wz, vectors,
         low, high, yplus, yminus, vz,
         zed, solution_out, direction_out) = refs
        step = scalars[1:2, 0:1]
        momentum = scalars[2:3, 0:1]

        def advance(x, carry):
            for c in range(3):
                d = zprev[c, x] + momentum * direction_in[c, x]
                direction_out[c, x] = d
                solution_out[c, x] = solution_in[c, x] + step * d
            return carry

        lax.fori_loop(0, 16, advance, 0)

    lane = iota((24, 128), 1)
    row = iota((8, 128), 0)

    def correct(source, i, region):
        accs = []
        for c in range(3):
            acc = wx[pl.ds(16 * region, 1), :] * source(0, c)
            for k in range(1, 16):
                acc = acc + wx[pl.ds(16 * region + k, 1), :] * source(k, c)
            accs.append(acc)
        for c in range(3):
            plus = jnp.sum(yplus[c, i] * wy[region, :16], axis=0, keepdims=True)
            minus = jnp.sum(yminus[c, i] * wy[region, 16:], axis=0, keepdims=True)
            ytile = jnp.where(row == 0, plus, jnp.where(row == 7, minus, 0.0))
            prod = vz[c, i] * wz[region]
            plus = jnp.sum(jnp.where(lane < 16, prod, 0.0), axis=1, keepdims=True)
            minus = jnp.sum(jnp.where(lane >= 16, prod, 0.0), axis=1, keepdims=True)
            side = jnp.where(lane == 0, plus, jnp.where(lane == 127, minus, 0.0))
            zed[c, i, 0:16, 0:128] = accs[c]
            zed[c, i, 16:24, 0:128] = ytile
            zed[c, i, :, 128:256] = side

    correct(lambda k, c: low[k, c], 0, 0)

    def correct_own(x, carry):
        correct(lambda k, c: vectors[k, c, x], x + 1, 1)
        return carry

    lax.fori_loop(0, 16, correct_own, 0)
    correct(lambda k, c: high[k, c], 17, 2)


def sweeps(residual, scale, s1, s2, emit):
    def sweep1(i, carry):
        w = scale[i]
        for c in range(3):
            s1[c, i] = w * residual[c, i]
        return carry

    lax.fori_loop(0, 22, sweep1, 0, unroll=2)

    def sweep2(i, carry):
        w = scale[i]
        u0, terms = stencil_terms(s1, i)
        for c in range(3):
            s2[c, i] = (1.0 - relaxation) * u0[c] + w * (residual[c, i] + terms[c])
        return carry

    lax.fori_loop(1, 21, sweep2, 0, unroll=2)

    def sweep3(i, carry):
        w = scale[i]
        u0, terms = stencil_terms(s2, i)
        for c in range(3):
            emit(c, i, (1.0 - relaxation) * u0[c] + w * (residual[c, i] + terms[c]))
        return carry

    lax.fori_loop(2, 20, sweep3, 0, unroll=2)


def sweeps_kernel(residual, scale, smooth, s1, s2):
    def emit(c, i, value):
        smooth[c, i - 2] = value

    sweeps(residual, scale, s1, s2, emit)


def main_kernel(first, *refs):
    if first:
        (residual_in, scale, correction, smooth, z_out, image_out, low_out, high_out, dots,
         zed) = refs
        residual = residual_in
    else:
        (scalars, residual_in, held_in, own, low, high, yplus, yminus, zplus, zminus, scale,
         correction, residual, held,
         z_out, image_out, low_out, high_out, dots, s1, s2, zed) = refs
        step = scalars[1:2, 0:1]
        momentum = scalars[2:3, 0:1]
        for i in range(22):
            for c in range(3):
                image = assemble(own, low, high, yplus, yminus, zplus, zminus, c, i)
                image = image + momentum * held_in[c, i]
                held[c, i] = image
                residual[c, i] = residual_in[c, i] - step * image

    if first:
        for i in range(2, 20):
            for c in range(3):
                zed[c, i] = smooth[c, i - 2] + correction[c, i - 2]
    else:

        def emit(c, i, value):
            zed[c, i] = correction[c, i - 2] + value

        sweeps(residual, scale, s1, s2, emit)

    def apply(x, carry):
        rz, zz = carry
        i = x + 3
        diagonal = relaxation / scale[i, 0:16, 0:128]
        u0, terms = stencil_terms(zed, i)
        for c in range(3):
            zc = u0[c][0:16, 0:128]
            image = diagonal * zc - terms[c][0:16, 0:128]
            z_out[c, x] = zc
            image_out[c, x] = image
            rz = rz + residual[c, i, 0:16, 0:128] * zc
            zz = zz + zc * image
        return rz, zz

    zero = jnp.zeros((16, 128), f32)
    rz, zz = lax.fori_loop(0, 16, apply, (zero, zero), unroll=2)
    for c in range(3):
        for x in range(H):
            low_out[c, x] = image_out[c, x]
            high_out[c, x] = image_out[c, 16 - H + x]
    dots[0:1] = jnp.sum(rz, axis=0, keepdims=True)
    dots[1:2] = jnp.sum(zz, axis=0, keepdims=True)
    dots[2:8] = jnp.zeros((6, 128), f32)


def sums_kernel(vectors, image, dots, payload):
    rows = jnp.concatenate([restrict_rows(vectors, image), dots[...]], axis=0)
    payload[...] = jnp.broadcast_to(lanes_of(rows), (128, 128))


def final_kernel(pieces, scalars, residual_in, held, image, zprev, solution_in, direction_in,
                 solution_out, residual_out, direction_out):
    totals = jnp.sum(pieces[...], axis=0, keepdims=True)
    lane = iota((1, 128), 1)
    rho = jnp.sum(jnp.where(lane == 16, totals, 0.0), axis=1, keepdims=True)
    energy = jnp.sum(jnp.where(lane == 17, totals, 0.0), axis=1, keepdims=True)
    momentum = rho / scalars[0:1, 0:1]
    step = rho / (energy - momentum * rho / scalars[1:2, 0:1])

    def plane(x, carry):
        for c in range(3):
            d = zprev[c, x] + momentum * direction_in[c, x]
            direction_out[c, x] = d
            solution_out[c, x] = solution_in[c, x] + step * d
            full = image[c, x] + momentum * held[c, x + H, 0:16, 0:128]
            residual_out[c, x] = residual_in[c, x + H, 0:16, 0:128] - step * full
        return carry

    lax.fori_loop(0, 16, plane, 0)


def both_ways(to_next, to_prev, axis):
    count = lax.axis_size(axis)
    ahead = [(i, (i + 1) % count) for i in range(count)]
    back = [((i + 1) % count, i) for i in range(count)]
    return lax.ppermute(to_next, axis, ahead), lax.ppermute(to_prev, axis, back)


def halo(own, low_edge, high_edge, before=None, middle=None):
    comps = own.shape[0]
    low, high = both_ways(high_edge, low_edge, "gx")
    (ypack,) = call(pack_y_kernel, [(comps, 22, 8, 128)], [own, low, high], after=before)
    yminus, yplus = both_ways(ypack, ypack, "gy")
    done = middle(ypack) if middle else None
    (zpack,) = call(
        pack_z_kernel, [(comps, 24, 256)], [own, low, high, yplus, yminus],
        after=done[0] if middle else None,
    )
    zminus, zplus = both_ways(zpack, zpack, GZ)
    return (low, high, yplus, yminus, zplus, zminus), zpack, done


def share(rows):
    count = lax.axis_size(EVERY)
    return lax.all_to_all(rows.reshape(count, 1, 128), EVERY, 0, 0, tiled=True).reshape(count, 128)


def vector_halo_y(faces, vectors, token):
    low, high = both_ways(*faces, "gx")
    shape = (3, 18, 16, 128)
    to_low, to_high = call(
        vectors_y_kernel, [shape, shape], [vectors, low, high], after=token, limit=12
    )
    yminus, yplus = both_ways(to_high, to_low, "gy")
    return to_low, (low, high, yplus, yminus)


def vector_halo_z(face, sides, row, token):
    packed, row = call(
        vectors_z_kernel, [(3, 5, 24, 128), (128, 128)], [face, *sides, row], after=token
    )
    zminus, zplus = both_ways(packed, packed, GZ)
    return packed, zplus, zminus, row


def body(forces, mass_shift, deflation, coarse_factor, coarse_slot):
    gx, gy, gz = lax.axis_index("gx"), lax.axis_index("gy"), lax.axis_index(GZ)
    nx, ny, nz = lax.axis_size("gx"), lax.axis_size("gy"), lax.axis_size(GZ)
    faces = deflation[:, :, 15], deflation[:, :, 0]
    place = jnp.stack([gz, gx]).astype(jnp.int32)
    keep, send = call(
        factor_kernel, [(9, 64, 128), (7, 64, 128)], [place, coarse_factor],
        [pltpu.VMEM((256, 256), f32)],
    )
    received = lax.ppermute(send, GZ, [(i, 7 - i) for i in range(8)])
    (folded,) = call(fold_kernel, [(9, 64, 128)], [place, keep, received], after=faces[0])
    factor = lax.all_gather(folded, ("gx", *GZ)).reshape(4, 8, 9, 64, 128)

    order = jnp.arange(coarse_slot.shape[0], dtype=jnp.int32)
    slots = (order[:, None] == coarse_slot[None, :]).astype(f32)
    slot_row = coarse_slot.astype(f32)[None, :]
    moves = jnp.arange(-1, 2, dtype=jnp.int32)
    px = (gx + moves)[:, None, None]
    py = (gy + moves)[None, :, None]
    pz = (gz + moves)[None, None, :]
    valid = (px >= 0) & (px < nx) & (py >= 0) & (py < ny) & (pz >= 0) & (pz < nz)
    where = ((px * ny + py) * nz + pz).reshape(-1)
    valid = valid.reshape(-1)
    chosen = (where[:, None] == order[None, :]) & valid[:, None]
    near = jnp.sum(jnp.where(chosen[:, None, :], slots[None], 0.0), axis=2)
    near = jnp.concatenate([near, jnp.zeros((5, near.shape[1]), f32)], axis=0)
    inside = jnp.stack([gx > 0, gx < nx - 1, gy > 0, gy < ny - 1, gz > 0, gz < nz - 1, gz > 0, gz > 0])
    inside = inside.astype(jnp.int32)

    scale_own = relaxation / (mass_shift + (6.0 * off_diagonal + 2.0 * stiffer))
    fields = jnp.concatenate([forces, scale_own[None]], axis=0)
    block = (3, 16, 16, 128)
    lines = (3, 16, 16, 128)
    row, face = call(vectors_kernel, [(128, 128), lines], [deflation, forces], limit=10, micros=6)
    def beside(token):
        return vector_halo_y(faces, deflation, token)

    received, zpack, (_, sides) = halo(fields, fields[:, :H], fields[:, 16 - H :], row, beside)
    packed, zplus, zminus, row = vector_halo_z(face, sides, row, zpack)
    pieces = share(row)
    ext = (22, 24, 256)
    patch = (3, 18, 24, 256)
    work = [pltpu.VMEM((3, *ext), f32)] * 3
    residual, scale = call(start_kernel, [(3, *ext), ext], [inside, fields, *received], after=packed)
    (vz,) = call(vectors_end_kernel, [(3, 18, 24, 128)], [zplus, zminus])
    (smooth,) = call(
        sweeps_kernel, [patch], [residual, scale], work[:2], after=vz, limit=8, micros=4
    )
    around = (*sides, vz)
    weight_shapes = [(48, 128), (3, 32, 128), (3, 24, 128)]
    edge = (3, H, 16, 128)
    main_outs = [block, block, edge, edge, (8, 128)]

    g, wx, wy, wz = call(
        functools.partial(coarse_kernel, 0), [(8, 256)] + weight_shapes,
        [pieces, slot_row, near, factor], limit=12, micros=5,
    )
    (correction,) = call(
        functools.partial(correct_kernel, True), [patch], [wx, wy, wz, deflation, *around],
        limit=13, micros=3,
    )
    z, image, low_edge, high_edge, dots = call(
        functools.partial(main_kernel, True), main_outs,
        [residual, scale, correction, smooth], work[:1], limit=10, micros=3,
    )
    (row,) = call(sums_kernel, [(128, 128)], [deflation, image, dots], limit=8, micros=2)
    held = jnp.zeros_like(residual)
    solution = jnp.zeros_like(forces)
    direction = jnp.zeros_like(forces)
    state = ()
    for iteration in range(1, ITERS):
        pieces = share(row)

        def coarse(token):
            return call(
                functools.partial(coarse_kernel, min(iteration, 2)),
                [(8, 256)] + weight_shapes + [(8, 256), (8, 128)],
                [pieces, slot_row, near, factor, g, *state],
                after=token, limit=12, micros=5,
            )

        received, zpack, done = halo(image, low_edge, high_edge, None, coarse)
        g, wx, wy, wz, hdir, scalars = done
        state = (hdir, scalars)
        correction, solution, direction = call(
            functools.partial(correct_kernel, False), [patch, block, block],
            [scalars, z, solution, direction, wx, wy, wz, deflation, *around],
            after=zpack, limit=14, micros=3,
        )
        residual, held, z, image, low_edge, high_edge, dots = call(
            functools.partial(main_kernel, False), [(3, *ext), (3, *ext)] + main_outs,
            [scalars, residual, held, image, *received, scale, correction],
            work, limit=17, micros=5,
        )
        (row,) = call(sums_kernel, [(128, 128)], [deflation, image, dots], limit=8, micros=2)
    pieces = share(row)
    return tuple(
        call(
            final_kernel,
            [block] * 3,
            [pieces, scalars, residual, held, image, z, solution, direction],
        )
    )


def solution(mesh):
    finer = Mesh(
        mesh.devices.reshape(mesh.shape["gx"], mesh.shape["gy"], 4, 2), ("gx", "gy", "gz_0", "gz_1")
    )
    return jax.shard_map(
        body,
        mesh=finer,
        in_specs=(
            P(None, "gx", "gy", GZ),
            P("gx", "gy", GZ),
            P(None, None, "gx", "gy", GZ),
            P(GZ, None),
            P(),
        ),
        out_specs=(P(None, "gx", "gy", GZ), P(None, "gx", "gy", GZ), P(None, "gx", "gy", GZ)),
        check_vma=False,
    )
```

```python
import functools

import jax
import jax.numpy as jnp
from jax import lax
from jax.experimental import pallas as pl
from jax.experimental.pallas import tpu as pltpu
from jax.sharding import Mesh
from jax.sharding import PartitionSpec as P

ITERS = 4
GZ = ("gz_0", "gz_1")
EVERY = ("gx", "gy", "gz_0", "gz_1")

relaxation = 0.6
off_diagonal = 0.25
stiffer = 0.625
highest = lax.Precision.HIGHEST
f32 = jnp.float32
H = 3
MIB = 1 << 20


def call(kernel, outs, ins, scratch=(), after=None, limit=8, micros=1):
    vmem = pl.BlockSpec(memory_space=pltpu.VMEM)
    specs = []
    for a in ins:
        specs.append(pl.BlockSpec(memory_space=pltpu.SMEM) if a.dtype == jnp.int32 else vmem)
    if after is not None:
        after = after if isinstance(after, list) else [after]
        count = len(after)
        specs = [pl.BlockSpec(memory_space=pl.ANY)] * count + specs
        ins = [*after, *ins]
        inner = kernel

        def kernel(*refs):
            inner(*refs[count:])

    return pl.pallas_call(
        kernel,
        out_shape=[jax.ShapeDtypeStruct(s, f32) for s in outs],
        in_specs=specs,
        out_specs=[vmem] * len(outs),
        scratch_shapes=list(scratch),
        cost_estimate=pl.CostEstimate(flops=0, bytes_accessed=micros * 3_000_000, transcendentals=0),
        compiler_params=pltpu.CompilerParams(vmem_limit_bytes=limit * MIB),
    )(*ins)


def iota(shape, dim):
    return lax.broadcasted_iota(jnp.int32, shape, dim)


def mm(a, b):
    return jnp.dot(a, b, precision=highest, preferred_element_type=f32)


def inverse_of(own):
    n = own.shape[0]
    i0, i1 = iota((n, n), 0), iota((n, n), 1)
    eye = i0 == i1
    across = 1.0 / jnp.sum(jnp.where(eye, own, 0.0), axis=1, keepdims=True)
    down = 1.0 / jnp.sum(jnp.where(eye, own, 0.0), axis=0, keepdims=True)
    lower = jnp.where(((i0 // 4) == (i1 // 4)) & (i0 > i1), own, 0.0) * across
    square = mm(lower, lower)
    inverse = jnp.where(eye, 1.0, 0.0) - lower + square - mm(lower, square)
    inverse = inverse * down
    size = 4
    while size < n:
        same = (i0 // (2 * size)) == (i1 // (2 * size))
        block = jnp.where(same & ((i0 // size) > (i1 // size)), own, 0.0)
        inverse = inverse - mm(inverse, mm(block, inverse))
        size *= 2
    return inverse


def factor_kernel(place, rows, keep, send, hold):
    j, part = place[0], place[1]
    n = rows.shape[0]
    share = keep.shape[1]
    tiles = n // 128
    start = pl.multiple_of(j * n, n)
    own = rows[:, pl.ds(start, n)]
    half = n // 2
    upper = inverse_of(own[:half, :half])
    lower = inverse_of(own[half:, half:])
    inverse = jnp.concatenate(
        [
            jnp.concatenate([upper, jnp.zeros_like(upper)], axis=1),
            jnp.concatenate([-mm(lower, mm(own[half:, :half], upper)), lower], axis=1),
        ],
        axis=0,
    )
    hold[...] = inverse
    mine = hold[pl.ds(pl.multiple_of(part * share, share), share), :]

    def put(t, value):
        for u in range(tiles):
            i = t * tiles + u
            piece = value[:, u * 128 : (u + 1) * 128]
            if i < keep.shape[0]:
                keep[i] = piece
            else:
                send[i - keep.shape[0]] = piece

    for t in range(rows.shape[1] // n):

        @pl.when(t < j)
        def _():
            put(t, mm(mine, rows[:, t * n : (t + 1) * n]))

        @pl.when(t == j)
        def _():
            put(t, mine)

        @pl.when(t > j)
        def _():
            put(t, jnp.zeros_like(mine))


def fold_kernel(place, keep, received, out):
    j = place[0]
    out[...] = keep[...]
    for i in range(7):

        @pl.when(i < 7 - 2 * j)
        def _():
            out[2 * j + 2 + i] = received[i]


def lanes_of(sums):
    count = sums.shape[0]
    column = jnp.sum(sums, axis=1, keepdims=True)
    placed = jnp.where(iota((count, 128), 0) == iota((count, 128), 1), column, 0.0)
    return jnp.sum(placed, axis=0, keepdims=True)


def restrict_rows(vectors, field):
    count = vectors.shape[0]

    def plane(x, acc):
        acc = list(acc)
        for c in range(3):
            values = field[c, x]
            for k in range(count):
                part = vectors[k, c, x] * values
                acc[k] = acc[k] + (part[:8] + part[8:])
        return tuple(acc)

    acc = lax.fori_loop(0, 16, plane, tuple(jnp.zeros((8, 128), f32) for _ in range(count)))
    rows = [jnp.sum(a, axis=0, keepdims=True) for a in acc]
    return jnp.concatenate(rows, axis=0)


def face_lanes(vector_of):
    lane = iota((16, 128), 1)
    face = jnp.zeros((16, 128), f32)
    for k in range(16):
        v = vector_of(k)
        first = pltpu.roll(v, k, 1) if k else v
        face = face + jnp.where(lane == k, first, jnp.where(lane == 16 + k, pltpu.roll(v, 17 + k, 1), 0.0))
    return face


def vectors_kernel(vectors, field, out, face):
    out[...] = jnp.broadcast_to(lanes_of(restrict_rows(vectors, field)), (128, 128))

    def plane(x, carry):
        for c in range(3):
            face[c, x] = face_lanes(lambda k: vectors[k, c, x])
        return carry

    lax.fori_loop(0, 16, plane, 0)


def vectors_y_kernel(vectors, low, high, sums, to_low, to_high, sums_out):
    sums_out[...] = sums[...]

    def plane(x, carry):
        for c in range(3):
            for k in range(16):
                to_low[c, x + 1, k : k + 1] = vectors[k, c, x, 0:1]
                to_high[c, x + 1, k : k + 1] = vectors[k, c, x, 15:16]
        return carry

    lax.fori_loop(0, 16, plane, 0)
    for c in range(3):
        for source, i in ((low, 0), (high, 17)):
            for k in range(16):
                to_low[c, i, k : k + 1] = source[k, c, 0:1]
                to_high[c, i, k : k + 1] = source[k, c, 15:16]


def vectors_z_kernel(face, low, high, yplus, yminus, out):
    row, lane = iota((16, 128), 0), iota((16, 128), 1)

    def lines(source, c, i):
        v = source[c, i]
        first = jnp.sum(jnp.where(lane == 0, v, 0.0), axis=1, keepdims=True)
        last = jnp.sum(jnp.where(lane == 127, v, 0.0), axis=1, keepdims=True)
        placed = jnp.where(lane == row, first, jnp.where(lane == row + 16, last, 0.0))
        return jnp.sum(placed, axis=0, keepdims=True)

    r8 = iota((8, 128), 0)

    for c in range(3):
        for group in range(5):
            packed = jnp.zeros((24, 128), f32)
            for i in range(4 * group, min(4 * group + 4, 18)):
                if i == 0:
                    own = face_lanes(lambda k: low[k, c])
                elif i == 17:
                    own = face_lanes(lambda k: high[k, c])
                else:
                    own = face[c, i - 1]
                line = jnp.where(
                    r8 == 0, lines(yplus, c, i), jnp.where(r8 == 7, lines(yminus, c, i), 0.0)
                )
                plane = jnp.concatenate([own, line], axis=0)
                if i % 4:
                    plane = pltpu.roll(plane, 32 * (i % 4), 1)
                packed = packed + plane
            out[c, group] = packed


def vectors_end_kernel(zplus, zminus, vz):
    lane = iota((24, 128), 1)
    for c in range(3):
        for i in range(18):
            plane = jnp.where(lane % 32 < 16, zplus[c, i // 4], zminus[c, i // 4])
            if i % 4:
                plane = pltpu.roll(plane, 128 - 32 * (i % 4), 1)
            vz[c, i] = plane


def pack_y(tile0, tile1):
    return jnp.where(iota(tile0.shape, tile0.ndim - 2) < 4, tile0, tile1)


def pack_y_kernel(own, low, high, out):
    for c in range(own.shape[0]):
        for x in range(H):
            out[c, x] = pack_y(low[c, x, :8], low[c, x, 8:])
            out[c, H + 16 + x] = pack_y(high[c, x, :8], high[c, x, 8:])
        for x in range(16):
            out[c, H + x] = pack_y(own[c, x, :8], own[c, x, 8:])


def plane_parts(own, low, high, c, i):
    if i < H:
        return low[c, i]
    if i < H + 16:
        return own[c, i - H]
    return high[c, i - H - 16]


def pack_z_kernel(own, low, high, yplus, yminus, out):
    lane = iota((24, 128), 1)
    edge = (lane < H) | (lane >= 128 - H)
    for c in range(own.shape[0]):
        packed = [jnp.zeros((24, 128), f32), jnp.zeros((24, 128), f32)]
        for i in range(22):
            ytile = pack_y(yplus[c, i], yminus[c, i])
            plane = jnp.concatenate([plane_parts(own, low, high, c, i), ytile], axis=0)
            plane = jnp.where(edge, plane, 0.0)
            shift = (8 * i) % 128
            if shift:
                plane = pltpu.roll(plane, shift, 1)
            packed[i // 16] = packed[i // 16] + plane
        out[c, :, :128] = packed[0]
        out[c, :, 128:] = packed[1]


def assemble(own, low, high, yplus, yminus, zplus, zminus, c, i):
    lane = iota((24, 128), 1)
    ytile = pack_y(yplus[c, i], yminus[c, i])
    centre = jnp.concatenate([plane_parts(own, low, high, c, i), ytile], axis=0)
    half = slice(0, 128) if i < 16 else slice(128, 256)
    side = jnp.where(lane % 8 < 4, zplus[c, :, half], zminus[c, :, half])
    shift = (8 * i) % 128
    if shift:
        side = pltpu.roll(side, 128 - shift, 1)
    side = jnp.where((lane < H) | (lane >= 128 - H), side, 0.0)
    return jnp.concatenate([centre, side], axis=1)


def start_kernel(place, own, low, high, yplus, yminus, zplus, zminus, residual, scale):
    inside = []
    for at, count in ((place[1], 4), (place[2], 4), (place[0], 8)):
        inside += [jnp.where(at > 0, 1, 0), jnp.where(at < count - 1, 1, 0)]
    row, lane = iota((24, 256), 0), iota((24, 256), 1)
    keep = jnp.where(row < 16, 1, jnp.where(row < 20, inside[3], inside[2]))
    keep = keep * jnp.where(lane < 128, 1, jnp.where(lane < 192, inside[5], inside[4]))
    keep = jnp.where((row >= 16 + H) & (row < 24 - H), 0, keep)
    for i in range(22):
        for c in range(4):
            plane = assemble(own, low, high, yplus, yminus, zplus, zminus, c, i)
            if c < 3:
                residual[c, i] = plane
            else:
                here = keep
                if i < H:
                    here = keep * inside[0]
                elif i >= H + 16:
                    here = keep * inside[1]
                lanes_in = (lane < 128 + H) | (lane >= 256 - H)
                scale[i] = jnp.where((here > 0) & lanes_in, plane, 0.0)


def rows_to_column(row, eye):
    return jnp.sum(jnp.where(eye, row, 0.0), axis=1, keepdims=True)


def column_to_row(column, eye):
    return jnp.sum(jnp.where(eye, column, 0.0), axis=0, keepdims=True)


def repeat_lanes(x):
    for shift in (16, 32, 64):
        x = x + pltpu.roll(x, shift, 1)
    return x


def neighbours(place):
    n, lane = iota((32, 128), 0), iota((32, 128), 1)
    x = jnp.where(n < 9, 0, jnp.where(n < 18, 1, 2))
    n = n - 9 * x
    y = jnp.where(n < 3, 0, jnp.where(n < 6, 1, 2))
    z = n - 3 * y
    px, py, pz = place[1] + x - 1, place[2] + y - 1, place[0] + z - 1
    valid = (px >= 0) & (px < 4) & (py >= 0) & (py < 4) & (pz >= 0) & (pz < 8) & (z < 3)
    return jnp.where(valid & ((px * 4 + py) * 8 + pz == lane), 1.0, 0.0)


def coarse_kernel(stage, first, pieces, second, factor, *refs):
    if stage == 0:
        g_out, wx, wy, wz, near_out, ordering_out = refs
    elif stage == 1:
        g_in, g_out, wx, wy, wz, hdir_out, scalars_out = refs
    else:
        g_in, hdir_in, scalars_in, g_out, wx, wy, wz, hdir_out, scalars_out = refs
    blocks = factor.shape[1]

    def tile(j, t):
        if t > 8:
            j, t = 7 - j, 2 * (7 - j) + t - 7
        return jnp.concatenate([factor[p, j, t] for p in range(factor.shape[0])], axis=0)

    q0, l256 = iota((128, 256), 0), iota((128, 256), 1)
    spot = (l256 // 16) == (q0 % 16)
    got = pieces[...]
    if stage == 0:
        ordering = jnp.where(iota((128, 128), 0).astype(f32) == second[...], 1.0, 0.0)
        near = lax.dot_general(
            neighbours(first), ordering, (((1,), (1,)), ((), ())), precision=highest,
            preferred_element_type=f32,
        )
        near_out[...] = near
        ordering_out[...] = ordering
    else:
        near, ordering = first[...], second[...]
    tiled = mm(ordering, repeat_lanes(jnp.where(iota((128, 128), 1) < 16, got, 0.0)))
    ordered = jnp.where(spot, jnp.concatenate([tiled, tiled], axis=1), 0.0)
    ordered = jnp.sum(ordered.reshape(8, 16, 256), axis=1)
    if stage == 0:
        g = ordered
    else:
        totals = jnp.sum(got, axis=0, keepdims=True)
        lane = iota((1, 128), 1)
        rho = jnp.sum(jnp.where(lane == 16, totals, 0.0), axis=1, keepdims=True)
        energy = jnp.sum(jnp.where(lane == 17, totals, 0.0), axis=1, keepdims=True)
        if stage == 1:
            momentum = jnp.zeros_like(rho)
            step = rho / energy
            hdir = ordered
        else:
            rho_prior = scalars_in[0:1, 0:1]
            step_prior = scalars_in[1:2, 0:1]
            momentum = rho / rho_prior
            step = rho / (energy - momentum * rho / step_prior)
            hdir = ordered + momentum * hdir_in[...]
        g = g_in[...] - step * hdir
        hdir_out[...] = hdir
        r8 = iota((8, 128), 0)
        scalars_out[...] = jnp.where(r8 == 0, rho, jnp.where(r8 == 1, step, momentum))
    g_out[...] = g
    eye = iota((128, 128), 0) == iota((128, 128), 1)
    yrow, ycol = [], []
    for j in range(blocks):
        acc = tile(j, 2 * j) * g[j : j + 1, :128] + tile(j, 2 * j + 1) * g[j : j + 1, 128:]
        for t in range(2 * j):
            acc = acc - tile(j, t) * yrow[t]
        column = jnp.sum(acc, axis=1, keepdims=True)
        for u in range(2):
            yrow.append(column_to_row(column[u * 128 : (u + 1) * 128], eye))
    vcol = [None] * blocks
    crow = [None] * blocks
    for i in range(blocks - 1, -1, -1):
        columns = []
        for u in range(2):
            t = 2 * i + u
            value = yrow[t]
            if i < blocks - 1:
                acc = tile(i + 1, t) * vcol[i + 1]
                for k in range(i + 2, blocks):
                    acc = acc + tile(k, t) * vcol[k]
                value = value - jnp.sum(acc, axis=0, keepdims=True)
            columns.append(rows_to_column(value, eye))
        vcol[i] = jnp.concatenate(columns, axis=0)
        crow[i] = jnp.concatenate(
            [jnp.sum(tile(i, 2 * i + u) * vcol[i], axis=0, keepdims=True) for u in range(2)],
            axis=1,
        )
    spread_c = jnp.concatenate(
        [jnp.broadcast_to(crow[b], (16, 256)) for b in range(blocks)], axis=0
    )
    spread_c = jnp.where(spot, spread_c, 0.0)
    by_slot = repeat_lanes(spread_c[:, :128] + spread_c[:, 128:])
    weights = mm(near, by_slot)

    def w(x, y, z):
        n = x * 9 + y * 3 + z
        return weights[n : n + 1, :]

    r16, l16 = iota((16, 128), 0), iota((16, 128), 1)
    pick16 = r16 == l16
    row24, lane24 = iota((24, 128), 0), iota((24, 128), 1)
    for x in range(3):
        wx[16 * x : 16 * x + 16] = jnp.broadcast_to(
            jnp.sum(jnp.where(pick16, w(x, 1, 1), 0.0), axis=1, keepdims=True), (16, 128)
        )
        for side, y in ((0, 2), (1, 0)):
            wy[x, 16 * side : 16 * side + 16] = jnp.broadcast_to(
                jnp.sum(jnp.where(pick16, w(x, y, 1), 0.0), axis=1, keepdims=True), (16, 128)
            )

        def side_plane(z):
            return jnp.where(
                row24 < 16,
                w(x, 1, z),
                jnp.where(row24 == 16, w(x, 2, z), jnp.where(row24 == 23, w(x, 0, z), 0.0)),
            )

        wz[x] = jnp.where(
            lane24 < 16, side_plane(2), jnp.where(lane24 < 32, side_plane(0), 0.0)
        )


def stencil_terms(u, i):
    um = [u[c, i - 1] for c in range(3)]
    u0 = [u[c, i] for c in range(3)]
    up = [u[c, i + 1] for c in range(3)]

    def y(f):
        return pltpu.roll(f, 23, 0), pltpu.roll(f, 1, 0)

    def z(f):
        return pltpu.roll(f, 255, 1), pltpu.roll(f, 1, 1)

    dx = [up[c] - um[c] for c in range(3)]
    sx = [up[c] + um[c] for c in range(3)]
    yp, ym, zp, zm = [], [], [], []
    for c in range(3):
        a, b = y(u0[c])
        yp.append(a)
        ym.append(b)
        a, b = z(u0[c])
        zp.append(a)
        zm.append(b)
    sy = [yp[c] + ym[c] for c in range(3)]
    sz = [zp[c] + zm[c] for c in range(3)]
    a, b = y(dx[1])
    mixed0 = a - b
    a, b = z(dx[2])
    mixed0 = mixed0 + (a - b)
    a, b = y(dx[0] + (zp[2] - zm[2]))
    mixed1 = a - b
    a, b = z(dx[0] + (yp[1] - ym[1]))
    mixed2 = a - b
    mixed = [mixed0, mixed1, mixed2]
    own = [sx[0], sy[1], sz[2]]
    return u0, [
        off_diagonal * (sx[c] + sy[c] + sz[c]) + stiffer * own[c] + (0.25 * stiffer) * mixed[c]
        for c in range(3)
    ]


def correct_kernel(stage, *refs):
    if stage == 0:
        wx, wy, wz, vectors, low, high, yplus, yminus, vz, zed = refs
    else:
        scalars, zprev, *refs = refs
        if stage > 1:
            solution_in, direction_in, *refs = refs
        wx, wy, wz, vectors, low, high, yplus, yminus, vz, zed, solution_out, direction_out = refs
        step = scalars[1:2, 0:1]
        momentum = scalars[2:3, 0:1]

        def advance(x, carry):
            for c in range(3):
                if stage == 1:
                    d = zprev[c, x]
                    solution_out[c, x] = step * d
                else:
                    d = zprev[c, x] + momentum * direction_in[c, x]
                    solution_out[c, x] = solution_in[c, x] + step * d
                direction_out[c, x] = d
            return carry

        lax.fori_loop(0, 16, advance, 0)

    lane = iota((24, 128), 1)
    row = iota((8, 128), 0)

    def correct(source, i, region):
        accs = []
        for c in range(3):
            acc = wx[pl.ds(16 * region, 1), :] * source(0, c)
            for k in range(1, 16):
                acc = acc + wx[pl.ds(16 * region + k, 1), :] * source(k, c)
            accs.append(acc)
        for c in range(3):
            plus = jnp.sum(yplus[c, i] * wy[region, :16], axis=0, keepdims=True)
            minus = jnp.sum(yminus[c, i] * wy[region, 16:], axis=0, keepdims=True)
            ytile = jnp.where(row == 0, plus, jnp.where(row == 7, minus, 0.0))
            prod = vz[c, i] * wz[region]
            plus = jnp.sum(jnp.where(lane < 16, prod, 0.0), axis=1, keepdims=True)
            minus = jnp.sum(jnp.where(lane >= 16, prod, 0.0), axis=1, keepdims=True)
            side = jnp.where(lane == 0, plus, jnp.where(lane == 127, minus, 0.0))
            zed[c, i, 0:16, 0:128] = accs[c]
            zed[c, i, 16:24, 0:128] = ytile
            zed[c, i, :, 128:256] = side

    correct(lambda k, c: low[k, c], 0, 0)

    def correct_own(x, carry):
        correct(lambda k, c: vectors[k, c, x], x + 1, 1)
        return carry

    lax.fori_loop(0, 16, correct_own, 0)
    correct(lambda k, c: high[k, c], 17, 2)


def sweeps(residual, scale, s1, s2, emit):
    def sweep1(i, carry):
        w = scale[i]
        for c in range(3):
            s1[c, i] = w * residual[c, i]
        return carry

    lax.fori_loop(0, 22, sweep1, 0, unroll=2)

    def sweep2(i, carry):
        w = scale[i]
        u0, terms = stencil_terms(s1, i)
        for c in range(3):
            s2[c, i] = (1.0 - relaxation) * u0[c] + w * (residual[c, i] + terms[c])
        return carry

    lax.fori_loop(1, 21, sweep2, 0, unroll=2)

    def sweep3(i, carry):
        w = scale[i]
        u0, terms = stencil_terms(s2, i)
        for c in range(3):
            emit(c, i, (1.0 - relaxation) * u0[c] + w * (residual[c, i] + terms[c]))
        return carry

    lax.fori_loop(2, 20, sweep3, 0, unroll=2)


def sweeps_kernel(residual, scale, smooth, s1, s2):
    def emit(c, i, value):
        smooth[c, i - 2] = value

    sweeps(residual, scale, s1, s2, emit)


def main_kernel(stage, *refs):
    if stage == 0:
        (residual_in, scale, correction, smooth, z_out, image_out, low_out, high_out, dots,
         zed) = refs
        residual = residual_in
    else:
        scalars, residual_in, *refs = refs
        if stage > 1:
            held_in, *refs = refs
        (own, low, high, yplus, yminus, zplus, zminus, scale, correction, residual, held,
         z_out, image_out, low_out, high_out, dots, s1, s2, zed) = refs
        step = scalars[1:2, 0:1]
        momentum = scalars[2:3, 0:1]
        for i in range(22):
            for c in range(3):
                image = assemble(own, low, high, yplus, yminus, zplus, zminus, c, i)
                if stage > 1:
                    image = image + momentum * held_in[c, i]
                held[c, i] = image
                residual[c, i] = residual_in[c, i] - step * image

    if stage == 0:
        for i in range(2, 20):
            for c in range(3):
                zed[c, i] = smooth[c, i - 2] + correction[c, i - 2]
    else:

        def emit(c, i, value):
            zed[c, i] = correction[c, i - 2] + value

        sweeps(residual, scale, s1, s2, emit)

    def apply(x, carry):
        rz, zz = carry
        i = x + 3
        diagonal = relaxation / scale[i, 0:16, 0:128]
        u0, terms = stencil_terms(zed, i)
        for c in range(3):
            zc = u0[c][0:16, 0:128]
            image = diagonal * zc - terms[c][0:16, 0:128]
            z_out[c, x] = zc
            image_out[c, x] = image
            rz = rz + residual[c, i, 0:16, 0:128] * zc
            zz = zz + zc * image
        return rz, zz

    zero = jnp.zeros((16, 128), f32)
    rz, zz = lax.fori_loop(0, 16, apply, (zero, zero), unroll=2)
    for c in range(3):
        for x in range(H):
            low_out[c, x] = image_out[c, x]
            high_out[c, x] = image_out[c, 16 - H + x]
    dots[0:1] = jnp.sum(rz, axis=0, keepdims=True)
    dots[1:2] = jnp.sum(zz, axis=0, keepdims=True)
    dots[2:8] = jnp.zeros((6, 128), f32)


def sums_kernel(vectors, image, dots, payload):
    rows = jnp.concatenate([restrict_rows(vectors, image), dots[...]], axis=0)
    payload[...] = jnp.broadcast_to(lanes_of(rows), (128, 128))


def final_kernel(pieces, scalars, residual_in, held, image, zprev, solution_in, direction_in,
                 solution_out, residual_out, direction_out):
    totals = jnp.sum(pieces[...], axis=0, keepdims=True)
    lane = iota((1, 128), 1)
    rho = jnp.sum(jnp.where(lane == 16, totals, 0.0), axis=1, keepdims=True)
    energy = jnp.sum(jnp.where(lane == 17, totals, 0.0), axis=1, keepdims=True)
    momentum = rho / scalars[0:1, 0:1]
    step = rho / (energy - momentum * rho / scalars[1:2, 0:1])

    def plane(x, carry):
        for c in range(3):
            d = zprev[c, x] + momentum * direction_in[c, x]
            direction_out[c, x] = d
            solution_out[c, x] = solution_in[c, x] + step * d
            full = image[c, x] + momentum * held[c, x + H, 0:16, 0:128]
            residual_out[c, x] = residual_in[c, x + H, 0:16, 0:128] - step * full
        return carry

    lax.fori_loop(0, 16, plane, 0)


def both_ways(to_next, to_prev, axis):
    count = lax.axis_size(axis)
    ahead = [(i, (i + 1) % count) for i in range(count)]
    back = [((i + 1) % count, i) for i in range(count)]
    return lax.ppermute(to_next, axis, ahead), lax.ppermute(to_prev, axis, back)


def halo(own, low_edge, high_edge, before=None, middle=None):
    comps = own.shape[0]
    low, high = both_ways(high_edge, low_edge, "gx")
    (ypack,) = call(pack_y_kernel, [(comps, 22, 8, 128)], [own, low, high], after=before)
    yminus, yplus = both_ways(ypack, ypack, "gy")
    done = middle(ypack) if middle else None
    (zpack,) = call(
        pack_z_kernel, [(comps, 24, 256)], [own, low, high, yplus, yminus],
        after=done[0] if middle else None,
    )
    zminus, zplus = both_ways(zpack, zpack, GZ)
    return (low, high, yplus, yminus, zplus, zminus), zpack, done


def share(rows):
    count = lax.axis_size(EVERY)
    return lax.all_to_all(rows.reshape(count, 1, 128), EVERY, 0, 0, tiled=True).reshape(count, 128)


def vector_halo_y(faces, vectors, row, token):
    low, high = both_ways(*faces, "gx")
    shape = (3, 18, 16, 128)
    to_low, to_high, row = call(
        vectors_y_kernel, [shape, shape, (128, 128)], [vectors, low, high, row], after=token, limit=12
    )
    yminus, yplus = both_ways(to_high, to_low, "gy")
    return to_low, (low, high, yplus, yminus), row


def vector_halo_z(face, sides, token):
    (packed,) = call(vectors_z_kernel, [(3, 5, 24, 128)], [face, *sides], after=token)
    zminus, zplus = both_ways(packed, packed, GZ)
    return packed, zplus, zminus


def body(forces, mass_shift, deflation, coarse_factor, coarse_slot):
    gx, gy, gz = lax.axis_index("gx"), lax.axis_index("gy"), lax.axis_index(GZ)
    faces = deflation[:, :, 15], deflation[:, :, 0]
    place = jnp.stack([gz, gx, gy]).astype(jnp.int32)
    slot_row = coarse_slot.astype(f32)[None, :]
    scale_own = relaxation / (mass_shift + (6.0 * off_diagonal + 2.0 * stiffer))
    fields = jnp.concatenate([forces, scale_own[None]], axis=0)
    keep, send = call(
        factor_kernel, [(9, 64, 128), (7, 64, 128)], [place, coarse_factor],
        [pltpu.VMEM((256, 256), f32)],
    )
    received = lax.ppermute(send, GZ, [(i, 7 - i) for i in range(8)])
    (folded,) = call(
        fold_kernel, [(9, 64, 128)], [place, keep, received], after=[faces[0], fields, slot_row]
    )
    factor = lax.all_gather(folded, ("gx", *GZ)).reshape(4, 8, 9, 64, 128)

    block = (3, 16, 16, 128)
    lines = (3, 16, 16, 128)
    row, face = call(vectors_kernel, [(128, 128), lines], [deflation, forces], limit=10, micros=6)
    def beside(token):
        return vector_halo_y(faces, deflation, row, token)

    received, zpack, (_, sides, row) = halo(
        fields, fields[:, :H], fields[:, 16 - H :], row, beside
    )
    pieces = share(row)
    packed, zplus, zminus = vector_halo_z(face, sides, zpack)
    ext = (22, 24, 256)
    patch = (3, 18, 24, 256)
    work = [pltpu.VMEM((3, *ext), f32)] * 3
    residual, scale = call(start_kernel, [(3, *ext), ext], [place, fields, *received], after=packed)
    (vz,) = call(vectors_end_kernel, [(3, 18, 24, 128)], [zplus, zminus])
    (smooth,) = call(
        sweeps_kernel, [patch], [residual, scale], work[:2], after=vz, limit=8, micros=4
    )
    around = (*sides, vz)
    weight_shapes = [(48, 128), (3, 32, 128), (3, 24, 128)]
    edge = (3, H, 16, 128)
    main_outs = [block, block, edge, edge, (8, 128)]

    g, wx, wy, wz, near, ordering = call(
        functools.partial(coarse_kernel, 0), [(8, 256)] + weight_shapes + [(32, 128), (128, 128)],
        [place, pieces, slot_row, factor], limit=12, micros=5,
    )
    (correction,) = call(
        functools.partial(correct_kernel, 0), [patch], [wx, wy, wz, deflation, *around],
        limit=13, micros=3,
    )
    z, image, low_edge, high_edge, dots = call(
        functools.partial(main_kernel, 0), main_outs,
        [residual, scale, correction, smooth], work[:1], limit=10, micros=3,
    )
    (row,) = call(sums_kernel, [(128, 128)], [deflation, image, dots], limit=8, micros=2)
    held, advanced, state = [], [], ()
    for iteration in range(1, ITERS):
        pieces = share(row)
        stage = min(iteration, 2)

        def coarse(token):
            return call(
                functools.partial(coarse_kernel, stage),
                [(8, 256)] + weight_shapes + [(8, 256), (8, 128)],
                [near, pieces, ordering, factor, g, *state],
                after=token, limit=12, micros=5,
            )

        received, zpack, done = halo(image, low_edge, high_edge, row, coarse)
        g, wx, wy, wz, hdir, scalars = done
        state = (hdir, scalars)
        correction, *advanced = call(
            functools.partial(correct_kernel, stage), [patch, block, block],
            [scalars, z, *advanced, wx, wy, wz, deflation, *around],
            after=zpack, limit=14, micros=3,
        )
        residual, *held, z, image, low_edge, high_edge, dots = call(
            functools.partial(main_kernel, stage), [(3, *ext), (3, *ext)] + main_outs,
            [scalars, residual, *held, image, *received, scale, correction],
            work, limit=17, micros=5,
        )
        (row,) = call(sums_kernel, [(128, 128)], [deflation, image, dots], limit=8, micros=2)
    pieces = share(row)
    return tuple(
        call(
            final_kernel,
            [block] * 3,
            [pieces, scalars, residual, *held, image, z, *advanced],
        )
    )


def solution(mesh):
    finer = Mesh(
        mesh.devices.reshape(mesh.shape["gx"], mesh.shape["gy"], 4, 2), ("gx", "gy", "gz_0", "gz_1")
    )
    return jax.shard_map(
        body,
        mesh=finer,
        in_specs=(
            P(None, "gx", "gy", GZ),
            P("gx", "gy", GZ),
            P(None, None, "gx", "gy", GZ),
            P(GZ, None),
            P(),
        ),
        out_specs=(P(None, "gx", "gy", GZ), P(None, "gx", "gy", GZ), P(None, "gx", "gy", GZ)),
        check_vma=False,
    )
```

```python
import functools

import jax
import jax.numpy as jnp
from jax import lax
from jax.experimental import pallas as pl
from jax.experimental.pallas import tpu as pltpu
from jax.sharding import Mesh
from jax.sharding import PartitionSpec as P

ITERS = 4
GZ = ("gz_0", "gz_1")
EVERY = ("gx", "gy", "gz_0", "gz_1")

relaxation = 0.6
off_diagonal = 0.25
stiffer = 0.625
highest = lax.Precision.HIGHEST
f32 = jnp.float32
H = 3
MIB = 1 << 20


def call(kernel, outs, ins, scratch=(), after=None, limit=8, micros=1):
    vmem = pl.BlockSpec(memory_space=pltpu.VMEM)
    specs = []
    for a in ins:
        specs.append(pl.BlockSpec(memory_space=pltpu.SMEM) if a.dtype == jnp.int32 else vmem)
    if after is not None:
        after = after if isinstance(after, list) else [after]
        count = len(after)
        specs = [pl.BlockSpec(memory_space=pl.ANY)] * count + specs
        ins = [*after, *ins]
        inner = kernel

        def kernel(*refs):
            inner(*refs[count:])

    return pl.pallas_call(
        kernel,
        out_shape=[jax.ShapeDtypeStruct(s, f32) for s in outs],
        in_specs=specs,
        out_specs=[vmem] * len(outs),
        scratch_shapes=list(scratch),
        cost_estimate=pl.CostEstimate(flops=0, bytes_accessed=micros * 3_000_000, transcendentals=0),
        compiler_params=pltpu.CompilerParams(vmem_limit_bytes=limit * MIB),
    )(*ins)


def iota(shape, dim):
    return lax.broadcasted_iota(jnp.int32, shape, dim)


def mm(a, b):
    return jnp.dot(a, b, precision=highest, preferred_element_type=f32)


def inverse_of(own):
    n = own.shape[0]
    i0, i1 = iota((n, n), 0), iota((n, n), 1)
    eye = i0 == i1
    across = 1.0 / jnp.sum(jnp.where(eye, own, 0.0), axis=1, keepdims=True)
    down = 1.0 / jnp.sum(jnp.where(eye, own, 0.0), axis=0, keepdims=True)
    lower = jnp.where(((i0 // 4) == (i1 // 4)) & (i0 > i1), own, 0.0) * across
    square = mm(lower, lower)
    inverse = jnp.where(eye, 1.0, 0.0) - lower + square - mm(lower, square)
    inverse = inverse * down
    size = 4
    while size < n:
        same = (i0 // (2 * size)) == (i1 // (2 * size))
        block = jnp.where(same & ((i0 // size) > (i1 // size)), own, 0.0)
        inverse = inverse - mm(inverse, mm(block, inverse))
        size *= 2
    return inverse


def factor_kernel(place, rows, keep, send, hold):
    j, part = place[0], place[1]
    n = rows.shape[0]
    share = keep.shape[1]
    tiles = n // 128
    start = pl.multiple_of(j * n, n)
    own = rows[:, pl.ds(start, n)]
    half = n // 2
    upper = inverse_of(own[:half, :half])
    lower = inverse_of(own[half:, half:])
    inverse = jnp.concatenate(
        [
            jnp.concatenate([upper, jnp.zeros_like(upper)], axis=1),
            jnp.concatenate([-mm(lower, mm(own[half:, :half], upper)), lower], axis=1),
        ],
        axis=0,
    )
    hold[...] = inverse
    mine = hold[pl.ds(pl.multiple_of(part * share, share), share), :]

    def put(t, value):
        for u in range(tiles):
            i = t * tiles + u
            piece = value[:, u * 128 : (u + 1) * 128]
            if i < keep.shape[0]:
                keep[i] = piece
            else:
                send[i - keep.shape[0]] = piece

    for t in range(rows.shape[1] // n):

        @pl.when(t < j)
        def _():
            put(t, mm(mine, rows[:, t * n : (t + 1) * n]))

        @pl.when(t == j)
        def _():
            put(t, mine)

        @pl.when(t > j)
        def _():
            put(t, jnp.zeros_like(mine))


def fold_kernel(place, keep, received, out):
    j = place[0]
    out[...] = keep[...]
    for i in range(7):

        @pl.when(i < 7 - 2 * j)
        def _():
            out[2 * j + 2 + i] = received[i]


def lanes_of(sums):
    count = sums.shape[0]
    column = jnp.sum(sums, axis=1, keepdims=True)
    placed = jnp.where(iota((count, 128), 0) == iota((count, 128), 1), column, 0.0)
    return jnp.sum(placed, axis=0, keepdims=True)


def restrict_rows(vectors, field):
    count = vectors.shape[0]

    def plane(x, acc):
        acc = list(acc)
        for c in range(3):
            values = field[c, x]
            for k in range(count):
                part = vectors[k, c, x] * values
                acc[k] = acc[k] + (part[:8] + part[8:])
        return tuple(acc)

    acc = lax.fori_loop(0, 16, plane, tuple(jnp.zeros((8, 128), f32) for _ in range(count)))
    rows = [jnp.sum(a, axis=0, keepdims=True) for a in acc]
    return jnp.concatenate(rows, axis=0)


def face_lanes(vector_of):
    lane = iota((16, 128), 1)
    face = jnp.zeros((16, 128), f32)
    for k in range(16):
        v = vector_of(k)
        first = pltpu.roll(v, k, 1) if k else v
        face = face + jnp.where(lane == k, first, jnp.where(lane == 16 + k, pltpu.roll(v, 17 + k, 1), 0.0))
    return face


def vectors_kernel(vectors, field, out, face):
    out[...] = jnp.broadcast_to(lanes_of(restrict_rows(vectors, field)), (128, 128))

    def plane(x, carry):
        for c in range(3):
            face[c, x] = face_lanes(lambda k: vectors[k, c, x])
        return carry

    lax.fori_loop(0, 16, plane, 0, unroll=4)


def vectors_y_kernel(vectors, low, high, sums, to_low, to_high, sums_out):
    sums_out[...] = sums[...]

    def plane(x, carry):
        for c in range(3):
            for k in range(16):
                to_low[c, x + 1, k : k + 1] = vectors[k, c, x, 0:1]
                to_high[c, x + 1, k : k + 1] = vectors[k, c, x, 15:16]
        return carry

    lax.fori_loop(0, 16, plane, 0, unroll=4)
    for c in range(3):
        for source, i in ((low, 0), (high, 17)):
            for k in range(16):
                to_low[c, i, k : k + 1] = source[k, c, 0:1]
                to_high[c, i, k : k + 1] = source[k, c, 15:16]


def vectors_z_kernel(face, low, high, yplus, yminus, out):
    row, lane = iota((16, 128), 0), iota((16, 128), 1)

    def lines(source, c, i):
        v = source[c, i]
        first = jnp.sum(jnp.where(lane == 0, v, 0.0), axis=1, keepdims=True)
        last = jnp.sum(jnp.where(lane == 127, v, 0.0), axis=1, keepdims=True)
        placed = jnp.where(lane == row, first, jnp.where(lane == row + 16, last, 0.0))
        return jnp.sum(placed, axis=0, keepdims=True)

    r8 = iota((8, 128), 0)

    for c in range(3):
        for group in range(5):
            packed = jnp.zeros((24, 128), f32)
            for i in range(4 * group, min(4 * group + 4, 18)):
                if i == 0:
                    own = face_lanes(lambda k: low[k, c])
                elif i == 17:
                    own = face_lanes(lambda k: high[k, c])
                else:
                    own = face[c, i - 1]
                line = jnp.where(
                    r8 == 0, lines(yplus, c, i), jnp.where(r8 == 7, lines(yminus, c, i), 0.0)
                )
                plane = jnp.concatenate([own, line], axis=0)
                if i % 4:
                    plane = pltpu.roll(plane, 32 * (i % 4), 1)
                packed = packed + plane
            out[c, group] = packed


def vectors_end_kernel(zplus, zminus, vz):
    lane = iota((24, 128), 1)
    for c in range(3):
        for i in range(18):
            plane = jnp.where(lane % 32 < 16, zplus[c, i // 4], zminus[c, i // 4])
            if i % 4:
                plane = pltpu.roll(plane, 128 - 32 * (i % 4), 1)
            vz[c, i] = plane


def pack_y(tile0, tile1):
    return jnp.where(iota(tile0.shape, tile0.ndim - 2) < 4, tile0, tile1)


def pack_y_kernel(own, low, high, out):
    for c in range(own.shape[0]):
        for x in range(H):
            out[c, x] = pack_y(low[c, x, :8], low[c, x, 8:])
            out[c, H + 16 + x] = pack_y(high[c, x, :8], high[c, x, 8:])
        for x in range(16):
            out[c, H + x] = pack_y(own[c, x, :8], own[c, x, 8:])


def plane_parts(own, low, high, c, i):
    if i < H:
        return low[c, i]
    if i < H + 16:
        return own[c, i - H]
    return high[c, i - H - 16]


def pack_z_kernel(own, low, high, yplus, yminus, out):
    lane = iota((24, 128), 1)
    edge = (lane < H) | (lane >= 128 - H)
    for c in range(own.shape[0]):
        packed = [jnp.zeros((24, 128), f32), jnp.zeros((24, 128), f32)]
        for i in range(22):
            ytile = pack_y(yplus[c, i], yminus[c, i])
            plane = jnp.concatenate([plane_parts(own, low, high, c, i), ytile], axis=0)
            plane = jnp.where(edge, plane, 0.0)
            shift = (8 * i) % 128
            if shift:
                plane = pltpu.roll(plane, shift, 1)
            packed[i // 16] = packed[i // 16] + plane
        out[c, :, :128] = packed[0]
        out[c, :, 128:] = packed[1]


def assemble(own, low, high, yplus, yminus, zplus, zminus, c, i):
    lane = iota((24, 128), 1)
    ytile = pack_y(yplus[c, i], yminus[c, i])
    centre = jnp.concatenate([plane_parts(own, low, high, c, i), ytile], axis=0)
    half = slice(0, 128) if i < 16 else slice(128, 256)
    side = jnp.where(lane % 8 < 4, zplus[c, :, half], zminus[c, :, half])
    shift = (8 * i) % 128
    if shift:
        side = pltpu.roll(side, 128 - shift, 1)
    side = jnp.where((lane < H) | (lane >= 128 - H), side, 0.0)
    return jnp.concatenate([centre, side], axis=1)


def start_kernel(place, own, low, high, yplus, yminus, zplus, zminus, residual, scale):
    inside = []
    for at, count in ((place[1], 4), (place[2], 4), (place[0], 8)):
        inside += [jnp.where(at > 0, 1, 0), jnp.where(at < count - 1, 1, 0)]
    row, lane = iota((24, 256), 0), iota((24, 256), 1)
    keep = jnp.where(row < 16, 1, jnp.where(row < 20, inside[3], inside[2]))
    keep = keep * jnp.where(lane < 128, 1, jnp.where(lane < 192, inside[5], inside[4]))
    keep = jnp.where((row >= 16 + H) & (row < 24 - H), 0, keep)
    for i in range(22):
        for c in range(4):
            plane = assemble(own, low, high, yplus, yminus, zplus, zminus, c, i)
            if c < 3:
                residual[c, i] = plane
            else:
                here = keep
                if i < H:
                    here = keep * inside[0]
                elif i >= H + 16:
                    here = keep * inside[1]
                lanes_in = (lane < 128 + H) | (lane >= 256 - H)
                scale[i] = jnp.where((here > 0) & lanes_in, plane, 0.0)


def rows_to_column(row, eye):
    return jnp.sum(jnp.where(eye, row, 0.0), axis=1, keepdims=True)


def column_to_row(column, eye):
    return jnp.sum(jnp.where(eye, column, 0.0), axis=0, keepdims=True)


def repeat_lanes(x):
    for shift in (16, 32, 64):
        x = x + pltpu.roll(x, shift, 1)
    return x


def neighbours(place):
    n, lane = iota((32, 128), 0), iota((32, 128), 1)
    x = jnp.where(n < 9, 0, jnp.where(n < 18, 1, 2))
    n = n - 9 * x
    y = jnp.where(n < 3, 0, jnp.where(n < 6, 1, 2))
    z = n - 3 * y
    px, py, pz = place[1] + x - 1, place[2] + y - 1, place[0] + z - 1
    valid = (px >= 0) & (px < 4) & (py >= 0) & (py < 4) & (pz >= 0) & (pz < 8) & (z < 3)
    return jnp.where(valid & ((px * 4 + py) * 8 + pz == lane), 1.0, 0.0)


def coarse_kernel(stage, first, pieces, second, factor, *refs):
    if stage == 0:
        g_out, wx, wy, wz, near_out, ordering_out = refs
    elif stage == 1:
        g_in, g_out, wx, wy, wz, hdir_out, scalars_out = refs
    else:
        g_in, hdir_in, scalars_in, g_out, wx, wy, wz, hdir_out, scalars_out = refs
    blocks = factor.shape[1]

    def tile(j, t):
        if t > 8:
            j, t = 7 - j, 2 * (7 - j) + t - 7
        return jnp.concatenate([factor[p, j, t] for p in range(factor.shape[0])], axis=0)

    q0, l256 = iota((128, 256), 0), iota((128, 256), 1)
    spot = (l256 // 16) == (q0 % 16)
    got = pieces[...]
    if stage == 0:
        ordering = jnp.where(iota((128, 128), 0).astype(f32) == second[...], 1.0, 0.0)
        near = lax.dot_general(
            neighbours(first), ordering, (((1,), (1,)), ((), ())), precision=highest,
            preferred_element_type=f32,
        )
        near_out[...] = near
        ordering_out[...] = ordering
    else:
        near, ordering = first[...], second[...]
    tiled = mm(ordering, repeat_lanes(jnp.where(iota((128, 128), 1) < 16, got, 0.0)))
    ordered = jnp.where(spot, jnp.concatenate([tiled, tiled], axis=1), 0.0)
    ordered = jnp.sum(ordered.reshape(8, 16, 256), axis=1)
    if stage == 0:
        g = ordered
    else:
        totals = jnp.sum(got, axis=0, keepdims=True)
        lane = iota((1, 128), 1)
        rho = jnp.sum(jnp.where(lane == 16, totals, 0.0), axis=1, keepdims=True)
        energy = jnp.sum(jnp.where(lane == 17, totals, 0.0), axis=1, keepdims=True)
        if stage == 1:
            momentum = jnp.zeros_like(rho)
            step = rho / energy
            hdir = ordered
        else:
            rho_prior = scalars_in[0:1, 0:1]
            step_prior = scalars_in[1:2, 0:1]
            momentum = rho / rho_prior
            step = rho / (energy - momentum * rho / step_prior)
            hdir = ordered + momentum * hdir_in[...]
        g = g_in[...] - step * hdir
        hdir_out[...] = hdir
        r8 = iota((8, 128), 0)
        scalars_out[...] = jnp.where(r8 == 0, rho, jnp.where(r8 == 1, step, momentum))
    g_out[...] = g
    eye = iota((128, 128), 0) == iota((128, 128), 1)
    yrow, ycol = [], []
    for j in range(blocks):
        acc = tile(j, 2 * j) * g[j : j + 1, :128] + tile(j, 2 * j + 1) * g[j : j + 1, 128:]
        for t in range(2 * j):
            acc = acc - tile(j, t) * yrow[t]
        column = jnp.sum(acc, axis=1, keepdims=True)
        for u in range(2):
            yrow.append(column_to_row(column[u * 128 : (u + 1) * 128], eye))
    vcol = [None] * blocks
    crow = [None] * blocks
    for i in range(blocks - 1, -1, -1):
        columns = []
        for u in range(2):
            t = 2 * i + u
            value = yrow[t]
            if i < blocks - 1:
                acc = tile(i + 1, t) * vcol[i + 1]
                for k in range(i + 2, blocks):
                    acc = acc + tile(k, t) * vcol[k]
                value = value - jnp.sum(acc, axis=0, keepdims=True)
            columns.append(rows_to_column(value, eye))
        vcol[i] = jnp.concatenate(columns, axis=0)
        crow[i] = jnp.concatenate(
            [jnp.sum(tile(i, 2 * i + u) * vcol[i], axis=0, keepdims=True) for u in range(2)],
            axis=1,
        )
    spread_c = jnp.concatenate(
        [jnp.broadcast_to(crow[b], (16, 256)) for b in range(blocks)], axis=0
    )
    spread_c = jnp.where(spot, spread_c, 0.0)
    by_slot = repeat_lanes(spread_c[:, :128] + spread_c[:, 128:])
    weights = mm(near, by_slot)

    def w(x, y, z):
        n = x * 9 + y * 3 + z
        return weights[n : n + 1, :]

    r16, l16 = iota((16, 128), 0), iota((16, 128), 1)
    pick16 = r16 == l16
    row24, lane24 = iota((24, 128), 0), iota((24, 128), 1)
    for x in range(3):
        wx[16 * x : 16 * x + 16] = jnp.broadcast_to(
            jnp.sum(jnp.where(pick16, w(x, 1, 1), 0.0), axis=1, keepdims=True), (16, 128)
        )
        for side, y in ((0, 2), (1, 0)):
            wy[x, 16 * side : 16 * side + 16] = jnp.broadcast_to(
                jnp.sum(jnp.where(pick16, w(x, y, 1), 0.0), axis=1, keepdims=True), (16, 128)
            )

        def side_plane(z):
            return jnp.where(
                row24 < 16,
                w(x, 1, z),
                jnp.where(row24 == 16, w(x, 2, z), jnp.where(row24 == 23, w(x, 0, z), 0.0)),
            )

        wz[x] = jnp.where(
            lane24 < 16, side_plane(2), jnp.where(lane24 < 32, side_plane(0), 0.0)
        )


def stencil_terms(u, i):
    um = [u[c, i - 1] for c in range(3)]
    u0 = [u[c, i] for c in range(3)]
    up = [u[c, i + 1] for c in range(3)]

    def y(f):
        return pltpu.roll(f, 23, 0), pltpu.roll(f, 1, 0)

    def z(f):
        return pltpu.roll(f, 255, 1), pltpu.roll(f, 1, 1)

    dx = [up[c] - um[c] for c in range(3)]
    sx = [up[c] + um[c] for c in range(3)]
    yp, ym, zp, zm = [], [], [], []
    for c in range(3):
        a, b = y(u0[c])
        yp.append(a)
        ym.append(b)
        a, b = z(u0[c])
        zp.append(a)
        zm.append(b)
    sy = [yp[c] + ym[c] for c in range(3)]
    sz = [zp[c] + zm[c] for c in range(3)]
    a, b = y(dx[1])
    mixed0 = a - b
    a, b = z(dx[2])
    mixed0 = mixed0 + (a - b)
    a, b = y(dx[0] + (zp[2] - zm[2]))
    mixed1 = a - b
    a, b = z(dx[0] + (yp[1] - ym[1]))
    mixed2 = a - b
    mixed = [mixed0, mixed1, mixed2]
    own = [sx[0], sy[1], sz[2]]
    return u0, [
        off_diagonal * (sx[c] + sy[c] + sz[c]) + stiffer * own[c] + (0.25 * stiffer) * mixed[c]
        for c in range(3)
    ]


def correct_kernel(stage, *refs):
    if stage == 0:
        wx, wy, wz, vectors, low, high, yplus, yminus, vz, zed = refs
    else:
        scalars, zprev, *refs = refs
        if stage > 1:
            solution_in, direction_in, *refs = refs
        wx, wy, wz, vectors, low, high, yplus, yminus, vz, zed, solution_out, direction_out = refs
        step = scalars[1:2, 0:1]
        momentum = scalars[2:3, 0:1]

        def advance(x, carry):
            for c in range(3):
                if stage == 1:
                    d = zprev[c, x]
                    solution_out[c, x] = step * d
                else:
                    d = zprev[c, x] + momentum * direction_in[c, x]
                    solution_out[c, x] = solution_in[c, x] + step * d
                direction_out[c, x] = d
            return carry

        lax.fori_loop(0, 16, advance, 0, unroll=4)

    lane = iota((24, 128), 1)
    row = iota((8, 128), 0)

    def correct(source, i, region):
        accs = []
        for c in range(3):
            acc = wx[pl.ds(16 * region, 1), :] * source(0, c)
            for k in range(1, 16):
                acc = acc + wx[pl.ds(16 * region + k, 1), :] * source(k, c)
            accs.append(acc)
        for c in range(3):
            plus = jnp.sum(yplus[c, i] * wy[region, :16], axis=0, keepdims=True)
            minus = jnp.sum(yminus[c, i] * wy[region, 16:], axis=0, keepdims=True)
            ytile = jnp.where(row == 0, plus, jnp.where(row == 7, minus, 0.0))
            prod = vz[c, i] * wz[region]
            plus = jnp.sum(jnp.where(lane < 16, prod, 0.0), axis=1, keepdims=True)
            minus = jnp.sum(jnp.where(lane >= 16, prod, 0.0), axis=1, keepdims=True)
            side = jnp.where(lane == 0, plus, jnp.where(lane == 127, minus, 0.0))
            zed[c, i, 0:16, 0:128] = accs[c]
            zed[c, i, 16:24, 0:128] = ytile
            zed[c, i, :, 128:256] = side

    correct(lambda k, c: low[k, c], 0, 0)

    def correct_own(x, carry):
        correct(lambda k, c: vectors[k, c, x], x + 1, 1)
        return carry

    lax.fori_loop(0, 16, correct_own, 0, unroll=8)
    correct(lambda k, c: high[k, c], 17, 2)


def sweeps(residual, scale, s1, s2, emit):
    def sweep1(i, carry):
        w = scale[i]
        for c in range(3):
            s1[c, i] = w * residual[c, i]
        return carry

    lax.fori_loop(0, 22, sweep1, 0, unroll=2)

    def sweep2(i, carry):
        w = scale[i]
        u0, terms = stencil_terms(s1, i)
        for c in range(3):
            s2[c, i] = (1.0 - relaxation) * u0[c] + w * (residual[c, i] + terms[c])
        return carry

    lax.fori_loop(1, 21, sweep2, 0, unroll=10)

    def sweep3(i, carry):
        w = scale[i]
        u0, terms = stencil_terms(s2, i)
        for c in range(3):
            emit(c, i, (1.0 - relaxation) * u0[c] + w * (residual[c, i] + terms[c]))
        return carry

    lax.fori_loop(2, 20, sweep3, 0, unroll=9)


def sweeps_kernel(residual, scale, smooth, s1, s2):
    def emit(c, i, value):
        smooth[c, i - 2] = value

    sweeps(residual, scale, s1, s2, emit)


def main_kernel(stage, *refs):
    if stage == 0:
        (residual_in, scale, correction, smooth, z_out, image_out, low_out, high_out, dots,
         zed) = refs
        residual = residual_in
    else:
        scalars, residual_in, *refs = refs
        if stage > 1:
            held_in, *refs = refs
        (own, low, high, yplus, yminus, zplus, zminus, scale, correction, residual, held,
         z_out, image_out, low_out, high_out, dots, s1, s2, zed) = refs
        step = scalars[1:2, 0:1]
        momentum = scalars[2:3, 0:1]
        for i in range(22):
            for c in range(3):
                image = assemble(own, low, high, yplus, yminus, zplus, zminus, c, i)
                if stage > 1:
                    image = image + momentum * held_in[c, i]
                held[c, i] = image
                residual[c, i] = residual_in[c, i] - step * image

    if stage == 0:
        for i in range(2, 20):
            for c in range(3):
                zed[c, i] = smooth[c, i - 2] + correction[c, i - 2]
    else:

        def emit(c, i, value):
            zed[c, i] = correction[c, i - 2] + value

        sweeps(residual, scale, s1, s2, emit)

    def apply(x, carry):
        rz, zz = carry
        i = x + 3
        diagonal = relaxation / scale[i, 0:16, 0:128]
        u0, terms = stencil_terms(zed, i)
        for c in range(3):
            zc = u0[c][0:16, 0:128]
            image = diagonal * zc - terms[c][0:16, 0:128]
            z_out[c, x] = zc
            image_out[c, x] = image
            rz = rz + residual[c, i, 0:16, 0:128] * zc
            zz = zz + zc * image
        return rz, zz

    zero = jnp.zeros((16, 128), f32)
    rz, zz = lax.fori_loop(0, 16, apply, (zero, zero), unroll=8)
    for c in range(3):
        for x in range(H):
            low_out[c, x] = image_out[c, x]
            high_out[c, x] = image_out[c, 16 - H + x]
    dots[0:1] = jnp.sum(rz, axis=0, keepdims=True)
    dots[1:2] = jnp.sum(zz, axis=0, keepdims=True)
    dots[2:8] = jnp.zeros((6, 128), f32)


def sums_kernel(vectors, image, dots, payload):
    rows = jnp.concatenate([restrict_rows(vectors, image), dots[...]], axis=0)
    payload[...] = jnp.broadcast_to(lanes_of(rows), (128, 128))


def final_kernel(pieces, scalars, residual_in, held, image, zprev, solution_in, direction_in,
                 solution_out, residual_out, direction_out):
    totals = jnp.sum(pieces[...], axis=0, keepdims=True)
    lane = iota((1, 128), 1)
    rho = jnp.sum(jnp.where(lane == 16, totals, 0.0), axis=1, keepdims=True)
    energy = jnp.sum(jnp.where(lane == 17, totals, 0.0), axis=1, keepdims=True)
    momentum = rho / scalars[0:1, 0:1]
    step = rho / (energy - momentum * rho / scalars[1:2, 0:1])

    def plane(x, carry):
        for c in range(3):
            d = zprev[c, x] + momentum * direction_in[c, x]
            direction_out[c, x] = d
            solution_out[c, x] = solution_in[c, x] + step * d
            full = image[c, x] + momentum * held[c, x + H, 0:16, 0:128]
            residual_out[c, x] = residual_in[c, x + H, 0:16, 0:128] - step * full
        return carry

    lax.fori_loop(0, 16, plane, 0, unroll=4)


def both_ways(to_next, to_prev, axis):
    count = lax.axis_size(axis)
    ahead = [(i, (i + 1) % count) for i in range(count)]
    back = [((i + 1) % count, i) for i in range(count)]
    return lax.ppermute(to_next, axis, ahead), lax.ppermute(to_prev, axis, back)


def halo(own, low_edge, high_edge, before=None, middle=None, pieces=None):
    comps = own.shape[0]
    low, high = both_ways(high_edge, low_edge, "gx")
    (ypack,) = call(pack_y_kernel, [(comps, 22, 8, 128)], [own, low, high], after=before)
    yminus, yplus = both_ways(ypack, ypack, "gy")
    done = middle(ypack) if middle else None
    (zpack,) = call(
        pack_z_kernel, [(comps, 24, 256)], [own, low, high, yplus, yminus],
        after=done[0] if middle else pieces,
    )
    zminus, zplus = both_ways(zpack, zpack, GZ)
    return (low, high, yplus, yminus, zplus, zminus), zpack, done


def share(rows):
    count = lax.axis_size(EVERY)
    return lax.all_to_all(rows.reshape(count, 1, 128), EVERY, 0, 0, tiled=True).reshape(count, 128)


def vector_halo_y(faces, vectors, row, token):
    low, high = both_ways(*faces, "gx")
    shape = (3, 18, 16, 128)
    to_low, to_high, row = call(
        vectors_y_kernel, [shape, shape, (128, 128)], [vectors, low, high, row], after=token, limit=12
    )
    yminus, yplus = both_ways(to_high, to_low, "gy")
    return to_low, (low, high, yplus, yminus), row


def vector_halo_z(face, sides, token):
    (packed,) = call(vectors_z_kernel, [(3, 5, 24, 128)], [face, *sides], after=token)
    zminus, zplus = both_ways(packed, packed, GZ)
    return packed, zplus, zminus


def body(forces, mass_shift, deflation, coarse_factor, coarse_slot):
    gx, gy, gz = lax.axis_index("gx"), lax.axis_index("gy"), lax.axis_index(GZ)
    faces = deflation[:, :, 15], deflation[:, :, 0]
    place = jnp.stack([gz, gx, gy]).astype(jnp.int32)
    slot_row = coarse_slot.astype(f32)[None, :]
    scale_own = relaxation / (mass_shift + (6.0 * off_diagonal + 2.0 * stiffer))
    fields = jnp.concatenate([forces, scale_own[None]], axis=0)
    keep, send = call(
        factor_kernel, [(9, 64, 128), (7, 64, 128)], [place, coarse_factor],
        [pltpu.VMEM((256, 256), f32)],
    )
    received = lax.ppermute(send, GZ, [(i, 7 - i) for i in range(8)])
    (folded,) = call(
        fold_kernel, [(9, 64, 128)], [place, keep, received], after=[faces[0], fields, slot_row]
    )
    factor = lax.all_gather(folded, ("gx", *GZ)).reshape(4, 8, 9, 64, 128)

    block = (3, 16, 16, 128)
    lines = (3, 16, 16, 128)
    row, face = call(vectors_kernel, [(128, 128), lines], [deflation, forces], limit=10, micros=6)
    def beside(token):
        return vector_halo_y(faces, deflation, row, token)

    received, zpack, (_, sides, row) = halo(
        fields, fields[:, :H], fields[:, 16 - H :], row, beside
    )
    pieces = share(row)
    packed, zplus, zminus = vector_halo_z(face, sides, zpack)
    ext = (22, 24, 256)
    patch = (3, 18, 24, 256)
    work = [pltpu.VMEM((3, *ext), f32)] * 3
    residual, scale = call(start_kernel, [(3, *ext), ext], [place, fields, *received], after=packed)
    (vz,) = call(vectors_end_kernel, [(3, 18, 24, 128)], [zplus, zminus])
    (smooth,) = call(
        sweeps_kernel, [patch], [residual, scale], work[:2], after=vz, limit=8, micros=4
    )
    around = (*sides, vz)
    weight_shapes = [(48, 128), (3, 32, 128), (3, 24, 128)]
    edge = (3, H, 16, 128)
    main_outs = [block, block, edge, edge, (8, 128)]

    g, wx, wy, wz, near, ordering = call(
        functools.partial(coarse_kernel, 0), [(8, 256)] + weight_shapes + [(32, 128), (128, 128)],
        [place, pieces, slot_row, factor], limit=12, micros=5,
    )
    (correction,) = call(
        functools.partial(correct_kernel, 0), [patch], [wx, wy, wz, deflation, *around],
        limit=13, micros=3,
    )
    z, image, low_edge, high_edge, dots = call(
        functools.partial(main_kernel, 0), main_outs,
        [residual, scale, correction, smooth], work[:1], limit=10, micros=3,
    )
    (row,) = call(sums_kernel, [(128, 128)], [deflation, image, dots], limit=8, micros=2)
    held, advanced, state = [], [], ()
    for iteration in range(1, ITERS):
        pieces = share(row)
        stage = min(iteration, 2)

        received, zpack, _ = halo(image, low_edge, high_edge, row, None, pieces)
        g, wx, wy, wz, hdir, scalars = call(
            functools.partial(coarse_kernel, stage),
            [(8, 256)] + weight_shapes + [(8, 256), (8, 128)],
            [near, pieces, ordering, factor, g, *state],
            after=zpack, limit=12, micros=5,
        )
        state = (hdir, scalars)
        correction, *advanced = call(
            functools.partial(correct_kernel, stage), [patch, block, block],
            [scalars, z, *advanced, wx, wy, wz, deflation, *around],
            after=zpack, limit=14, micros=3,
        )
        residual, *held, z, image, low_edge, high_edge, dots = call(
            functools.partial(main_kernel, stage), [(3, *ext), (3, *ext)] + main_outs,
            [scalars, residual, *held, image, *received, scale, correction],
            work, limit=17, micros=5,
        )
        (row,) = call(sums_kernel, [(128, 128)], [deflation, image, dots], limit=8, micros=2)
    pieces = share(row)
    return tuple(
        call(
            final_kernel,
            [block] * 3,
            [pieces, scalars, residual, *held, image, z, *advanced],
        )
    )


def solution(mesh):
    finer = Mesh(
        mesh.devices.reshape(mesh.shape["gx"], mesh.shape["gy"], 4, 2), ("gx", "gy", "gz_0", "gz_1")
    )
    return jax.shard_map(
        body,
        mesh=finer,
        in_specs=(
            P(None, "gx", "gy", GZ),
            P("gx", "gy", GZ),
            P(None, None, "gx", "gy", GZ),
            P(GZ, None),
            P(),
        ),
        out_specs=(P(None, "gx", "gy", GZ), P(None, "gx", "gy", GZ), P(None, "gx", "gy", GZ)),
        check_vma=False,
    )
```
